512 devices in a mesh: ctx: 16 (over z_lo, y), exp: 32 (over x, z_hi, core).
Axes of the slice: x: 4, y: 8, z: 8 (z_hi: 4, z_lo: 2; z = z_hi * 2 + z_lo), core: 2. Of those that a mesh axis runs over, the one named last changes fastest.
Arguments:
- queries: bfloat16 [2048, 8192], P('ctx', 'exp'), may hold values from -6 to 6
- keys: bfloat16 [2048, 512], P('ctx'), may hold values from -6 to 6
- values: bfloat16 [2048, 512], P('ctx'), may hold values from -5 to 5
- residual: bfloat16 [2048, 4096], P(('ctx', 'exp')), may hold values from -6 to 6
- out_weight: bfloat16 [8192, 4096], P('exp'), may hold values from -0.125 to 0.125
- norm_gain: float32 [4096], replicated, may hold values from 0.25 to 1.75
- expert_ids: int32 [2048, 8], P(('ctx', 'exp')), may hold values from 0 to 31, all different within a row; in each aligned block of 4 rows (0 to 3, 4 to 7, ...) at most 2 rows name the same one
- expert_gates: float32 [2048, 8], P(('ctx', 'exp')), may hold values from 0.05 to 0.35
- w_gate: bfloat16 [32, 4096, 1536], P('exp', None, 'ctx'), may hold values from -0.09375 to 0.09375
- w_up: bfloat16 [32, 4096, 1536], P('exp', None, 'ctx'), may hold values from -0.09375 to 0.09375
- w_down: bfloat16 [32, 1536, 4096], P('exp', None, 'ctx'), may hold values from -0.3125 to 0.3125
Outputs:
- mixed: bfloat16 [2048, 4096], P(('ctx', 'exp'))
- experts_out: bfloat16 [2048, 4096], P(('ctx', 'exp'))
The draws below stay inside these ranges and needn't reach their ends.
Inputs may be any that keep to these rules, and one draw needn't show every extreme that they name: `expert_ids`: in each aligned block of 4 rows (the rows of one device) no expert is named by more than 2 rows, a bound that some block reaches.
All inputs are finite; a program needn't handle non-finite values.
Results may differ from the reference program's by a relative error of at most 0.034.
Values may be sent and summed in bfloat16 or wider, within the bound.
No kernel may reach another device: no remote copies, remote signals or barrier semaphores. Data moves between devices by JAX's collectives and lax.ppermute only.
A program may use at most 64 MiB of HBM per device.

```python
import math
import jax
import jax.numpy as jnp
import numpy as np
from jax import lax

D = 4096
QUERY_HEAD_COUNT = 64
KEY_VALUE_HEADS = 4
HEAD_WIDTH = 128
FF = 1536
TOPK = 8
SEQUENCE_TOKENS = 2048
EXPERTS = 32
TOK_DEV = 4
SLOTS = 2


def draw_queries(key, part):
    random_seed_key = jax.random.fold_in(key, 1)
    filled_tensor = jnp.clip(jax.random.normal(random_seed_key, (SEQUENCE_TOKENS, QUERY_HEAD_COUNT * HEAD_WIDTH), jnp.float32), -4.0, 4.0)
    return filled_tensor.astype(jnp.bfloat16)


def draw_keys(key, part):
    random_seed_key = jax.random.fold_in(key, 2)
    filled_tensor = jnp.clip(jax.random.normal(random_seed_key, (SEQUENCE_TOKENS, KEY_VALUE_HEADS * HEAD_WIDTH), jnp.float32), -4.0, 4.0)
    return filled_tensor.astype(jnp.bfloat16)


def block_levels(rng, shape, pieces, smallest, high):
    level, own = 1.0, jax.random.fold_in(rng, 6)
    for position, shards_of in pieces:
        draws = jnp.exp(jax.random.uniform(jax.random.fold_in(own, position), (shards_of,), jnp.float32, smallest / len(pieces), high / len(pieces)))
        level = level * jnp.repeat(draws, shape[position] // shards_of).reshape([-1 if axis == position else 1 for axis in range(len(shape))])
    return level


def assign_block(stream_key, own, number, rows, amount, top, bound, skew):
    order = jax.random.permutation(stream_key, amount)
    heavy_load, usual = shares(amount, rows * top, bound, skew, True), shares(amount, rows * top, bound, skew, False)
    places = jnp.arange(amount)

    def named(tallies, rotation):
        used = int((tallies > 0).sum())
        fixed = max(1, used // 4)
        passed = fixed + (places - fixed + rotation * (used - fixed)) % max(1, amount - fixed)
        return jnp.zeros((amount,), jnp.int32).at[order[jnp.where(places < fixed, places, passed)]].set(jnp.asarray(tallies, jnp.int32))

    tallies = jnp.where(number % 4 == 0, named(heavy_load, number // 4), named(usual, number - number // 4 - 1))
    mixed = jax.random.permutation(jax.random.fold_in(own, 3), amount)
    donor, taker = mixed[0:amount // 2 * 2:2], mixed[1:amount // 2 * 2:2]
    margin = jnp.minimum(tallies[donor] - 1, bound - tallies[taker]) // 2
    margin = jnp.where((donor == order[0]) | (taker == order[0]) | (tallies[taker] == 0), 0, jnp.maximum(margin, 0))
    passed = jax.random.randint(jax.random.fold_in(own, 4), (amount // 2,), 0, 1 << 20) % (margin + 1)
    tallies = tallies.at[donor].add(-passed).at[taker].add(passed)
    members = jnp.searchsorted(jnp.cumsum(tallies), jnp.arange(rows * top), side="right").astype(jnp.int32)
    table = members.reshape(top, rows).T
    table = table[jax.random.permutation(jax.random.fold_in(own, 1), rows)]
    rotation = jax.random.randint(jax.random.fold_in(own, 2), (rows, 1), 0, top)
    return jnp.take_along_axis(table, (jnp.arange(top)[None, :] + rotation) % top, axis=1)


def shares(amount, total, limit, skew, full):
    weights = [(1 << 20) // math.isqrt(grade ** skew) + 1 for grade in range(1, amount + 1)]
    largest = limit if full else min(limit, max(-(-total // amount), total * weights[0] // sum(weights)))
    least = 1 if total - largest >= amount - 1 else 0
    given, rest = [largest] + [least] * (amount - 1), total - largest - least * (amount - 1)
    while rest > 0:
        movable = [i for i in range(1, amount) if given[i] < largest] or [i for i in range(1, amount) if given[i] < limit]
        mass, left = sum([weights[i] for i in movable]), rest
        for i in movable:
            more = min(limit - given[i], max(1, left * weights[i] // mass), rest)
            given[i] = given[i] + more
            rest = rest - more
    return np.array(given)


def centred(stream_key, shape, spread, bound, shards=(), kind=jnp.bfloat16):
    drawn = spread * jax.random.normal(stream_key, shape, jnp.float32)
    if shards:
        drawn = drawn * block_levels(stream_key, shape, shards, -0.22, 0.18)
    return jnp.clip(drawn, -bound, bound).astype(kind)


def setup_inputs(seed: int = 0) -> dict:
    key_of = jax.random.split(jax.random.key(seed), 12)
    queries = draw_queries(jax.random.fold_in(key_of[11], 71), 0)
    keys = draw_keys(jax.random.fold_in(key_of[11], 71), 0)
    values = centred(key_of[2], (SEQUENCE_TOKENS, KEY_VALUE_HEADS * HEAD_WIDTH), 1.0, 5.0, ((0, 16),))
    residual = centred(key_of[3], (SEQUENCE_TOKENS, D), 1.0, 6.0, ((0, 512),))
    out_weight = centred(key_of[4], (QUERY_HEAD_COUNT * HEAD_WIDTH, D), (QUERY_HEAD_COUNT * HEAD_WIDTH // 4) ** -0.5, 0.125, ((0, 32),))
    norm_gain = jnp.clip(1.0 + 0.15 * jax.random.normal(key_of[5], (D,), jnp.float32), 0.25, 1.75)
    expert_ids_keys = jax.random.split(jax.random.fold_in(key_of[6], 1), SEQUENCE_TOKENS // TOK_DEV)
    expert_ids_turns = jax.random.permutation(jax.random.fold_in(key_of[6], 3), SEQUENCE_TOKENS // TOK_DEV)
    expert_ids = jax.vmap(lambda own, number: assign_block(jax.random.fold_in(key_of[6], 2), own, number, TOK_DEV, EXPERTS, TOPK, SLOTS, 2))(expert_ids_keys, expert_ids_turns).reshape((SEQUENCE_TOKENS, TOPK))
    expert_gates = jnp.clip(0.05 + 0.29999999 * jax.random.uniform(key_of[7], (SEQUENCE_TOKENS, TOPK), jnp.float32) ** block_levels(key_of[7], (SEQUENCE_TOKENS, TOPK), ((0, 512),), -0.2, 0.2), 0.05, 0.35)
    w_gate = centred(key_of[8], (EXPERTS, D, FF), D ** -0.5, 0.09375, ((0, 32), (2, 16)))
    w_up = centred(key_of[9], (EXPERTS, D, FF), D ** -0.5, 0.09375, ((0, 32), (2, 16)))
    w_down = centred(key_of[10], (EXPERTS, FF, D), (FF // 4) ** -0.5, 0.3125, ((0, 32), (2, 16)))
    return dict(queries=queries, keys=keys, values=values, residual=residual, out_weight=out_weight, norm_gain=norm_gain, expert_ids=expert_ids, expert_gates=expert_gates, w_gate=w_gate, w_up=w_up, w_down=w_down)


def reference(queries, keys, values, residual, out_weight, norm_gain, expert_ids, expert_gates, w_gate, w_up, w_down):
    group_width = QUERY_HEAD_COUNT // KEY_VALUE_HEADS
    scale = 1.0 / HEAD_WIDTH ** 0.5
    positions = jnp.arange(SEQUENCE_TOKENS, dtype=jnp.int32)
    allowed = positions[None, :] <= positions[:, None]

    def one_head(head):
        key_value_head = head // group_width
        query_cols = lax.dynamic_slice_in_dim(queries, (head * HEAD_WIDTH).astype(jnp.int32), HEAD_WIDTH, 1)
        key_cols = lax.dynamic_slice_in_dim(keys, (key_value_head * HEAD_WIDTH).astype(jnp.int32), HEAD_WIDTH, 1)
        value_cols = lax.dynamic_slice_in_dim(values, (key_value_head * HEAD_WIDTH).astype(jnp.int32), HEAD_WIDTH, 1)
        scores = jnp.dot(query_cols, key_cols.T, preferred_element_type=jnp.float32) * scale
        scores = jnp.where(allowed, scores, jnp.float32(-1e+30))
        row_max = lax.optimization_barrier(jnp.max(scores, axis=1, keepdims=True))
        weights = jnp.where(allowed, jnp.exp(scores - row_max), jnp.float32(0.0))
        total = lax.optimization_barrier(jnp.sum(weights, axis=1, keepdims=True))
        numer = jnp.dot(weights.astype(jnp.bfloat16), value_cols, preferred_element_type=jnp.float32)
        return (numer / total).astype(jnp.bfloat16)
    heads_all = lax.map(one_head, jnp.arange(QUERY_HEAD_COUNT, dtype=jnp.int32))
    heads_out = jnp.transpose(heads_all, (1, 0, 2)).reshape(SEQUENCE_TOKENS, QUERY_HEAD_COUNT * HEAD_WIDTH)
    projected = jnp.dot(heads_out, out_weight, preferred_element_type=jnp.float32)
    mixed = (residual.astype(jnp.float32) + projected).astype(jnp.bfloat16)
    stream = mixed.astype(jnp.float32)
    mean_sq = lax.optimization_barrier(jnp.mean(stream * stream, axis=1, keepdims=True))
    normed = (stream * lax.rsqrt(mean_sq + 1e-06) * norm_gain[None, :]).astype(jnp.bfloat16)
    most_rows = SEQUENCE_TOKENS // TOK_DEV * SLOTS
    slot_index = jnp.arange(most_rows, dtype=jnp.int32)

    def expert_step(accum, expert):
        picked = expert_ids == expert
        chosen = jnp.any(picked, axis=1)
        token_weight = lax.optimization_barrier(jnp.sum(jnp.where(picked, expert_gates, jnp.float32(0.0)), axis=1))
        count = jnp.sum(chosen.astype(jnp.int32))
        rows = jnp.nonzero(chosen, size=most_rows, fill_value=0)[0].astype(jnp.int32)
        inputs = normed[rows]
        gate = jnp.dot(inputs, w_gate[expert], preferred_element_type=jnp.float32)
        upper = jnp.dot(inputs, w_up[expert], preferred_element_type=jnp.float32)
        hidden = (jax.nn.silu(gate) * upper).astype(jnp.bfloat16)
        output = jnp.dot(hidden, w_down[expert], preferred_element_type=jnp.float32).astype(jnp.bfloat16)
        factor = jnp.where(slot_index < count, token_weight[rows], jnp.float32(0.0))
        accum = accum.at[rows].add(output.astype(jnp.float32) * factor[:, None])
        return (accum, None)
    start_acc = jnp.zeros((SEQUENCE_TOKENS, D), jnp.float32)
    accum, _ = lax.scan(expert_step, start_acc, jnp.arange(EXPERTS, dtype=jnp.int32))
    return (mixed, accum.astype(jnp.bfloat16))
```

```python
import jax
import jax.numpy as jnp
import numpy as np
from jax import lax
from jax.sharding import Mesh, PartitionSpec as P

HEAD_WIDTH = 128
EXTRA = 128

CTX = ("zl", "y")
EXP = ("x", "zh", "co")
EPS_NORM = 1e-06
NEG_LARGE = -1e30


def exchange(pieces, axis):
    return lax.all_to_all(pieces, axis, 0, 0, tiled=True)


def spread(value, axis, count):
    return exchange(jnp.broadcast_to(value[None], (count,) + value.shape), axis)


def added(pieces):
    return jnp.sum(pieces.astype(jnp.float32), axis=0)


def rows_dot(left, right):
    return lax.dot_general(
        left, right, (((1,), (1,)), ((), ())), preferred_element_type=jnp.float32
    )


def route(expert_ids, expert_gates, expert_count, slots):
    flat_ids = expert_ids.reshape(-1)
    tok_rows, top_count = expert_ids.shape
    owner_row = jnp.arange(tok_rows * top_count, dtype=jnp.int32) // top_count
    earlier = (flat_ids[:, None] == flat_ids[None, :]) & (owner_row[None, :] < owner_row[:, None])
    slot_ids = jnp.sum(earlier.astype(jnp.int32), axis=1).reshape(tok_rows, top_count)
    expert_hit = (
        expert_ids[None, None] == jnp.arange(expert_count, dtype=jnp.int32)[:, None, None, None]
    )
    slot_hit = slot_ids[None, None] == jnp.arange(slots, dtype=jnp.int32)[None, :, None, None]
    hits = expert_hit & slot_hit
    table = jnp.any(hits, axis=3).astype(jnp.bfloat16)
    mix = jnp.sum(jnp.where(hits, expert_gates[None, None], 0.0), axis=3)
    return table.reshape(expert_count * slots, tok_rows), mix.reshape(
        expert_count * slots, tok_rows
    )


def on_device(
    queries,
    keys,
    values,
    residual,
    out_weight,
    norm_gain,
    expert_ids,
    expert_gates,
    w_gate,
    w_up,
    w_down,
):
    n_zl, n_y = lax.axis_size("zl"), lax.axis_size("y")
    n_x, n_zh, n_co = lax.axis_size("x"), lax.axis_size("zh"), lax.axis_size("co")
    zl, y_pos, x_pos, co = (lax.axis_index(a) for a in ("zl", "y", "x", "co"))
    ctx_count, expert_count = n_zl * n_y, n_x * n_zh * n_co
    width = residual.shape[1]
    tok_dev, top_count = expert_ids.shape
    slots = 2
    tok_block = queries.shape[0]
    heads = queries.shape[1] // HEAD_WIDTH
    swap = [(i, n_zl - 1 - i) for i in range(n_zl)]

    gate_up = jnp.stack([w_gate[0].T, w_up[0].T])
    gate_up_other = lax.ppermute(gate_up, "zl", swap)
    down_other = lax.ppermute(w_down[0], "zl", swap)

    mine = jnp.where(co == 0, keys, values)
    mine = lax.dynamic_slice_in_dim(mine, x_pos * HEAD_WIDTH, HEAD_WIDTH, 1)
    gathered = spread(mine, CTX, ctx_count).reshape(ctx_count * tok_block, HEAD_WIDTH)
    key_all, value_all = spread(gathered, "co", n_co)

    order = np.arange(tok_block).reshape(n_x, n_zh, n_co, tok_dev).transpose(2, 0, 1, 3)
    split = queries.reshape(n_x, n_zh, n_co, tok_dev, heads, HEAD_WIDTH)
    query_rows = jnp.transpose(split, (4, 2, 0, 1, 3, 5)).reshape(heads * tok_block, HEAD_WIDTH)
    query_pos = (zl * n_y + y_pos) * tok_block + jnp.asarray(
        np.tile(order.reshape(-1), heads), jnp.int32
    )
    key_pos = jnp.arange(key_all.shape[0], dtype=jnp.int32)
    allowed = key_pos[None, :] <= query_pos[:, None]
    scores = rows_dot(query_rows, key_all) * (1.0 / HEAD_WIDTH**0.5)
    scores = jnp.where(allowed, scores, NEG_LARGE)
    weights = jnp.exp(scores - jnp.max(scores, axis=1, keepdims=True))
    total = jnp.sum(weights, axis=1, keepdims=True)
    numer = jnp.dot(weights.astype(jnp.bfloat16), value_all, preferred_element_type=jnp.float32)
    done = (numer / total).astype(jnp.bfloat16).reshape(heads, tok_block, HEAD_WIDTH)
    heads_out = jnp.transpose(done, (1, 0, 2)).reshape(tok_block, heads * HEAD_WIDTH)

    partial = jnp.dot(heads_out, out_weight, preferred_element_type=jnp.float32)
    partial = partial.astype(jnp.bfloat16).reshape(n_co, tok_block // n_co, width)
    partial = added(exchange(partial, "co")).astype(jnp.bfloat16)
    projected = added(exchange(partial.reshape(n_x * n_zh, tok_dev, width), ("x", "zh")))
    mixed = (residual.astype(jnp.float32) + projected).astype(jnp.bfloat16)

    stream = mixed.astype(jnp.float32)
    mean_sq = jnp.mean(stream * stream, axis=1, keepdims=True)
    normed = (stream * lax.rsqrt(mean_sq + EPS_NORM) * norm_gain[None, :]).astype(jnp.bfloat16)

    table, mix = route(expert_ids, expert_gates, expert_count, slots)
    mix_high = mix.astype(jnp.bfloat16)
    mix_low = (mix - mix_high.astype(jnp.float32)).astype(jnp.bfloat16)
    extra = jnp.concatenate([mix_high, mix_low], axis=1)
    extra = jnp.pad(extra, ((0, 0), (0, EXTRA - extra.shape[1])))
    outgoing = jnp.dot(table, normed, preferred_element_type=jnp.float32).astype(jnp.bfloat16)
    outgoing = jnp.concatenate([outgoing, extra], axis=1)
    arrived = exchange(outgoing.reshape(expert_count, slots, width + EXTRA), EXP)
    rows = lax.all_gather(
        arrived.reshape(expert_count * slots, width + EXTRA), "y", axis=0, tiled=True
    )

    weight_in = jnp.stack([gate_up, gate_up_other], axis=1)
    weight_in = jnp.pad(weight_in, ((0, 0),) * 3 + ((0, EXTRA),)).reshape(-1, width + EXTRA)
    both = rows_dot(weight_in, rows)
    units = both.shape[0] // 2
    hidden = (jax.nn.silu(both[:units]) * both[units:]).astype(jnp.bfloat16)
    hidden = spread(hidden, "y", n_y).reshape(n_y * units, -1)

    down = jnp.concatenate([w_down[0], down_other], axis=1)
    down = down.reshape(n_zl, n_y, units // n_zl, down.shape[1])
    down = jnp.where(zl == 0, down, down[::-1])
    down = jnp.transpose(down, (1, 0, 2, 3)).reshape(n_y * units, -1)
    result = lax.dot_general(
        hidden, down, (((0,), (0,)), ((), ())), preferred_element_type=jnp.float32
    )
    gates = rows[:, width : width + 2 * tok_dev].astype(jnp.float32)
    gates = gates[:, :tok_dev] + gates[:, tok_dev:]
    result = (result * jnp.sum(gates, axis=1, keepdims=True)).astype(jnp.bfloat16)

    block_of = np.arange(n_y * expert_count).reshape(n_y, n_x, n_zh, n_co)
    block_of = block_of.transpose(3, 1, 2, 0).reshape(-1)
    token_of = (block_of[:, None] * tok_dev + np.arange(tok_dev)[None, :]).reshape(-1)
    place = jnp.sum(
        (gates != 0).astype(jnp.int32) * jnp.arange(1, tok_dev + 1, dtype=jnp.int32)[None, :],
        axis=1,
    )
    slot_block = jnp.arange(n_y * expert_count * slots, dtype=jnp.int32) // slots
    slot_token = jnp.where(place > 0, slot_block * tok_dev + place - 1, -1)
    onehot = (jnp.asarray(token_of, jnp.int32)[:, None] == slot_token[None, :]).astype(jnp.bfloat16)
    tokens = jnp.dot(onehot, result, preferred_element_type=jnp.float32).astype(jnp.bfloat16)

    cols = tokens.shape[1]
    tokens = added(exchange(tokens.reshape(n_co, -1, cols), "co")).astype(jnp.bfloat16)
    tokens = added(exchange(tokens.reshape(n_x, -1, cols), "x")).astype(jnp.bfloat16)
    tokens = exchange(tokens.reshape(n_zh * n_y, tok_dev, cols), ("zh", "y"))
    tokens = added(tokens.reshape(n_zh, n_y, tok_dev, cols))
    tokens = tokens.reshape(n_y, tok_dev, n_zl, cols // n_zl).transpose(1, 2, 0, 3)
    tokens = jnp.where(zl == 0, tokens, tokens[:, ::-1])
    return (mixed, tokens.reshape(tok_dev, width).astype(jnp.bfloat16))


def solution(mesh):
    fine = Mesh(mesh.devices.reshape(2, 8, 4, 4, 2), CTX + EXP)
    return jax.shard_map(
        on_device,
        mesh=fine,
        in_specs=(
            P(CTX, EXP),
            P(CTX, None),
            P(CTX, None),
            P(CTX + EXP, None),
            P(EXP, None),
            P(),
            P(CTX + EXP, None),
            P(CTX + EXP, None),
            P(EXP, None, CTX),
            P(EXP, None, CTX),
            P(EXP, None, CTX),
        ),
        out_specs=(P(CTX + EXP, None), P(CTX + EXP, None)),
        check_vma=False,
    )
```

```python
import jax
import jax.numpy as jnp
import numpy as np
from jax import lax
from jax.sharding import Mesh, PartitionSpec as P

HEAD_WIDTH = 128
EXTRA = 128

CTX = ("zl", "y")
EXP = ("x", "zh", "co")
EPS_NORM = 1e-06
NEG_LARGE = -1e30


def exchange(pieces, axis):
    return lax.all_to_all(pieces, axis, 0, 0, tiled=True)


def spread(value, axis, count):
    return exchange(jnp.broadcast_to(value[None], (count,) + value.shape), axis)


def added(pieces):
    return jnp.sum(pieces.astype(jnp.float32), axis=0)


def rows_dot(left, right):
    return lax.dot_general(
        left, right, (((1,), (1,)), ((), ())), preferred_element_type=jnp.float32
    )


def route(expert_ids, expert_gates, expert_count, slots):
    flat_ids = expert_ids.reshape(-1)
    tok_rows, top_count = expert_ids.shape
    owner_row = jnp.arange(tok_rows * top_count, dtype=jnp.int32) // top_count
    earlier = (flat_ids[:, None] == flat_ids[None, :]) & (owner_row[None, :] < owner_row[:, None])
    slot_ids = jnp.sum(earlier.astype(jnp.int32), axis=1).reshape(tok_rows, top_count)
    expert_hit = (
        expert_ids[None, None] == jnp.arange(expert_count, dtype=jnp.int32)[:, None, None, None]
    )
    slot_hit = slot_ids[None, None] == jnp.arange(slots, dtype=jnp.int32)[None, :, None, None]
    hits = expert_hit & slot_hit
    table = jnp.any(hits, axis=3).astype(jnp.bfloat16)
    mix = jnp.sum(jnp.where(hits, expert_gates[None, None], 0.0), axis=3)
    return table.reshape(expert_count * slots, tok_rows), mix.reshape(
        expert_count * slots, tok_rows
    )


def on_device(
    queries,
    keys,
    values,
    residual,
    out_weight,
    norm_gain,
    expert_ids,
    expert_gates,
    w_gate,
    w_up,
    w_down,
):
    n_zl, n_y = lax.axis_size("zl"), lax.axis_size("y")
    n_x, n_zh, n_co = lax.axis_size("x"), lax.axis_size("zh"), lax.axis_size("co")
    zl, y_pos, x_pos, co = (lax.axis_index(a) for a in ("zl", "y", "x", "co"))
    ctx_count, expert_count = n_zl * n_y, n_x * n_zh * n_co
    width = residual.shape[1]
    tok_dev, top_count = expert_ids.shape
    slots = 2
    tok_block = queries.shape[0]
    heads = queries.shape[1] // HEAD_WIDTH
    swap = [(i, n_zl - 1 - i) for i in range(n_zl)]

    gate_up = jnp.stack([w_gate[0].T, w_up[0].T])
    gate_up_other = lax.ppermute(gate_up, "zl", swap)
    down_other = lax.ppermute(w_down[0], "zl", swap)

    mine = jnp.where(co == 0, keys, values)
    mine = lax.dynamic_slice_in_dim(mine, x_pos * HEAD_WIDTH, HEAD_WIDTH, 1)
    gathered = spread(mine, CTX, ctx_count).reshape(ctx_count * tok_block, HEAD_WIDTH)
    key_all, value_all = spread(gathered, "co", n_co)

    order = np.arange(tok_block).reshape(n_x, n_zh, n_co, tok_dev).transpose(2, 0, 1, 3)
    split = queries.reshape(n_x, n_zh, n_co, tok_dev, heads, HEAD_WIDTH)
    query_rows = jnp.transpose(split, (4, 2, 0, 1, 3, 5)).reshape(heads * tok_block, HEAD_WIDTH)
    query_pos = (zl * n_y + y_pos) * tok_block + jnp.asarray(
        np.tile(order.reshape(-1), heads), jnp.int32
    )
    key_pos = jnp.arange(key_all.shape[0], dtype=jnp.int32)
    allowed = key_pos[None, :] <= query_pos[:, None]
    scores = rows_dot(query_rows, key_all) * (1.0 / HEAD_WIDTH**0.5)
    scores = jnp.where(allowed, scores, NEG_LARGE)
    weights = jnp.exp(scores - jnp.max(scores, axis=1, keepdims=True))
    total = jnp.sum(weights, axis=1, keepdims=True)
    numer = jnp.dot(weights.astype(jnp.bfloat16), value_all, preferred_element_type=jnp.float32)
    done = (numer / total).astype(jnp.bfloat16).reshape(heads, tok_block, HEAD_WIDTH)
    heads_out = jnp.transpose(done, (1, 0, 2)).reshape(tok_block, heads * HEAD_WIDTH)

    partial = jnp.dot(heads_out, out_weight, preferred_element_type=jnp.float32)
    partial = partial.astype(jnp.bfloat16).reshape(n_co, tok_block // n_co, width)
    partial = added(exchange(partial, "co")).astype(jnp.bfloat16)
    partial = added(exchange(partial.reshape(n_x, -1, width), "x")).astype(jnp.bfloat16)
    projected = added(exchange(partial.reshape(n_zh, tok_dev, width), "zh"))
    mixed = (residual.astype(jnp.float32) + projected).astype(jnp.bfloat16)

    stream = mixed.astype(jnp.float32)
    mean_sq = jnp.mean(stream * stream, axis=1, keepdims=True)
    normed = (stream * lax.rsqrt(mean_sq + EPS_NORM) * norm_gain[None, :]).astype(jnp.bfloat16)

    normed, gate_up_other, down_other = lax.optimization_barrier(
        (normed, gate_up_other, down_other)
    )

    table, mix = route(expert_ids, expert_gates, expert_count, slots)
    mix_high = mix.astype(jnp.bfloat16)
    mix_low = (mix - mix_high.astype(jnp.float32)).astype(jnp.bfloat16)
    extra = jnp.concatenate([mix_high, mix_low], axis=1)
    extra = jnp.pad(extra, ((0, 0), (0, EXTRA - extra.shape[1])))
    outgoing = jnp.dot(table, normed, preferred_element_type=jnp.float32).astype(jnp.bfloat16)
    outgoing = jnp.concatenate([outgoing, extra], axis=1)
    arrived = exchange(outgoing.reshape(expert_count, slots, width + EXTRA), EXP)
    rows = lax.all_gather(
        arrived.reshape(expert_count * slots, width + EXTRA), "y", axis=0, tiled=True
    )

    weight_in = jnp.stack([gate_up, gate_up_other], axis=1)
    weight_in = jnp.pad(weight_in, ((0, 0),) * 3 + ((0, EXTRA),)).reshape(-1, width + EXTRA)
    both = rows_dot(weight_in, rows)
    units = both.shape[0] // 2
    hidden = (jax.nn.silu(both[:units]) * both[units:]).astype(jnp.bfloat16)
    hidden = spread(hidden, "y", n_y).reshape(n_y * units, -1)

    down = jnp.concatenate([w_down[0], down_other], axis=1)
    down = down.reshape(n_zl, n_y, units // n_zl, down.shape[1])
    down = jnp.where(zl == 0, down, down[::-1])
    down = jnp.transpose(down, (1, 0, 2, 3)).reshape(n_y * units, -1)
    result = lax.dot_general(
        hidden, down, (((0,), (0,)), ((), ())), preferred_element_type=jnp.float32
    )
    gates = rows[:, width : width + 2 * tok_dev].astype(jnp.float32)
    gates = gates[:, :tok_dev] + gates[:, tok_dev:]
    result = (result * jnp.sum(gates, axis=1, keepdims=True)).astype(jnp.bfloat16)

    block_of = np.arange(n_y * expert_count).reshape(n_y, n_x, n_zh, n_co)
    block_of = block_of.transpose(3, 1, 2, 0).reshape(-1)
    token_of = (block_of[:, None] * tok_dev + np.arange(tok_dev)[None, :]).reshape(-1)
    place = jnp.sum(
        (gates != 0).astype(jnp.int32) * jnp.arange(1, tok_dev + 1, dtype=jnp.int32)[None, :],
        axis=1,
    )
    slot_block = jnp.arange(n_y * expert_count * slots, dtype=jnp.int32) // slots
    slot_token = jnp.where(place > 0, slot_block * tok_dev + place - 1, -1)
    onehot = (jnp.asarray(token_of, jnp.int32)[:, None] == slot_token[None, :]).astype(jnp.bfloat16)
    tokens = jnp.dot(onehot, result, preferred_element_type=jnp.float32).astype(jnp.bfloat16)

    cols = tokens.shape[1]
    tokens = added(exchange(tokens.reshape(n_co, -1, cols), "co")).astype(jnp.bfloat16)
    tokens = added(exchange(tokens.reshape(n_x, -1, cols), "x")).astype(jnp.bfloat16)
    tokens = exchange(tokens.reshape(n_zh * n_y, tok_dev, cols), ("zh", "y"))
    tokens = added(tokens.reshape(n_zh, n_y, tok_dev, cols))
    tokens = tokens.reshape(n_y, tok_dev, n_zl, cols // n_zl).transpose(1, 2, 0, 3)
    tokens = jnp.where(zl == 0, tokens, tokens[:, ::-1])
    return (mixed, tokens.reshape(tok_dev, width).astype(jnp.bfloat16))


def solution(mesh):
    fine = Mesh(mesh.devices.reshape(2, 8, 4, 4, 2), CTX + EXP)
    return jax.shard_map(
        on_device,
        mesh=fine,
        in_specs=(
            P(CTX, EXP),
            P(CTX, None),
            P(CTX, None),
            P(CTX + EXP, None),
            P(EXP, None),
            P(),
            P(CTX + EXP, None),
            P(CTX + EXP, None),
            P(EXP, None, CTX),
            P(EXP, None, CTX),
            P(EXP, None, CTX),
        ),
        out_specs=(P(CTX + EXP, None), P(CTX + EXP, None)),
        check_vma=False,
    )
```

```python
import jax
import jax.numpy as jnp
import numpy as np
from jax import lax
from jax.sharding import Mesh, PartitionSpec as P

HEAD_WIDTH = 128
EXTRA = 128

CTX = ("zl", "y")
EXP = ("x", "zh", "co")
EPS_NORM = 1e-06
NEG_LARGE = -1e30


def exchange(pieces, axis):
    return lax.all_to_all(pieces, axis, 0, 0, tiled=True)


def spread(value, axis, count):
    return exchange(jnp.broadcast_to(value[None], (count,) + value.shape), axis)


def added(pieces):
    return jnp.sum(pieces.astype(jnp.float32), axis=0)


def rows_dot(left, right):
    return lax.dot_general(
        left, right, (((1,), (1,)), ((), ())), preferred_element_type=jnp.float32
    )


def route(expert_ids, expert_gates, expert_count, slots):
    flat_ids = expert_ids.reshape(-1)
    tok_rows, top_count = expert_ids.shape
    owner_row = jnp.arange(tok_rows * top_count, dtype=jnp.int32) // top_count
    earlier = (flat_ids[:, None] == flat_ids[None, :]) & (owner_row[None, :] < owner_row[:, None])
    slot_ids = jnp.sum(earlier.astype(jnp.int32), axis=1).reshape(tok_rows, top_count)
    expert_hit = (
        expert_ids[None, None] == jnp.arange(expert_count, dtype=jnp.int32)[:, None, None, None]
    )
    slot_hit = slot_ids[None, None] == jnp.arange(slots, dtype=jnp.int32)[None, :, None, None]
    hits = expert_hit & slot_hit
    table = jnp.any(hits, axis=3).astype(jnp.bfloat16)
    mix = jnp.sum(jnp.where(hits, expert_gates[None, None], 0.0), axis=3)
    return table.reshape(expert_count * slots, tok_rows), mix.reshape(
        expert_count * slots, tok_rows
    )


def on_device(
    queries,
    keys,
    values,
    residual,
    out_weight,
    norm_gain,
    expert_ids,
    expert_gates,
    w_gate,
    w_up,
    w_down,
):
    n_zl, n_y = lax.axis_size("zl"), lax.axis_size("y")
    n_x, n_zh, n_co = lax.axis_size("x"), lax.axis_size("zh"), lax.axis_size("co")
    zl, y_pos, x_pos, co = (lax.axis_index(a) for a in ("zl", "y", "x", "co"))
    ctx_count, expert_count = n_zl * n_y, n_x * n_zh * n_co
    width = residual.shape[1]
    tok_dev, top_count = expert_ids.shape
    slots = 2
    tok_block = queries.shape[0]
    heads = queries.shape[1] // HEAD_WIDTH
    swap = [(i, n_zl - 1 - i) for i in range(n_zl)]

    mine = jnp.where(co == 0, keys, values)
    mine = lax.dynamic_slice_in_dim(mine, x_pos * HEAD_WIDTH, HEAD_WIDTH, 1)
    gathered = spread(mine, CTX, ctx_count).reshape(ctx_count * tok_block, HEAD_WIDTH)

    table, mix = route(expert_ids, expert_gates, expert_count, slots)
    places = n_y * tok_dev
    own_place = jnp.arange(places, dtype=jnp.int32) // tok_dev == y_pos
    mix = jnp.where(own_place[None, :], jnp.tile(mix, (1, n_y)), 0.0)
    mix_high = mix.astype(jnp.bfloat16)
    mix_low = (mix - mix_high.astype(jnp.float32)).astype(jnp.bfloat16)
    extra = jnp.concatenate([mix_high, mix_low], axis=1)
    extra = jnp.pad(extra, ((0, 0), (0, EXTRA - extra.shape[1])))
    gathered, table, extra = lax.optimization_barrier((gathered, table, extra))
    key_all, value_all = spread(gathered, "co", n_co)

    order = np.arange(tok_block).reshape(n_x, n_zh, n_co, tok_dev).transpose(2, 0, 1, 3)
    split = queries.reshape(n_x, n_zh, n_co, tok_dev, heads, HEAD_WIDTH)
    query_rows = jnp.transpose(split, (4, 2, 0, 1, 3, 5)).reshape(heads * tok_block, HEAD_WIDTH)
    query_pos = (zl * n_y + y_pos) * tok_block + jnp.asarray(
        np.tile(order.reshape(-1), heads), jnp.int32
    )
    key_pos = jnp.arange(key_all.shape[0], dtype=jnp.int32)
    allowed = key_pos[None, :] <= query_pos[:, None]
    scores = rows_dot(query_rows, key_all) * (1.0 / HEAD_WIDTH**0.5)
    scores = jnp.where(allowed, scores, NEG_LARGE)
    weights = jnp.exp(scores - jnp.max(scores, axis=1, keepdims=True))
    total = jnp.sum(weights, axis=1, keepdims=True)
    numer = jnp.dot(weights.astype(jnp.bfloat16), value_all, preferred_element_type=jnp.float32)
    done = (numer / total).astype(jnp.bfloat16).reshape(heads, tok_block, HEAD_WIDTH)
    heads_out = jnp.transpose(done, (1, 0, 2)).reshape(tok_block, heads * HEAD_WIDTH)

    partial = jnp.dot(heads_out, out_weight, preferred_element_type=jnp.float32)
    partial = partial.astype(jnp.bfloat16).reshape(n_co, tok_block // n_co, width)
    partial = added(exchange(partial, "co")).astype(jnp.bfloat16)
    partial = added(exchange(partial.reshape(n_x, -1, width), "x")).astype(jnp.bfloat16)
    projected = added(exchange(partial.reshape(n_zh, tok_dev, width), "zh"))
    mixed = (residual.astype(jnp.float32) + projected).astype(jnp.bfloat16)

    stream = mixed.astype(jnp.float32)
    mean_sq = jnp.mean(stream * stream, axis=1, keepdims=True)
    normed = (stream * lax.rsqrt(mean_sq + EPS_NORM) * norm_gain[None, :]).astype(jnp.bfloat16)

    outgoing = jnp.dot(table, normed, preferred_element_type=jnp.float32).astype(jnp.bfloat16)
    outgoing = jnp.concatenate([outgoing, extra], axis=1)
    arrived = exchange(outgoing.reshape(expert_count, slots, width + EXTRA), EXP)
    arrived = arrived.reshape(expert_count * slots, width + EXTRA)

    gate_up = jnp.stack([w_gate[0].T, w_up[0].T])
    arrived, gate_up, down_own = lax.optimization_barrier((arrived, gate_up, w_down[0]))
    rows = lax.all_gather(arrived, "y", axis=0, tiled=True)
    weight_in = jnp.stack([gate_up, lax.ppermute(gate_up, "zl", swap)], axis=1)
    weight_in = jnp.pad(weight_in, ((0, 0),) * 3 + ((0, EXTRA),)).reshape(-1, width + EXTRA)
    units = weight_in.shape[0] // 2
    down = jnp.concatenate([down_own, lax.ppermute(down_own, "zl", swap)], axis=1)
    down = down.reshape(n_zl, n_y, units // n_zl, down.shape[1])
    down = jnp.where(zl == 0, down, down[::-1])
    down = jnp.transpose(down, (1, 0, 2, 3)).reshape(n_y * units, -1)
    rows, weight_in, down = lax.optimization_barrier((rows, weight_in, down))

    both = rows_dot(weight_in, rows)
    hidden = (jax.nn.silu(both[:units]) * both[units:]).astype(jnp.bfloat16)
    hidden, down, extra = lax.optimization_barrier((hidden, down, rows[:, width:]))
    hidden = spread(hidden, "y", n_y).reshape(n_y * units, -1)

    result = lax.dot_general(
        hidden, down, (((0,), (0,)), ((), ())), preferred_element_type=jnp.float32
    ).astype(jnp.bfloat16)
    cols = result.shape[1]
    result = jnp.concatenate([result, extra], axis=1)
    result = result.reshape(n_y, expert_count, slots, cols + EXTRA).transpose(1, 0, 2, 3)
    result = exchange(result.reshape(expert_count, n_y * slots, cols + EXTRA), EXP)
    result = result.reshape(-1, cols + EXTRA)

    tokens = lax.dot_general(
        result[:, cols : cols + 2 * places],
        result[:, :cols],
        (((0,), (0,)), ((), ())),
        preferred_element_type=jnp.float32,
    )
    tokens = (tokens[:places] + tokens[places:]).astype(jnp.bfloat16)
    tokens = exchange(tokens.reshape(n_y, tok_dev, cols), "y")
    tokens = tokens.reshape(n_y, tok_dev, n_zl, cols // n_zl).transpose(1, 2, 0, 3)
    tokens = jnp.where(zl == 0, tokens, tokens[:, ::-1])
    return (mixed, tokens.reshape(tok_dev, width))


def solution(mesh):
    fine = Mesh(mesh.devices.reshape(2, 8, 4, 4, 2), CTX + EXP)
    return jax.shard_map(
        on_device,
        mesh=fine,
        in_specs=(
            P(CTX, EXP),
            P(CTX, None),
            P(CTX, None),
            P(CTX + EXP, None),
            P(EXP, None),
            P(),
            P(CTX + EXP, None),
            P(CTX + EXP, None),
            P(EXP, None, CTX),
            P(EXP, None, CTX),
            P(EXP, None, CTX),
        ),
        out_specs=(P(CTX + EXP, None), P(CTX + EXP, None)),
        check_vma=False,
    )
```

```python
import jax
import jax.numpy as jnp
import numpy as np
from jax import lax
from jax.experimental import pallas as pl
from jax.experimental.pallas import tpu as pltpu
from jax.sharding import Mesh, PartitionSpec as P

HEAD_WIDTH = 128
EXTRA = 128

CTX = ("zl", "y")
EXP = ("x", "zh", "co")
EPS_NORM = 1e-06
NEG_LARGE = -1e30


def exchange(pieces, axis):
    return lax.all_to_all(pieces, axis, 0, 0, tiled=True)


def spread(value, axis, count):
    return exchange(jnp.broadcast_to(value[None], (count,) + value.shape), axis)


def added(pieces):
    return jnp.sum(pieces.astype(jnp.float32), axis=0)


def rows_dot(left, right):
    return lax.dot_general(
        left, right, (((1,), (1,)), ((), ())), preferred_element_type=jnp.float32
    )


def route(expert_ids, expert_gates, expert_count, slots):
    flat_ids = expert_ids.reshape(-1)
    tok_rows, top_count = expert_ids.shape
    owner_row = jnp.arange(tok_rows * top_count, dtype=jnp.int32) // top_count
    earlier = (flat_ids[:, None] == flat_ids[None, :]) & (owner_row[None, :] < owner_row[:, None])
    slot_ids = jnp.sum(earlier.astype(jnp.int32), axis=1).reshape(tok_rows, top_count)
    expert_hit = (
        expert_ids[None, None] == jnp.arange(expert_count, dtype=jnp.int32)[:, None, None, None]
    )
    slot_hit = slot_ids[None, None] == jnp.arange(slots, dtype=jnp.int32)[None, :, None, None]
    hits = expert_hit & slot_hit
    table = jnp.any(hits, axis=3).astype(jnp.bfloat16)
    mix = jnp.sum(jnp.where(hits, expert_gates[None, None], 0.0), axis=3)
    return table.reshape(expert_count * slots, tok_rows), mix.reshape(
        expert_count * slots, tok_rows
    )


def whole(shape):
    return pl.BlockSpec(shape, lambda *_: (0,) * len(shape))


def hidden_kernel(zl_ref, rows_ref, gate_a, gate_b, up_a, up_b, out_ref, weight, total):
    step = pl.program_id(0)
    units = gate_a.shape[0]

    for place, (own, other) in enumerate(((gate_a, gate_b), (up_a, up_b))):
        low = pl.ds(2 * place * units, units)
        high = pl.ds((2 * place + 1) * units, units)

        @pl.when(zl_ref[0] == 0)
        def _():
            weight[low, :] = own[...]
            weight[high, :] = other[...]

        @pl.when(zl_ref[0] != 0)
        def _():
            weight[low, :] = other[...]
            weight[high, :] = own[...]

    @pl.when(step == 0)
    def _():
        total[...] = jnp.zeros_like(total)

    total[...] += rows_dot(weight[...], rows_ref[...])

    @pl.when(step == pl.num_programs(0) - 1)
    def _():
        gate, upper = total[: 2 * units, :], total[2 * units :, :]
        hidden = (gate / (1.0 + jnp.exp(-gate)) * upper).astype(jnp.bfloat16)
        half = hidden.shape[1] // 2
        for peer in range(out_ref.shape[0]):
            start = (peer % 2) * half
            out_ref[peer] = hidden[:, start : start + half]


def hidden_pieces(rows, zl, weights, width, peers):
    units = weights[0].shape[0]
    count, step = rows.shape[0], 1024 if width % 1024 == 0 else width
    weight_spec = pl.BlockSpec((units, step), lambda k, *_: (0, k))
    return pl.pallas_call(
        hidden_kernel,
        out_shape=jax.ShapeDtypeStruct((peers, 2 * units, count // 2), jnp.bfloat16),
        grid_spec=pltpu.PrefetchScalarGridSpec(
            num_scalar_prefetch=1,
            grid=(width // step,),
            in_specs=[pl.BlockSpec((count, step), lambda k, *_: (0, k))] + [weight_spec] * 4,
            out_specs=whole((peers, 2 * units, count // 2)),
            scratch_shapes=[
                pltpu.VMEM((4 * units, step), jnp.bfloat16),
                pltpu.VMEM((4 * units, count), jnp.float32),
            ],
        ),
        compiler_params=pltpu.CompilerParams(vmem_limit_bytes=60 * 2**20),
        cost_estimate=pl.CostEstimate(
            flops=8 * units * count * width, bytes_accessed=2 * count * width, transcendentals=0
        ),
    )(zl.reshape(1), rows, *weights)


def down_kernel(half_ref, hidden_ref, extra_ref, *refs):
    weights, out_ref, stacked = refs[:4], refs[4], refs[5]
    peers, units, count = hidden_ref.shape
    for peer in range(peers):
        for z in range(2):
            rows = pl.ds((z * peers + peer) * (units // 2), units // 2)
            stacked[rows, :] = hidden_ref[peer, z * (units // 2) : (z + 1) * (units // 2), :]
    blocks = peers // 2
    each = count // blocks
    to = lax.broadcasted_iota(jnp.int32, (count, count), 0)
    source = (to % (2 * blocks)) // 2 * each + to // (2 * blocks) * 2 + to % 2
    move = (lax.broadcasted_iota(jnp.int32, (count, count), 1) == source).astype(jnp.bfloat16)
    rows = stacked[...].T
    cols = weights[0].shape[1]
    for place, weight in enumerate(weights):
        result = jnp.dot(rows, weight[...], preferred_element_type=jnp.float32)
        result = jnp.dot(
            move, result.astype(jnp.bfloat16), preferred_element_type=jnp.float32
        )
        out_ref[:, place * cols : (place + 1) * cols] = result.astype(jnp.bfloat16)
    extra = jnp.where(half_ref[0] == 0, extra_ref[:count, :], extra_ref[count:, :])
    extra = jnp.dot(move, extra, preferred_element_type=jnp.float32)
    out_ref[:, 4 * cols :] = extra.astype(jnp.bfloat16)


def down_slots(half, hidden, extra, weights):
    peers, units, count = hidden.shape
    deep, cols = weights[0].shape
    out = (count, 4 * cols + EXTRA)
    return pl.pallas_call(
        down_kernel,
        out_shape=jax.ShapeDtypeStruct(out, jnp.bfloat16),
        grid_spec=pltpu.PrefetchScalarGridSpec(
            num_scalar_prefetch=1,
            grid=(1,),
            in_specs=[
                whole(hidden.shape),
                whole(extra.shape),
            ]
            + [whole((deep, cols))] * 4,
            out_specs=whole(out),
            scratch_shapes=[pltpu.VMEM((deep, count), jnp.bfloat16)],
        ),
        compiler_params=pltpu.CompilerParams(vmem_limit_bytes=60 * 2**20),
        cost_estimate=pl.CostEstimate(
            flops=8 * deep * count * cols, bytes_accessed=8 * deep * cols, transcendentals=0
        ),
    )(half.reshape(1), hidden, extra, *weights)


def on_device(
    queries,
    keys,
    values,
    residual,
    out_weight,
    norm_gain,
    expert_ids,
    expert_gates,
    w_gate,
    w_up,
    w_down,
):
    n_zl, n_y = lax.axis_size("zl"), lax.axis_size("y")
    n_x, n_zh, n_co = lax.axis_size("x"), lax.axis_size("zh"), lax.axis_size("co")
    zl, y_pos, x_pos, co = (lax.axis_index(a) for a in ("zl", "y", "x", "co"))
    ctx_count, expert_count = n_zl * n_y, n_x * n_zh * n_co
    width = residual.shape[1]
    tok_dev, top_count = expert_ids.shape
    slots = 2
    tok_block = queries.shape[0]
    heads = queries.shape[1] // HEAD_WIDTH
    swap_z = [(i, i ^ 1) for i in range(n_zl)]
    swap_y = [(i, i ^ 1) for i in range(n_y)]
    gate_own, up_own, down_own = w_gate[0].T, w_up[0].T, w_down[0]

    gate_z, up_z = lax.ppermute(gate_own, "zl", swap_z), lax.ppermute(up_own, "zl", swap_z)

    mine = jnp.where(co == 0, keys, values)
    mine = lax.dynamic_slice_in_dim(mine, x_pos * HEAD_WIDTH, HEAD_WIDTH, 1)
    gathered = spread(mine, CTX, ctx_count).reshape(ctx_count * tok_block, HEAD_WIDTH)

    table, mix = route(expert_ids, expert_gates, expert_count, slots)
    places = n_y * tok_dev
    own_place = jnp.arange(places, dtype=jnp.int32) // tok_dev == y_pos
    mix = jnp.where(own_place[None, :], jnp.tile(mix, (1, n_y)), 0.0)
    mix_high = mix.astype(jnp.bfloat16)
    mix_low = (mix - mix_high.astype(jnp.float32)).astype(jnp.bfloat16)
    extra = jnp.concatenate([mix_high, mix_low], axis=1)
    extra = jnp.pad(extra, ((0, 0), (0, EXTRA - extra.shape[1])))
    gathered, table, extra = lax.optimization_barrier((gathered, table, extra))
    key_all, value_all = spread(gathered, "co", n_co)

    order = np.arange(tok_block).reshape(n_x, n_zh, n_co, tok_dev).transpose(2, 0, 1, 3)
    split = queries.reshape(n_x, n_zh, n_co, tok_dev, heads, HEAD_WIDTH)
    query_rows = jnp.transpose(split, (4, 2, 0, 1, 3, 5)).reshape(heads * tok_block, HEAD_WIDTH)
    query_pos = (zl * n_y + y_pos) * tok_block + jnp.asarray(
        np.tile(order.reshape(-1), heads), jnp.int32
    )
    key_pos = jnp.arange(key_all.shape[0], dtype=jnp.int32)
    allowed = key_pos[None, :] <= query_pos[:, None]
    scores = rows_dot(query_rows, key_all) * (1.0 / HEAD_WIDTH**0.5)
    scores = jnp.where(allowed, scores, NEG_LARGE)
    weights = jnp.exp(scores - jnp.max(scores, axis=1, keepdims=True))
    total = jnp.sum(weights, axis=1, keepdims=True)
    numer = jnp.dot(weights.astype(jnp.bfloat16), value_all, preferred_element_type=jnp.float32)
    done = (numer / total).astype(jnp.bfloat16).reshape(heads, tok_block, HEAD_WIDTH)
    heads_out = jnp.transpose(done, (1, 0, 2)).reshape(tok_block, heads * HEAD_WIDTH)

    heads_out, down_own = lax.optimization_barrier((heads_out, down_own))
    down_y = lax.ppermute(down_own, "y", swap_y)

    partial = jnp.dot(heads_out, out_weight, preferred_element_type=jnp.float32)
    partial = partial.astype(jnp.bfloat16).reshape(n_co, tok_block // n_co, width)
    partial = added(exchange(partial, "co")).astype(jnp.bfloat16)
    partial = added(exchange(partial.reshape(n_x, -1, width), "x")).astype(jnp.bfloat16)
    partial, gate_z, up_z, down_y = lax.optimization_barrier((partial, gate_z, up_z, down_y))
    projected = added(exchange(partial.reshape(n_zh, tok_dev, width), "zh"))
    mixed = (residual.astype(jnp.float32) + projected).astype(jnp.bfloat16)

    stream = mixed.astype(jnp.float32)
    mean_sq = jnp.mean(stream * stream, axis=1, keepdims=True)
    normed = (stream * lax.rsqrt(mean_sq + EPS_NORM) * norm_gain[None, :]).astype(jnp.bfloat16)

    outgoing = jnp.dot(table, normed, preferred_element_type=jnp.float32).astype(jnp.bfloat16)
    outgoing = jnp.concatenate([outgoing, extra], axis=1)
    arrived = exchange(outgoing.reshape(expert_count, slots, width + EXTRA), EXP)
    arrived = arrived.reshape(expert_count * slots, width + EXTRA)

    arrived, down_own, down_y = lax.optimization_barrier((arrived, down_own, down_y))
    rows = lax.all_gather(arrived, "y", axis=0, tiled=True)
    down_z, down_zy = lax.ppermute(down_own, "zl", swap_z), lax.ppermute(down_y, "zl", swap_z)
    rows, down_z, down_zy = lax.optimization_barrier((rows, down_z, down_zy))

    hidden = hidden_pieces(rows, zl, (gate_own, gate_z, up_own, up_z), width, n_y)
    hidden, extra = lax.optimization_barrier((hidden, rows[:, width:]))
    hidden = exchange(hidden, "y")

    result = down_slots(y_pos % 2, hidden, extra, (down_own, down_y, down_z, down_zy))
    cols = result.shape[1] - EXTRA
    result = exchange(result.reshape(expert_count, -1, cols + EXTRA), EXP)
    result = result.reshape(-1, cols + EXTRA)
    tokens = lax.dot_general(
        result[:, cols : cols + 2 * places],
        result[:, :cols],
        (((0,), (0,)), ((), ())),
        preferred_element_type=jnp.float32,
    )
    tokens = (tokens[:places] + tokens[places:]).astype(jnp.bfloat16)
    tokens = exchange(tokens.reshape(n_y, tok_dev, cols), "y")
    tokens = added(tokens.reshape(n_y // 2, 2, tok_dev, cols).transpose(1, 0, 2, 3))
    tokens = tokens.astype(jnp.bfloat16).reshape(n_y // 2, tok_dev, n_zl, 2, cols // 4)
    tokens = jnp.where(zl == 0, tokens, tokens[:, :, ::-1])
    tokens = jnp.where(y_pos < n_y // 2, tokens, tokens[:, :, :, ::-1])
    tokens = tokens.transpose(1, 2, 0, 3, 4)
    return (mixed, tokens.reshape(tok_dev, width))


def solution(mesh):
    fine = Mesh(mesh.devices.reshape(2, 8, 4, 4, 2), CTX + EXP)
    return jax.shard_map(
        on_device,
        mesh=fine,
        in_specs=(
            P(CTX, EXP),
            P(CTX, None),
            P(CTX, None),
            P(CTX + EXP, None),
            P(EXP, None),
            P(),
            P(CTX + EXP, None),
            P(CTX + EXP, None),
            P(EXP, None, CTX),
            P(EXP, None, CTX),
            P(EXP, None, CTX),
        ),
        out_specs=(P(CTX + EXP, None), P(CTX + EXP, None)),
        check_vma=False,
    )
```

```python
import jax
import jax.numpy as jnp
import numpy as np
from jax import lax
from jax.experimental import pallas as pl
from jax.experimental.pallas import tpu as pltpu
from jax.sharding import Mesh, PartitionSpec as P

HEAD_WIDTH = 128
EXTRA = 128

CTX = ("zl", "y")
EXP = ("x", "zh", "co")
EPS_NORM = 1e-06
NEG_LARGE = -1e30


def exchange(pieces, axis):
    return lax.all_to_all(pieces, axis, 0, 0, tiled=True)


def spread(value, axis, count):
    return exchange(jnp.broadcast_to(value[None], (count,) + value.shape), axis)


def added(pieces):
    return jnp.sum(pieces.astype(jnp.float32), axis=0)


def rows_dot(left, right):
    return lax.dot_general(
        left, right, (((1,), (1,)), ((), ())), preferred_element_type=jnp.float32
    )


def route(expert_ids, expert_gates, expert_count, slots):
    flat_ids = expert_ids.reshape(-1)
    tok_rows, top_count = expert_ids.shape
    owner_row = jnp.arange(tok_rows * top_count, dtype=jnp.int32) // top_count
    earlier = (flat_ids[:, None] == flat_ids[None, :]) & (owner_row[None, :] < owner_row[:, None])
    slot_ids = jnp.sum(earlier.astype(jnp.int32), axis=1).reshape(tok_rows, top_count)
    expert_hit = (
        expert_ids[None, None] == jnp.arange(expert_count, dtype=jnp.int32)[:, None, None, None]
    )
    slot_hit = slot_ids[None, None] == jnp.arange(slots, dtype=jnp.int32)[None, :, None, None]
    hits = expert_hit & slot_hit
    table = jnp.any(hits, axis=3).astype(jnp.bfloat16)
    mix = jnp.sum(jnp.where(hits, expert_gates[None, None], 0.0), axis=3)
    return table.reshape(expert_count * slots, tok_rows), mix.reshape(
        expert_count * slots, tok_rows
    )


def whole(shape):
    return pl.BlockSpec(shape, lambda *_: (0,) * len(shape))


def weight_rows(zl_ref, refs, weight):
    units = refs[0].shape[0]
    for place in range(2):
        own, other = refs[2 * place], refs[2 * place + 1]
        low = pl.ds(2 * place * units, units)
        high = pl.ds((2 * place + 1) * units, units)

        @pl.when(zl_ref[0] == 0)
        def _():
            weight[low, :] = own[...]
            weight[high, :] = other[...]

        @pl.when(zl_ref[0] != 0)
        def _():
            weight[low, :] = other[...]
            weight[high, :] = own[...]


def gated(total, units):
    gate, upper = total[: 2 * units, :], total[2 * units :, :]
    return (gate / (1.0 + jnp.exp(-gate)) * upper).astype(jnp.bfloat16)


def accumulate(weight, rows, block_refs, total):
    start = 0
    for block in block_refs:
        rows[pl.ds(start, block.shape[0]), :] = block[...]
        start += block.shape[0]

    @pl.when(pl.program_id(0) == 0)
    def _():
        total[...] = jnp.zeros_like(total)

    total[...] += rows_dot(weight[...], rows[...])


def first_kernel(zl_ref, *refs):
    blocks, weights, (out_ref, weight, rows, total) = refs[:-8], refs[-8:-4], refs[-4:]
    weight_rows(zl_ref, weights, weight)
    accumulate(weight, rows, blocks, total)

    @pl.when(pl.program_id(0) == pl.num_programs(0) - 1)
    def _():
        out_ref[...] = gated(total, weights[0].shape[0])


def last_kernel(count, place_ref, *refs):
    blocks, weights, first = refs[:count], refs[count : count + 4], refs[count + 4]
    extras, (out_ref, extra_ref, weight, rows, total, tags) = refs[count + 5 : -6], refs[-6:]
    weight_rows(place_ref, weights, weight)
    accumulate(weight, rows, blocks, total)

    @pl.when(pl.program_id(0) == pl.num_programs(0) - 1)
    def _():
        hidden = jnp.concatenate([first[...], gated(total, weights[0].shape[0])], axis=1)
        slots = hidden.shape[1]
        peers = out_ref.shape[0]
        each = slots // peers
        start = 0
        for extra in extras:
            tags[pl.ds(start, extra.shape[0]), :] = extra[...]
            start += extra.shape[0]
        held = lax.broadcasted_iota(jnp.int32, (slots, slots), 0)
        turn = held // each
        away = jnp.where(turn % 2 == 1, peers - (turn + 1) // 2, turn // 2)
        goal = (place_ref[1] + away) % peers * each + held % each
        column = lax.broadcasted_iota(jnp.int32, (slots, slots), 1)
        move = jnp.where(goal == column, 1.0, 0.0).astype(jnp.bfloat16)
        hidden = jnp.dot(hidden, move, preferred_element_type=jnp.float32).astype(jnp.bfloat16)
        half = slots // 2
        for peer in range(peers):
            out_ref[peer] = hidden[:, (peer % 2) * half : (peer % 2 + 1) * half]
        extra_ref[...] = lax.dot_general(
            move, tags[...], (((0,), (0,)), ((), ())), preferred_element_type=jnp.float32
        ).astype(jnp.bfloat16)


def row_specs(blocks, weights, step):
    return [pl.BlockSpec((b.shape[0], step), lambda k, *_: (0, k)) for b in blocks] + [
        pl.BlockSpec((w.shape[0], step), lambda k, *_: (0, k)) for w in weights
    ]


def held_scratch(units, count, step):
    return [
        pltpu.VMEM((4 * units, step), jnp.bfloat16),
        pltpu.VMEM((count, step), jnp.bfloat16),
        pltpu.VMEM((4 * units, count), jnp.float32),
    ]


def cost(units, count, width):
    return pl.CostEstimate(
        flops=8 * units * count * width,
        bytes_accessed=2 * (count + 4 * units) * width,
        transcendentals=0,
    )


def first_hidden(zl, blocks, weights, width):
    units, step = weights[0].shape[0], 1024
    count = sum(b.shape[0] for b in blocks)
    return pl.pallas_call(
        first_kernel,
        out_shape=jax.ShapeDtypeStruct((2 * units, count), jnp.bfloat16),
        grid_spec=pltpu.PrefetchScalarGridSpec(
            num_scalar_prefetch=1,
            grid=(width // step,),
            in_specs=row_specs(blocks, weights, step),
            out_specs=whole((2 * units, count)),
            scratch_shapes=held_scratch(units, count, step),
        ),
        compiler_params=pltpu.CompilerParams(vmem_limit_bytes=60 * 2**20),
        cost_estimate=cost(units, count, width),
    )(zl.reshape(1), *blocks, *weights)


def last_hidden(place, blocks, weights, first, every, width, peers):
    units, step = weights[0].shape[0], 1024
    count = sum(b.shape[0] for b in blocks)
    slots = sum(b.shape[0] for b in every)
    pieces = (peers, 2 * units, slots // 2)
    return pl.pallas_call(
        lambda *refs: last_kernel(len(blocks), *refs),
        out_shape=(
            jax.ShapeDtypeStruct(pieces, jnp.bfloat16),
            jax.ShapeDtypeStruct((slots, EXTRA), jnp.bfloat16),
        ),
        grid_spec=pltpu.PrefetchScalarGridSpec(
            num_scalar_prefetch=1,
            grid=(width // step,),
            in_specs=row_specs(blocks, weights, step)
            + [whole(first.shape)]
            + [
                pl.BlockSpec((b.shape[0], EXTRA), lambda k, *_: (0, width // EXTRA))
                for b in every
            ],
            out_specs=(whole(pieces), whole((slots, EXTRA))),
            scratch_shapes=held_scratch(units, count, step)
            + [pltpu.VMEM((slots, EXTRA), jnp.bfloat16)],
        ),
        compiler_params=pltpu.CompilerParams(vmem_limit_bytes=60 * 2**20),
        cost_estimate=cost(units, count, width),
    )(place, *blocks, *weights, first, *every)


def down_kernel(half_ref, hidden_ref, extra_ref, *refs):
    weights, out_ref, stacked, held, arrived = refs[:4], refs[4], refs[5], refs[6], refs[7]
    copies = [
        pltpu.make_async_copy(weight, held.at[i], arrived.at[i]) for i, weight in enumerate(weights)
    ]
    for copy in copies:
        copy.start()
    peers, units, count = hidden_ref.shape
    for peer in range(peers):
        for z in range(2):
            rows = pl.ds((z * peers + peer) * (units // 2), units // 2)
            stacked[rows, :] = hidden_ref[peer, z * (units // 2) : (z + 1) * (units // 2), :]
    blocks = peers // 2
    each = count // blocks
    to = lax.broadcasted_iota(jnp.int32, (count, count), 0)
    source = (to % (2 * blocks)) // 2 * each + to // (2 * blocks) * 2 + to % 2
    column = lax.broadcasted_iota(jnp.int32, (count, count), 1)
    move = jnp.where(source == column, 1.0, 0.0).astype(jnp.bfloat16)
    rows = rows_dot(move, stacked[...]).astype(jnp.bfloat16)
    cols = held.shape[2]
    extra = jnp.where(half_ref[0] == 0, extra_ref[:count, :], extra_ref[count:, :])
    extra = jnp.dot(move, extra, preferred_element_type=jnp.float32)
    out_ref[:, 4 * cols :] = extra.astype(jnp.bfloat16)
    for i, copy in enumerate(copies):
        copy.wait()
        result = jnp.dot(rows, held[i], preferred_element_type=jnp.float32)
        out_ref[:, i * cols : (i + 1) * cols] = result.astype(jnp.bfloat16)


def down_slots(half, hidden, extra, weights):
    peers, units, count = hidden.shape
    deep, cols = weights[0].shape
    out = (count, 4 * cols + EXTRA)
    return pl.pallas_call(
        down_kernel,
        out_shape=jax.ShapeDtypeStruct(out, jnp.bfloat16),
        grid_spec=pltpu.PrefetchScalarGridSpec(
            num_scalar_prefetch=1,
            grid=(1,),
            in_specs=[whole(hidden.shape), whole(extra.shape)]
            + [pl.BlockSpec(memory_space=pl.ANY)] * 4,
            out_specs=whole(out),
            scratch_shapes=[
                pltpu.VMEM((deep, count), jnp.bfloat16),
                pltpu.VMEM((4, deep, cols), jnp.bfloat16),
                pltpu.SemaphoreType.DMA((4,)),
            ],
        ),
        compiler_params=pltpu.CompilerParams(vmem_limit_bytes=60 * 2**20),
        cost_estimate=pl.CostEstimate(
            flops=8 * deep * count * cols, bytes_accessed=8 * deep * cols, transcendentals=0
        ),
    )(half.reshape(1), hidden, extra, *weights)


def on_device(
    queries,
    keys,
    values,
    residual,
    out_weight,
    norm_gain,
    expert_ids,
    expert_gates,
    w_gate,
    w_up,
    w_down,
):
    n_zl, n_y = lax.axis_size("zl"), lax.axis_size("y")
    n_x, n_zh, n_co = lax.axis_size("x"), lax.axis_size("zh"), lax.axis_size("co")
    zl, y_pos, x_pos, co = (lax.axis_index(a) for a in ("zl", "y", "x", "co"))
    ctx_count, expert_count = n_zl * n_y, n_x * n_zh * n_co
    width = residual.shape[1]
    tok_dev, top_count = expert_ids.shape
    slots = 2
    tok_block = queries.shape[0]
    heads = queries.shape[1] // HEAD_WIDTH
    swap_z = [(i, i ^ 1) for i in range(n_zl)]
    swap_y = [(i, i ^ 1) for i in range(n_y)]
    gate_own, up_own, down_own = w_gate[0].T, w_up[0].T, w_down[0]

    gate_z, up_z = lax.ppermute(gate_own, "zl", swap_z), lax.ppermute(up_own, "zl", swap_z)

    mine = jnp.where(co == 0, keys, values)
    mine = lax.dynamic_slice_in_dim(mine, x_pos * HEAD_WIDTH, HEAD_WIDTH, 1)
    gathered = spread(mine, CTX, ctx_count).reshape(ctx_count * tok_block, HEAD_WIDTH)

    table, mix = route(expert_ids, expert_gates, expert_count, slots)
    places = n_y * tok_dev
    own_place = jnp.arange(places, dtype=jnp.int32) // tok_dev == y_pos
    mix = jnp.where(own_place[None, :], jnp.tile(mix, (1, n_y)), 0.0)
    mix_high = mix.astype(jnp.bfloat16)
    mix_low = (mix - mix_high.astype(jnp.float32)).astype(jnp.bfloat16)
    extra = jnp.concatenate([mix_high, mix_low], axis=1)
    extra = jnp.pad(extra, ((0, 0), (0, EXTRA - extra.shape[1])))
    gathered, table, extra = lax.optimization_barrier((gathered, table, extra))
    key_all, value_all = spread(gathered, "co", n_co)

    order = np.arange(tok_block).reshape(n_x, n_zh, n_co, tok_dev).transpose(2, 0, 1, 3)
    split = queries.reshape(n_x, n_zh, n_co, tok_dev, heads, HEAD_WIDTH)
    query_rows = jnp.transpose(split, (4, 2, 0, 1, 3, 5)).reshape(heads * tok_block, HEAD_WIDTH)
    query_pos = (zl * n_y + y_pos) * tok_block + jnp.asarray(
        np.tile(order.reshape(-1), heads), jnp.int32
    )
    key_pos = jnp.arange(key_all.shape[0], dtype=jnp.int32)
    allowed = key_pos[None, :] <= query_pos[:, None]
    scores = rows_dot(query_rows, key_all) * (1.0 / HEAD_WIDTH**0.5)
    scores = jnp.where(allowed, scores, NEG_LARGE)
    weights = jnp.exp(scores - jnp.max(scores, axis=1, keepdims=True))
    total = jnp.sum(weights, axis=1, keepdims=True)
    numer = jnp.dot(weights.astype(jnp.bfloat16), value_all, preferred_element_type=jnp.float32)
    done = (numer / total).astype(jnp.bfloat16).reshape(heads, tok_block, HEAD_WIDTH)
    heads_out = jnp.transpose(done, (1, 0, 2)).reshape(tok_block, heads * HEAD_WIDTH)

    heads_out, down_own = lax.optimization_barrier((heads_out, down_own))
    down_y = lax.ppermute(down_own, "y", swap_y)

    partial = jnp.dot(heads_out, out_weight, preferred_element_type=jnp.float32)
    partial = partial.astype(jnp.bfloat16).reshape(n_co, tok_block // n_co, width)
    partial = added(exchange(partial, "co")).astype(jnp.bfloat16)
    partial = added(exchange(partial.reshape(n_x, -1, width), "x")).astype(jnp.bfloat16)
    partial, gate_z, up_z, down_y = lax.optimization_barrier((partial, gate_z, up_z, down_y))
    projected = added(exchange(partial.reshape(n_zh, tok_dev, width), "zh"))
    mixed = (residual.astype(jnp.float32) + projected).astype(jnp.bfloat16)

    stream = mixed.astype(jnp.float32)
    mean_sq = jnp.mean(stream * stream, axis=1, keepdims=True)
    normed = (stream * lax.rsqrt(mean_sq + EPS_NORM) * norm_gain[None, :]).astype(jnp.bfloat16)

    outgoing = jnp.dot(table, normed, preferred_element_type=jnp.float32).astype(jnp.bfloat16)
    outgoing = jnp.concatenate([outgoing, extra], axis=1)
    arrived = exchange(outgoing.reshape(expert_count, slots, width + EXTRA), EXP)
    arrived = arrived.reshape(expert_count * slots, width + EXTRA)

    arrived, down_own, down_y = lax.optimization_barrier((arrived, down_own, down_y))
    after = [(i, (i + 1) % n_y) for i in range(n_y)]
    before = [(b, a) for a, b in after]
    blocks, left, right = [arrived], arrived, arrived
    for _ in range(n_y // 2 - 1):
        left, right = lax.ppermute(left, "y", after), lax.ppermute(right, "y", before)
        blocks += [left, right]
    part = arrived.shape[0] // 2
    blocks.append(lax.ppermute(left[:part], "y", after))
    blocks.append(lax.ppermute(right[part:], "y", before))
    down_z, down_zy = lax.ppermute(down_own, "zl", swap_z), lax.ppermute(down_y, "zl", swap_z)
    weights = (gate_own, gate_z, up_own, up_z)
    first = first_hidden(zl, blocks[:5], weights, width)
    last, first, down_z, down_zy = lax.optimization_barrier((blocks[5:], first, down_z, down_zy))

    hidden, extra = last_hidden(
        jnp.stack([zl, y_pos]), last, weights, first, blocks[:5] + last, width, n_y
    )
    hidden = exchange(hidden, "y")

    result = down_slots(y_pos % 2, hidden, extra, (down_own, down_y, down_z, down_zy))
    cols = result.shape[1] - EXTRA
    result = exchange(result.reshape(expert_count, -1, cols + EXTRA), EXP)
    result = result.reshape(-1, cols + EXTRA)
    tokens = lax.dot_general(
        result[:, cols : cols + 2 * places],
        result[:, :cols],
        (((0,), (0,)), ((), ())),
        preferred_element_type=jnp.float32,
    )
    tokens = (tokens[:places] + tokens[places:]).astype(jnp.bfloat16)
    tokens = exchange(tokens.reshape(n_y, tok_dev, cols), "y")
    tokens = added(tokens.reshape(n_y // 2, 2, tok_dev, cols).transpose(1, 0, 2, 3))
    tokens = tokens.astype(jnp.bfloat16).reshape(n_y // 2, tok_dev, n_zl, 2, cols // 4)
    tokens = jnp.where(zl == 0, tokens, tokens[:, :, ::-1])
    tokens = jnp.where(y_pos < n_y // 2, tokens, tokens[:, :, :, ::-1])
    tokens = tokens.transpose(1, 2, 0, 3, 4)
    return (mixed, tokens.reshape(tok_dev, width))


def solution(mesh):
    fine = Mesh(mesh.devices.reshape(2, 8, 4, 4, 2), CTX + EXP)
    return jax.shard_map(
        on_device,
        mesh=fine,
        in_specs=(
            P(CTX, EXP),
            P(CTX, None),
            P(CTX, None),
            P(CTX + EXP, None),
            P(EXP, None),
            P(),
            P(CTX + EXP, None),
            P(CTX + EXP, None),
            P(EXP, None, CTX),
            P(EXP, None, CTX),
            P(EXP, None, CTX),
        ),
        out_specs=(P(CTX + EXP, None), P(CTX + EXP, None)),
        check_vma=False,
    )
```

```python
import jax
import jax.numpy as jnp
import numpy as np
from jax import lax
from jax.experimental import pallas as pl
from jax.experimental.pallas import tpu as pltpu
from jax.sharding import Mesh, PartitionSpec as P

HEAD_WIDTH = 128
EXTRA = 128

CTX = ("zl", "ya", "yb")
EXP = ("x", "zh", "co")
EPS_NORM = 1e-06
NEG_LARGE = -1e30


def exchange(pieces, axis):
    return lax.all_to_all(pieces, axis, 0, 0, tiled=True)


def spread(value, axis, count):
    return exchange(jnp.broadcast_to(value[None], (count,) + value.shape), axis)


def added(pieces):
    return jnp.sum(pieces.astype(jnp.float32), axis=0)


def rows_dot(left, right):
    return lax.dot_general(
        left, right, (((1,), (1,)), ((), ())), preferred_element_type=jnp.float32
    )


def route(expert_ids, expert_gates, expert_count, slots):
    flat_ids = expert_ids.reshape(-1)
    tok_rows, top_count = expert_ids.shape
    owner_row = jnp.arange(tok_rows * top_count, dtype=jnp.int32) // top_count
    earlier = (flat_ids[:, None] == flat_ids[None, :]) & (owner_row[None, :] < owner_row[:, None])
    slot_ids = jnp.sum(earlier.astype(jnp.int32), axis=1).reshape(tok_rows, top_count)
    expert_hit = (
        expert_ids[None, None] == jnp.arange(expert_count, dtype=jnp.int32)[:, None, None, None]
    )
    slot_hit = slot_ids[None, None] == jnp.arange(slots, dtype=jnp.int32)[None, :, None, None]
    hits = expert_hit & slot_hit
    table = jnp.any(hits, axis=3).astype(jnp.bfloat16)
    mix = jnp.sum(jnp.where(hits, expert_gates[None, None], 0.0), axis=3)
    return table.reshape(expert_count * slots, tok_rows), mix.reshape(
        expert_count * slots, tok_rows
    )


def whole(shape):
    return pl.BlockSpec(shape, lambda *_: (0,) * len(shape))


def weight_rows(place_ref, refs, weight):
    units = refs[0].shape[0]
    for at, ref in enumerate(refs):
        turn = (0, 2, 1, 3)[at % 4]
        start = (at // 4 * 4 + (place_ref[0] ^ turn)) * units
        weight[pl.ds(pl.multiple_of(start, 32), units), :] = ref[...]


def gated(total, units):
    gate, upper = total[: 4 * units, :], total[4 * units :, :]
    return (gate / (1.0 + jnp.exp(-gate)) * upper).astype(jnp.bfloat16)


def accumulate(weight, rows, block_refs, total):
    start = 0
    for block in block_refs:
        rows[pl.ds(start, block.shape[0]), :] = block[...]
        start += block.shape[0]

    @pl.when(pl.program_id(0) == 0)
    def _():
        total[...] = jnp.zeros_like(total)

    total[...] += rows_dot(weight[...], rows[...])


def first_kernel(place_ref, *refs):
    blocks, weights, (out_ref, weight, rows, total) = refs[:-12], refs[-12:-4], refs[-4:]
    weight_rows(place_ref, weights, weight)
    accumulate(weight, rows, blocks, total)

    @pl.when(pl.program_id(0) == pl.num_programs(0) - 1)
    def _():
        out_ref[...] = gated(total, weights[0].shape[0])


def last_kernel(count, place_ref, *refs):
    blocks, weights, first = refs[:count], refs[count : count + 8], refs[count + 8]
    extras, (out_ref, extra_ref, weight, rows, total, tags) = refs[count + 9 : -6], refs[-6:]
    weight_rows(place_ref, weights, weight)
    accumulate(weight, rows, blocks, total)

    @pl.when(pl.program_id(0) == pl.num_programs(0) - 1)
    def _():
        hidden = jnp.concatenate([first[...], gated(total, weights[0].shape[0])], axis=1)
        slots = hidden.shape[1]
        peers = out_ref.shape[0]
        each = slots // peers
        start = 0
        for extra in extras:
            tags[pl.ds(start, extra.shape[0]), :] = extra[...]
            start += extra.shape[0]
        held = lax.broadcasted_iota(jnp.int32, (slots, slots), 0)
        turn = held // each
        away = jnp.where(turn % 2 == 1, peers - (turn + 1) // 2, turn // 2)
        goal = (place_ref[1] + away) % peers * each + held % each
        column = lax.broadcasted_iota(jnp.int32, (slots, slots), 1)
        move = jnp.where(goal == column, 1.0, 0.0).astype(jnp.bfloat16)
        hidden = jnp.dot(hidden, move, preferred_element_type=jnp.float32).astype(jnp.bfloat16)
        for peer in range(peers):
            out_ref[peer] = hidden
        extra_ref[...] = lax.dot_general(
            move, tags[...], (((0,), (0,)), ((), ())), preferred_element_type=jnp.float32
        ).astype(jnp.bfloat16)


def row_specs(blocks, weights, step):
    return [pl.BlockSpec((b.shape[0], step), lambda k, *_: (0, k)) for b in blocks] + [
        pl.BlockSpec((w.shape[0], step), lambda k, *_: (0, k)) for w in weights
    ]


def held_scratch(units, count, step):
    return [
        pltpu.VMEM((8 * units, step), jnp.bfloat16),
        pltpu.VMEM((count, step), jnp.bfloat16),
        pltpu.VMEM((8 * units, count), jnp.float32),
    ]


def cost(units, count, width):
    return pl.CostEstimate(
        flops=16 * units * count * width,
        bytes_accessed=2 * (count + 8 * units) * width,
        transcendentals=0,
    )


def first_hidden(place, blocks, weights, width):
    units, step = weights[0].shape[0], 1024
    count = sum(b.shape[0] for b in blocks)
    return pl.pallas_call(
        first_kernel,
        out_shape=jax.ShapeDtypeStruct((4 * units, count), jnp.bfloat16),
        grid_spec=pltpu.PrefetchScalarGridSpec(
            num_scalar_prefetch=1,
            grid=(width // step,),
            in_specs=row_specs(blocks, weights, step),
            out_specs=whole((4 * units, count)),
            scratch_shapes=held_scratch(units, count, step),
        ),
        compiler_params=pltpu.CompilerParams(vmem_limit_bytes=60 * 2**20),
        cost_estimate=cost(units, count, width),
    )(place, *blocks, *weights)


def last_hidden(place, blocks, weights, first, every, width, peers):
    units, step = weights[0].shape[0], 1024
    count = sum(b.shape[0] for b in blocks)
    slots = sum(b.shape[0] for b in every)
    pieces = (peers, 4 * units, slots)
    return pl.pallas_call(
        lambda *refs: last_kernel(len(blocks), *refs),
        out_shape=(
            jax.ShapeDtypeStruct(pieces, jnp.bfloat16),
            jax.ShapeDtypeStruct((slots, EXTRA), jnp.bfloat16),
        ),
        grid_spec=pltpu.PrefetchScalarGridSpec(
            num_scalar_prefetch=1,
            grid=(width // step,),
            in_specs=row_specs(blocks, weights, step)
            + [whole(first.shape)]
            + [
                pl.BlockSpec((b.shape[0], EXTRA), lambda k, *_: (0, width // EXTRA))
                for b in every
            ],
            out_specs=(whole(pieces), whole((slots, EXTRA))),
            scratch_shapes=held_scratch(units, count, step)
            + [pltpu.VMEM((slots, EXTRA), jnp.bfloat16)],
        ),
        compiler_params=pltpu.CompilerParams(vmem_limit_bytes=60 * 2**20),
        cost_estimate=cost(units, count, width),
    )(place, *blocks, *weights, first, *every)


def down_kernel(hidden_ref, extra_ref, *refs):
    weights, out_ref, stacked, held, arrived = refs[:4], refs[4], refs[5], refs[6], refs[7]
    copies = [
        pltpu.make_async_copy(weight, held.at[i], arrived.at[i]) for i, weight in enumerate(weights)
    ]
    for copy in copies:
        copy.start()
    peers, units, count = hidden_ref.shape
    half = units // 2
    for peer in range(peers):
        for z in range(2):
            rows = pl.ds((z * peers + peer) * half, half)
            stacked[rows, :] = hidden_ref[peer, z * half : (z + 1) * half, :]
    each = count // peers
    to = lax.broadcasted_iota(jnp.int32, (count, count), 0)
    source = (to % (2 * peers)) // 2 * each + to // (2 * peers) * 2 + to % 2
    column = lax.broadcasted_iota(jnp.int32, (count, count), 1)
    move = jnp.where(source == column, 1.0, 0.0).astype(jnp.bfloat16)
    rows = rows_dot(move, stacked[...]).astype(jnp.bfloat16)
    cols = held.shape[2]
    extra = jnp.dot(move, extra_ref[...], preferred_element_type=jnp.float32)
    out_ref[:, 4 * cols :] = extra.astype(jnp.bfloat16)
    for i, copy in enumerate(copies):
        copy.wait()
        result = jnp.dot(rows, held[i], preferred_element_type=jnp.float32)
        out_ref[:, i * cols : (i + 1) * cols] = result.astype(jnp.bfloat16)


def down_slots(hidden, extra, weights):
    peers, units, count = hidden.shape
    deep, cols = weights[0].shape
    out = (count, 4 * cols + EXTRA)
    return pl.pallas_call(
        down_kernel,
        out_shape=jax.ShapeDtypeStruct(out, jnp.bfloat16),
        grid=(1,),
        in_specs=[whole(hidden.shape), whole(extra.shape)]
        + [pl.BlockSpec(memory_space=pl.ANY)] * 4,
        out_specs=whole(out),
        scratch_shapes=[
            pltpu.VMEM((deep, count), jnp.bfloat16),
            pltpu.VMEM((4, deep, cols), jnp.bfloat16),
            pltpu.SemaphoreType.DMA((4,)),
        ],
        compiler_params=pltpu.CompilerParams(vmem_limit_bytes=60 * 2**20),
        cost_estimate=pl.CostEstimate(
            flops=8 * deep * count * cols, bytes_accessed=8 * deep * cols, transcendentals=0
        ),
    )(hidden, extra, *weights)


def on_device(
    queries,
    keys,
    values,
    residual,
    out_weight,
    norm_gain,
    expert_ids,
    expert_gates,
    w_gate,
    w_up,
    w_down,
):
    n_zl, n_ya, n_yb = lax.axis_size("zl"), lax.axis_size("ya"), lax.axis_size("yb")
    n_x, n_zh, n_co = lax.axis_size("x"), lax.axis_size("zh"), lax.axis_size("co")
    zl, ya, yb, x_pos, co = (lax.axis_index(a) for a in ("zl", "ya", "yb", "x", "co"))
    ctx_count, expert_count = n_zl * n_ya * n_yb, n_x * n_zh * n_co
    width = residual.shape[1]
    tok_dev, top_count = expert_ids.shape
    slots = 2
    tok_block = queries.shape[0]
    heads = queries.shape[1] // HEAD_WIDTH
    swap = [(0, 1), (1, 0)]
    gate_own, up_own, down_own = w_gate[0].T, w_up[0].T, w_down[0]

    gate_z, up_z = lax.ppermute(gate_own, "zl", swap), lax.ppermute(up_own, "zl", swap)
    gate_y, up_y = lax.ppermute(gate_own, "yb", swap), lax.ppermute(up_own, "yb", swap)

    mine = jnp.where(co == 0, keys, values)
    mine = lax.dynamic_slice_in_dim(mine, x_pos * HEAD_WIDTH, HEAD_WIDTH, 1)
    gathered = spread(mine, CTX, ctx_count).reshape(ctx_count * tok_block, HEAD_WIDTH)

    table, mix = route(expert_ids, expert_gates, expert_count, slots)
    places = n_ya * tok_dev
    own_place = jnp.arange(places, dtype=jnp.int32) // tok_dev == ya
    mix = jnp.where(own_place[None, :], jnp.tile(mix, (1, n_ya)), 0.0)
    mix_high = mix.astype(jnp.bfloat16)
    mix_low = (mix - mix_high.astype(jnp.float32)).astype(jnp.bfloat16)
    extra = jnp.concatenate([mix_high, mix_low], axis=1)
    extra = jnp.pad(extra, ((0, 0), (0, EXTRA - extra.shape[1])))
    key_all, value_all = spread(gathered, "co", n_co)

    order = np.arange(tok_block).reshape(n_x, n_zh, n_co, tok_dev).transpose(2, 0, 1, 3)
    split = queries.reshape(n_x, n_zh, n_co, tok_dev, heads, HEAD_WIDTH)
    query_rows = jnp.transpose(split, (4, 2, 0, 1, 3, 5)).reshape(heads * tok_block, HEAD_WIDTH)
    query_pos = ((zl * n_ya + ya) * n_yb + yb) * tok_block + jnp.asarray(
        np.tile(order.reshape(-1), heads), jnp.int32
    )
    key_pos = jnp.arange(key_all.shape[0], dtype=jnp.int32)
    allowed = key_pos[None, :] <= query_pos[:, None]
    scores = rows_dot(query_rows, key_all) * (1.0 / HEAD_WIDTH**0.5)
    scores = jnp.where(allowed, scores, NEG_LARGE)
    weights = jnp.exp(scores - jnp.max(scores, axis=1, keepdims=True))
    total = jnp.sum(weights, axis=1, keepdims=True)
    numer = jnp.dot(weights.astype(jnp.bfloat16), value_all, preferred_element_type=jnp.float32)
    done = (numer / total).astype(jnp.bfloat16).reshape(heads, tok_block, HEAD_WIDTH)
    heads_out = jnp.transpose(done, (1, 0, 2)).reshape(tok_block, heads * HEAD_WIDTH)

    heads_out, down_own = lax.optimization_barrier((heads_out, down_own))
    down_y = lax.ppermute(down_own, "yb", swap)

    partial = jnp.dot(heads_out, out_weight, preferred_element_type=jnp.float32)
    partial = partial.astype(jnp.bfloat16).reshape(n_co, tok_block // n_co, width)
    partial = added(exchange(partial, "co")).astype(jnp.bfloat16)
    partial, gate_z, up_z = lax.optimization_barrier((partial, gate_z, up_z))
    gate_zy = lax.ppermute(gate_z, "yb", swap)
    partial = added(exchange(partial.reshape(n_x, -1, width), "x")).astype(jnp.bfloat16)
    partial, gate_y, up_y, down_y = lax.optimization_barrier((partial, gate_y, up_y, down_y))
    projected = added(exchange(partial.reshape(n_zh, tok_dev, width), "zh"))
    mixed = (residual.astype(jnp.float32) + projected).astype(jnp.bfloat16)

    stream = mixed.astype(jnp.float32)
    mean_sq = jnp.mean(stream * stream, axis=1, keepdims=True)
    normed = (stream * lax.rsqrt(mean_sq + EPS_NORM) * norm_gain[None, :]).astype(jnp.bfloat16)

    normed, gate_zy, up_z = lax.optimization_barrier((normed, gate_zy, up_z))
    up_zy = lax.ppermute(up_z, "yb", swap)
    outgoing = jnp.dot(table, normed, preferred_element_type=jnp.float32).astype(jnp.bfloat16)
    outgoing = jnp.concatenate([outgoing, extra], axis=1)
    arrived = exchange(outgoing.reshape(expert_count, slots, width + EXTRA), EXP)
    arrived = arrived.reshape(expert_count * slots, width + EXTRA)

    arrived, down_own, up_zy = lax.optimization_barrier((arrived, down_own, up_zy))
    after = [(i, (i + 1) % n_ya) for i in range(n_ya)]
    before = [(b, a) for a, b in after]
    left, right = lax.ppermute(arrived, "ya", after), lax.ppermute(arrived, "ya", before)
    down_z = lax.ppermute(down_own, "zl", swap)
    left, right, down_z, down_y = lax.optimization_barrier((left, right, down_z, down_y))
    part = arrived.shape[0] // 2
    last = [lax.ppermute(left[:part], "ya", after), lax.ppermute(right[part:], "ya", before)]
    down_zy = lax.ppermute(down_y, "zl", swap)
    weights = (gate_own, gate_z, gate_y, gate_zy, up_own, up_z, up_y, up_zy)
    blocks = [arrived, left, right]
    place = jnp.stack([zl * 2 + yb, ya])
    first = first_hidden(place, blocks, weights, width)
    last, first, down_zy = lax.optimization_barrier((last, first, down_zy))

    hidden, extra = last_hidden(place, last, weights, first, blocks + last, width, n_ya)
    hidden = exchange(hidden, "ya")

    result = down_slots(hidden, extra, (down_own, down_y, down_z, down_zy))
    cols = result.shape[1] - EXTRA
    result = exchange(result.reshape(expert_count, -1, cols + EXTRA), EXP)
    result = result.reshape(-1, cols + EXTRA)
    tokens = lax.dot_general(
        result[:, cols : cols + 2 * places],
        result[:, :cols],
        (((0,), (0,)), ((), ())),
        preferred_element_type=jnp.float32,
    )
    tokens = (tokens[:places] + tokens[places:]).astype(jnp.bfloat16)
    tokens = exchange(tokens.reshape(n_ya, tok_dev, cols), "ya")
    tokens = tokens.reshape(n_ya, tok_dev, n_zl, n_yb, cols // 4)
    tokens = jnp.where(zl == 0, tokens, tokens[:, :, ::-1])
    tokens = jnp.where(yb == 0, tokens, tokens[:, :, :, ::-1])
    tokens = tokens.transpose(1, 2, 0, 3, 4)
    return (mixed, tokens.reshape(tok_dev, width))


def solution(mesh):
    fine = Mesh(mesh.devices.reshape(2, 4, 2, 4, 4, 2), CTX + EXP)
    return jax.shard_map(
        on_device,
        mesh=fine,
        in_specs=(
            P(CTX, EXP),
            P(CTX, None),
            P(CTX, None),
            P(CTX + EXP, None),
            P(EXP, None),
            P(),
            P(CTX + EXP, None),
            P(CTX + EXP, None),
            P(EXP, None, CTX),
            P(EXP, None, CTX),
            P(EXP, None, CTX),
        ),
        out_specs=(P(CTX + EXP, None), P(CTX + EXP, None)),
        check_vma=False,
    )
```

```python
import jax
import jax.numpy as jnp
import numpy as np
from jax import lax
from jax.experimental import pallas as pl
from jax.experimental.pallas import tpu as pltpu
from jax.sharding import Mesh, PartitionSpec as P

HEAD_WIDTH = 128
EXTRA = 128

CTX = ("zl", "y")
EXP = ("x", "zh", "co")
EPS_NORM = 1e-06
NEG_LARGE = -1e30


def exchange(pieces, axis):
    return lax.all_to_all(pieces, axis, 0, 0, tiled=True)


def spread(value, axis, count):
    return exchange(jnp.broadcast_to(value[None], (count,) + value.shape), axis)


def added(pieces):
    return jnp.sum(pieces.astype(jnp.float32), axis=0)


def rows_dot(left, right):
    return lax.dot_general(
        left, right, (((1,), (1,)), ((), ())), preferred_element_type=jnp.float32
    )


def route(expert_ids, expert_gates, expert_count, slots):
    flat_ids = expert_ids.reshape(-1)
    tok_rows, top_count = expert_ids.shape
    owner_row = jnp.arange(tok_rows * top_count, dtype=jnp.int32) // top_count
    earlier = (flat_ids[:, None] == flat_ids[None, :]) & (owner_row[None, :] < owner_row[:, None])
    slot_ids = jnp.sum(earlier.astype(jnp.int32), axis=1).reshape(tok_rows, top_count)
    expert_hit = (
        expert_ids[None, None] == jnp.arange(expert_count, dtype=jnp.int32)[:, None, None, None]
    )
    slot_hit = slot_ids[None, None] == jnp.arange(slots, dtype=jnp.int32)[None, :, None, None]
    hits = expert_hit & slot_hit
    table = jnp.any(hits, axis=3).astype(jnp.bfloat16)
    mix = jnp.sum(jnp.where(hits, expert_gates[None, None], 0.0), axis=3)
    return table.reshape(expert_count * slots, tok_rows), mix.reshape(
        expert_count * slots, tok_rows
    )


def whole(shape):
    return pl.BlockSpec(shape, lambda *_: (0,) * len(shape))


def weight_rows(zl_ref, refs, weight):
    units = refs[0].shape[0]
    for place in range(2):
        own, other = refs[2 * place], refs[2 * place + 1]
        low = pl.ds(2 * place * units, units)
        high = pl.ds((2 * place + 1) * units, units)

        @pl.when(zl_ref[0] == 0)
        def _():
            weight[low, :] = own[...]
            weight[high, :] = other[...]

        @pl.when(zl_ref[0] != 0)
        def _():
            weight[low, :] = other[...]
            weight[high, :] = own[...]


def gated(total, units):
    gate, upper = total[: 2 * units, :], total[2 * units :, :]
    return (gate / (1.0 + jnp.exp(-gate)) * upper).astype(jnp.bfloat16)


def accumulate(weight, rows, block_refs, total):
    start = 0
    for block in block_refs:
        rows[pl.ds(start, block.shape[0]), :] = block[...]
        start += block.shape[0]

    @pl.when(pl.program_id(0) == 0)
    def _():
        total[...] = jnp.zeros_like(total)

    total[...] += rows_dot(weight[...], rows[...])


def first_kernel(zl_ref, *refs):
    blocks, weights, (out_ref, weight, rows, total) = refs[:-8], refs[-8:-4], refs[-4:]
    weight_rows(zl_ref, weights, weight)
    accumulate(weight, rows, blocks, total)

    @pl.when(pl.program_id(0) == pl.num_programs(0) - 1)
    def _():
        out_ref[...] = gated(total, weights[0].shape[0])


def last_kernel(count, parts, place_ref, *refs):
    blocks, weights, refs = refs[:count], refs[count : count + 4], refs[count + 4 :]
    done, extras = refs[:parts], refs[parts:-6]
    out_ref, extra_ref, weight, rows, total, tags = refs[-6:]
    weight_rows(place_ref, weights, weight)
    accumulate(weight, rows, blocks, total)

    @pl.when(pl.program_id(0) == pl.num_programs(0) - 1)
    def _():
        held = [part[...] for part in done] + [gated(total, weights[0].shape[0])]
        hidden = jnp.concatenate(held, axis=1)
        slots = hidden.shape[1]
        peers = out_ref.shape[0]
        each = slots // peers
        start = 0
        for extra in extras:
            tags[pl.ds(start, extra.shape[0]), :] = extra[...]
            start += extra.shape[0]
        held = lax.broadcasted_iota(jnp.int32, (slots, slots), 0)
        turn = held // each
        away = jnp.where(turn % 2 == 1, peers - (turn + 1) // 2, turn // 2)
        goal = (place_ref[1] + away) % peers * each + held % each
        column = lax.broadcasted_iota(jnp.int32, (slots, slots), 1)
        move = jnp.where(goal == column, 1.0, 0.0).astype(jnp.bfloat16)
        hidden = jnp.dot(hidden, move, preferred_element_type=jnp.float32).astype(jnp.bfloat16)
        half = slots // 2
        for peer in range(peers):
            out_ref[peer] = hidden[:, (peer % 2) * half : (peer % 2 + 1) * half]
        extra_ref[...] = lax.dot_general(
            move, tags[...], (((0,), (0,)), ((), ())), preferred_element_type=jnp.float32
        ).astype(jnp.bfloat16)


def row_specs(blocks, weights, step):
    return [pl.BlockSpec((b.shape[0], step), lambda k, *_: (0, k)) for b in blocks] + [
        pl.BlockSpec((w.shape[0], step), lambda k, *_: (0, k)) for w in weights
    ]


def held_scratch(units, count, step):
    return [
        pltpu.VMEM((4 * units, step), jnp.bfloat16),
        pltpu.VMEM((count, step), jnp.bfloat16),
        pltpu.VMEM((4 * units, count), jnp.float32),
    ]


def cost(units, count, width):
    return pl.CostEstimate(
        flops=8 * units * count * width,
        bytes_accessed=2 * (count + 4 * units) * width,
        transcendentals=0,
    )


def first_hidden(zl, blocks, weights, width):
    units, step = weights[0].shape[0], 1024
    count = sum(b.shape[0] for b in blocks)
    return pl.pallas_call(
        first_kernel,
        out_shape=jax.ShapeDtypeStruct((2 * units, count), jnp.bfloat16),
        grid_spec=pltpu.PrefetchScalarGridSpec(
            num_scalar_prefetch=1,
            grid=(width // step,),
            in_specs=row_specs(blocks, weights, step),
            out_specs=whole((2 * units, count)),
            scratch_shapes=held_scratch(units, count, step),
        ),
        compiler_params=pltpu.CompilerParams(vmem_limit_bytes=60 * 2**20),
        cost_estimate=cost(units, count, width),
    )(zl.reshape(1), *blocks, *weights)


def last_hidden(place, blocks, weights, first, every, width, peers):
    units, step = weights[0].shape[0], 1024
    count = sum(b.shape[0] for b in blocks)
    slots = sum(b.shape[0] for b in every)
    pieces = (peers, 2 * units, slots // 2)
    return pl.pallas_call(
        lambda *refs: last_kernel(len(blocks), len(first), *refs),
        out_shape=(
            jax.ShapeDtypeStruct(pieces, jnp.bfloat16),
            jax.ShapeDtypeStruct((slots, EXTRA), jnp.bfloat16),
        ),
        grid_spec=pltpu.PrefetchScalarGridSpec(
            num_scalar_prefetch=1,
            grid=(width // step,),
            in_specs=row_specs(blocks, weights, step)
            + [whole(part.shape) for part in first]
            + [
                pl.BlockSpec((b.shape[0], EXTRA), lambda k, *_: (0, width // EXTRA))
                for b in every
            ],
            out_specs=(whole(pieces), whole((slots, EXTRA))),
            scratch_shapes=held_scratch(units, count, step)
            + [pltpu.VMEM((slots, EXTRA), jnp.bfloat16)],
        ),
        compiler_params=pltpu.CompilerParams(vmem_limit_bytes=60 * 2**20),
        cost_estimate=cost(units, count, width),
    )(place, *blocks, *weights, *first, *every)


def down_kernel(half_ref, hidden_ref, extra_ref, *refs):
    weights, (out_ref, stacked, held, placed, arrived) = refs[:4], refs[4:]
    peers, units, count = hidden_ref.shape
    half = units // 2
    moves = [
        pltpu.make_async_copy(
            hidden_ref.at[peer, pl.ds(z * half, half), :],
            stacked.at[pl.ds((z * peers + peer) * half, half), :],
            placed.at[z * peers + peer],
        )
        for z in range(2)
        for peer in range(peers)
    ]
    copies = [
        pltpu.make_async_copy(weight, held.at[i], arrived.at[i]) for i, weight in enumerate(weights)
    ]
    for copy in moves + copies:
        copy.start()
    blocks = peers // 2
    each = count // blocks
    to = lax.broadcasted_iota(jnp.int32, (count, count), 0)
    source = (to % (2 * blocks)) // 2 * each + to // (2 * blocks) * 2 + to % 2
    column = lax.broadcasted_iota(jnp.int32, (count, count), 1)
    move = jnp.where(source == column, 1.0, 0.0).astype(jnp.bfloat16)
    for copy in moves:
        copy.wait()
    rows = rows_dot(move, stacked[...]).astype(jnp.bfloat16)
    cols = held.shape[2]
    extra = jnp.where(half_ref[0] == 0, extra_ref[:count, :], extra_ref[count:, :])
    extra = jnp.dot(move, extra, preferred_element_type=jnp.float32)
    out_ref[:, 4 * cols :] = extra.astype(jnp.bfloat16)
    for i, copy in enumerate(copies):
        copy.wait()
        result = jnp.dot(rows, held[i], preferred_element_type=jnp.float32)
        out_ref[:, i * cols : (i + 1) * cols] = result.astype(jnp.bfloat16)


def down_slots(half, hidden, extra, weights):
    peers, units, count = hidden.shape
    deep, cols = weights[0].shape
    out = (count, 4 * cols + EXTRA)
    return pl.pallas_call(
        down_kernel,
        out_shape=jax.ShapeDtypeStruct(out, jnp.bfloat16),
        grid_spec=pltpu.PrefetchScalarGridSpec(
            num_scalar_prefetch=1,
            grid=(1,),
            in_specs=[pl.BlockSpec(memory_space=pl.ANY), whole(extra.shape)]
            + [pl.BlockSpec(memory_space=pl.ANY)] * 4,
            out_specs=whole(out),
            scratch_shapes=[
                pltpu.VMEM((deep, count), jnp.bfloat16),
                pltpu.VMEM((4, deep, cols), jnp.bfloat16),
                pltpu.SemaphoreType.DMA((2 * peers,)),
                pltpu.SemaphoreType.DMA((4,)),
            ],
        ),
        compiler_params=pltpu.CompilerParams(vmem_limit_bytes=60 * 2**20),
        cost_estimate=pl.CostEstimate(
            flops=8 * deep * count * cols, bytes_accessed=8 * deep * cols, transcendentals=0
        ),
    )(half.reshape(1), hidden, extra, *weights)


def on_device(
    queries,
    keys,
    values,
    residual,
    out_weight,
    norm_gain,
    expert_ids,
    expert_gates,
    w_gate,
    w_up,
    w_down,
):
    n_zl, n_y = lax.axis_size("zl"), lax.axis_size("y")
    n_x, n_zh, n_co = lax.axis_size("x"), lax.axis_size("zh"), lax.axis_size("co")
    zl, y_pos, x_pos, co = (lax.axis_index(a) for a in ("zl", "y", "x", "co"))
    ctx_count, expert_count = n_zl * n_y, n_x * n_zh * n_co
    width = residual.shape[1]
    tok_dev, top_count = expert_ids.shape
    slots = 2
    tok_block = queries.shape[0]
    heads = queries.shape[1] // HEAD_WIDTH
    swap_z = [(i, i ^ 1) for i in range(n_zl)]
    swap_y = [(i, i ^ 1) for i in range(n_y)]
    gate_own, up_own, down_own = w_gate[0].T, w_up[0].T, w_down[0]

    gate_z, up_z = lax.ppermute(gate_own, "zl", swap_z), lax.ppermute(up_own, "zl", swap_z)

    mine = jnp.where(co == 0, keys, values)
    mine = lax.dynamic_slice_in_dim(mine, x_pos * HEAD_WIDTH, HEAD_WIDTH, 1)
    gathered = spread(mine, CTX, ctx_count).reshape(ctx_count * tok_block, HEAD_WIDTH)

    table, mix = route(expert_ids, expert_gates, expert_count, slots)
    places = n_y * tok_dev
    own_place = jnp.arange(places, dtype=jnp.int32) // tok_dev == y_pos
    mix = jnp.where(own_place[None, :], jnp.tile(mix, (1, n_y)), 0.0)
    mix_high = mix.astype(jnp.bfloat16)
    mix_low = (mix - mix_high.astype(jnp.float32)).astype(jnp.bfloat16)
    extra = jnp.concatenate([mix_high, mix_low], axis=1)
    extra = jnp.pad(extra, ((0, 0), (0, EXTRA - extra.shape[1])))
    gathered, table, extra = lax.optimization_barrier((gathered, table, extra))
    key_all, value_all = spread(gathered, "co", n_co)

    order = np.arange(tok_block).reshape(n_x, n_zh, n_co, tok_dev).transpose(2, 0, 1, 3)
    split = queries.reshape(n_x, n_zh, n_co, tok_dev, heads, HEAD_WIDTH)
    query_rows = jnp.transpose(split, (4, 2, 0, 1, 3, 5)).reshape(heads * tok_block, HEAD_WIDTH)
    query_pos = (zl * n_y + y_pos) * tok_block + jnp.asarray(
        np.tile(order.reshape(-1), heads), jnp.int32
    )
    key_pos = jnp.arange(key_all.shape[0], dtype=jnp.int32)
    allowed = key_pos[None, :] <= query_pos[:, None]
    scores = rows_dot(query_rows, key_all) * (1.0 / HEAD_WIDTH**0.5)
    scores = jnp.where(allowed, scores, NEG_LARGE)
    weights = jnp.exp(scores - jnp.max(scores, axis=1, keepdims=True))
    total = jnp.sum(weights, axis=1, keepdims=True)
    numer = jnp.dot(weights.astype(jnp.bfloat16), value_all, preferred_element_type=jnp.float32)
    done = (numer / total).astype(jnp.bfloat16).reshape(heads, tok_block, HEAD_WIDTH)
    heads_out = jnp.transpose(done, (1, 0, 2)).reshape(tok_block, heads * HEAD_WIDTH)

    partial = jnp.dot(heads_out, out_weight, preferred_element_type=jnp.float32)
    partial = partial.astype(jnp.bfloat16).reshape(n_co, tok_block // n_co, width)
    partial = added(exchange(partial, "co")).astype(jnp.bfloat16)
    partial = added(exchange(partial.reshape(n_x, -1, width), "x")).astype(jnp.bfloat16)
    partial, gate_z, up_z, down_own = lax.optimization_barrier((partial, gate_z, up_z, down_own))
    down_y = lax.ppermute(down_own, "y", swap_y)
    projected = added(exchange(partial.reshape(n_zh, tok_dev, width), "zh"))
    mixed = (residual.astype(jnp.float32) + projected).astype(jnp.bfloat16)

    stream = mixed.astype(jnp.float32)
    mean_sq = jnp.mean(stream * stream, axis=1, keepdims=True)
    normed = (stream * lax.rsqrt(mean_sq + EPS_NORM) * norm_gain[None, :]).astype(jnp.bfloat16)

    outgoing = jnp.dot(table, normed, preferred_element_type=jnp.float32).astype(jnp.bfloat16)
    outgoing = jnp.concatenate([outgoing, extra], axis=1)
    arrived = exchange(outgoing.reshape(expert_count, slots, width + EXTRA), EXP)
    arrived = arrived.reshape(expert_count * slots, width + EXTRA)

    arrived, down_own, down_y = lax.optimization_barrier((arrived, down_own, down_y))
    after = [(i, (i + 1) % n_y) for i in range(n_y)]
    before = [(b, a) for a, b in after]
    weights = (gate_own, gate_z, up_own, up_z)

    def onward(left, right):
        return lax.ppermute(left, "y", after), lax.ppermute(right, "y", before)

    one = onward(arrived, arrived)
    two = onward(*one)
    down_z = lax.ppermute(down_own, "zl", swap_z)
    two, down_z, down_y = lax.optimization_barrier((two, down_z, down_y))
    three = onward(*two)
    down_zy = lax.ppermute(down_y, "zl", swap_z)
    first = first_hidden(zl, (arrived,) + one + two, weights, width)
    three, first = lax.optimization_barrier((three, first))
    last = lax.ppermute(three[0], "y", after)
    second = first_hidden(zl, three, weights, width)
    last, second, down_zy = lax.optimization_barrier((last, second, down_zy))

    hidden, extra = last_hidden(
        jnp.stack([zl, y_pos]),
        (last,),
        weights,
        (first, second),
        (arrived,) + one + two + three + (last,),
        width,
        n_y,
    )
    hidden = exchange(hidden, "y")

    result = down_slots(y_pos % 2, hidden, extra, (down_own, down_y, down_z, down_zy))
    cols = result.shape[1] - EXTRA
    result = exchange(result.reshape(expert_count, -1, cols + EXTRA), EXP)
    result = result.reshape(-1, cols + EXTRA)
    tokens = lax.dot_general(
        result[:, cols : cols + 2 * places],
        result[:, :cols],
        (((0,), (0,)), ((), ())),
        preferred_element_type=jnp.float32,
    )
    tokens = (tokens[:places] + tokens[places:]).astype(jnp.bfloat16)
    tokens = exchange(tokens.reshape(n_y, tok_dev, cols), "y")
    tokens = added(tokens.reshape(n_y // 2, 2, tok_dev, cols).transpose(1, 0, 2, 3))
    tokens = tokens.astype(jnp.bfloat16).reshape(n_y // 2, tok_dev, n_zl, 2, cols // 4)
    tokens = jnp.where(zl == 0, tokens, tokens[:, :, ::-1])
    tokens = jnp.where(y_pos < n_y // 2, tokens, tokens[:, :, :, ::-1])
    tokens = tokens.transpose(1, 2, 0, 3, 4)
    return (mixed, tokens.reshape(tok_dev, width))


def solution(mesh):
    fine = Mesh(mesh.devices.reshape(2, 8, 4, 4, 2), CTX + EXP)
    return jax.shard_map(
        on_device,
        mesh=fine,
        in_specs=(
            P(CTX, EXP),
            P(CTX, None),
            P(CTX, None),
            P(CTX + EXP, None),
            P(EXP, None),
            P(),
            P(CTX + EXP, None),
            P(CTX + EXP, None),
            P(EXP, None, CTX),
            P(EXP, None, CTX),
            P(EXP, None, CTX),
        ),
        out_specs=(P(CTX + EXP, None), P(CTX + EXP, None)),
        check_vma=False,
    )
```

```python
import jax
import jax.numpy as jnp
import numpy as np
from jax import lax
from jax.experimental import pallas as pl
from jax.experimental.pallas import tpu as pltpu
from jax.sharding import Mesh, PartitionSpec as P

HEAD_WIDTH = 128
EXTRA = 128

CTX = ("zl", "y")
EXP = ("x", "zh", "co")
EPS_NORM = 1e-06
NEG_LARGE = -1e30


def exchange(pieces, axis):
    return lax.all_to_all(pieces, axis, 0, 0, tiled=True)


def spread(value, axis, count):
    return exchange(jnp.broadcast_to(value[None], (count,) + value.shape), axis)


def added(pieces):
    return jnp.sum(pieces.astype(jnp.float32), axis=0)


def rows_dot(left, right):
    return lax.dot_general(
        left, right, (((1,), (1,)), ((), ())), preferred_element_type=jnp.float32
    )


def whole(shape):
    return pl.BlockSpec(shape, lambda *_: (0,) * len(shape))


def dispatch_kernel(place_ref, parts_ref, gain_ref, mixed_ref, out_ref):
    parts, tokens, wide = parts_ref.shape
    peers, rows = out_ref.shape[0], out_ref.shape[1]
    width = wide - EXTRA
    tok_dev = tokens // parts
    top = EXTRA // 4
    whole_sum = parts_ref[0].astype(jnp.float32)
    for part in range(1, parts):
        whole_sum += parts_ref[part].astype(jnp.float32)
    mixed = whole_sum[:, :width].astype(jnp.bfloat16)
    for part in range(parts):

        @pl.when(place_ref[0] == part)
        def _():
            mixed_ref[...] = mixed[part * tok_dev : (part + 1) * tok_dev, :]

    stream = mixed.astype(jnp.float32)
    mean_sq = jnp.mean(stream * stream, axis=1, keepdims=True)
    normed = (stream * lax.rsqrt(mean_sq + EPS_NORM) * gain_ref[...]).astype(jnp.bfloat16)

    extra = whole_sum[:, width:]
    named = extra[:, :top]
    high, low = extra[:, top : 2 * top], extra[:, 2 * top : 3 * top]
    place = place_ref[0]
    hits, highs, lows = [], [], []
    for peer in range(peers):
        expert = peer // 2 * (2 * parts) + 2 * place + peer % 2
        match = named == (expert + 1).astype(jnp.float32)
        hits.append(jnp.sum(match.astype(jnp.float32), axis=1, keepdims=True))
        highs.append(jnp.sum(jnp.where(match, high, 0.0), axis=1, keepdims=True))
        lows.append(jnp.sum(jnp.where(match, low, 0.0), axis=1, keepdims=True))
    token = lax.broadcasted_iota(jnp.int32, (tokens, tokens), 0)
    other = lax.broadcasted_iota(jnp.int32, (tokens, tokens), 1)
    earlier = (token // tok_dev == other // tok_dev) & (other < token)
    row = lax.broadcasted_iota(jnp.int32, (rows, tokens), 0)
    column = lax.broadcasted_iota(jnp.int32, (rows, tokens), 1)
    from_block = row // 2 == column // tok_dev
    lane = lax.broadcasted_iota(jnp.int32, (tokens, EXTRA), 1)
    local = lax.broadcasted_iota(jnp.int32, (tokens, EXTRA), 0) % tok_dev
    goal = place_ref[1] * tok_dev + local
    for peer in range(peers):
        hit = hits[peer]
        hit_row = jnp.sum(jnp.where(token == other, hit, 0.0), axis=0, keepdims=True)
        rank = jnp.sum(jnp.where(earlier, hit_row, 0.0), axis=1, keepdims=True)
        rank_row = jnp.sum(jnp.where(token == other, rank, 0.0), axis=0, keepdims=True)
        take = from_block & (hit_row > 0.5) & (rank_row == (row % 2).astype(jnp.float32))
        take = jnp.where(take, 1.0, 0.0).astype(jnp.bfloat16)
        sent = jnp.dot(take, normed, preferred_element_type=jnp.float32)
        out_ref[peer, :, :width] = sent.astype(jnp.bfloat16)
        tag = jnp.where(lane == goal, highs[peer], 0.0)
        tag += jnp.where(lane == goal + 32, lows[peer], 0.0)
        tag = jnp.dot(take, tag.astype(jnp.bfloat16), preferred_element_type=jnp.float32)
        out_ref[peer, :, width:] = tag.astype(jnp.bfloat16)


def dispatch_rows(place, parts, gain, peers):
    count, tokens, wide = parts.shape
    width = wide - EXTRA
    out = (peers, 2 * count, wide)
    return pl.pallas_call(
        dispatch_kernel,
        out_shape=(
            jax.ShapeDtypeStruct((tokens // count, width), jnp.bfloat16),
            jax.ShapeDtypeStruct(out, jnp.bfloat16),
        ),
        grid_spec=pltpu.PrefetchScalarGridSpec(
            num_scalar_prefetch=1,
            grid=(1,),
            in_specs=[whole(parts.shape), whole((1, width))],
            out_specs=(whole((tokens // count, width)), whole(out)),
        ),
        compiler_params=pltpu.CompilerParams(vmem_limit_bytes=24 * 2**20),
        cost_estimate=pl.CostEstimate(
            flops=2 * peers * 2 * count * tokens * wide,
            bytes_accessed=4 * peers * count * wide,
            transcendentals=0,
        ),
    )(place, parts, gain.reshape(1, width))


def weight_rows(zl_ref, refs, weight):
    units = refs[0].shape[0]
    for place in range(2):
        own, other = refs[2 * place], refs[2 * place + 1]
        low = pl.ds(2 * place * units, units)
        high = pl.ds((2 * place + 1) * units, units)

        @pl.when(zl_ref[0] == 0)
        def _():
            weight[low, :] = own[...]
            weight[high, :] = other[...]

        @pl.when(zl_ref[0] != 0)
        def _():
            weight[low, :] = other[...]
            weight[high, :] = own[...]


def gated(total, units):
    gate, upper = total[: 2 * units, :], total[2 * units :, :]
    return (gate / (1.0 + jnp.exp(-gate)) * upper).astype(jnp.bfloat16)


def accumulate(weight, rows, block_refs, total):
    start = 0
    for block in block_refs:
        rows[pl.ds(start, block.shape[0]), :] = block[...]
        start += block.shape[0]

    @pl.when(pl.program_id(0) == 0)
    def _():
        total[...] = jnp.zeros_like(total)

    total[...] += rows_dot(weight[...], rows[...])


def first_kernel(zl_ref, *refs):
    blocks, weights, (out_ref, weight, rows, total) = refs[:-8], refs[-8:-4], refs[-4:]
    weight_rows(zl_ref, weights, weight)
    accumulate(weight, rows, blocks, total)

    @pl.when(pl.program_id(0) == pl.num_programs(0) - 1)
    def _():
        out_ref[...] = gated(total, weights[0].shape[0])


def last_kernel(count, parts, place_ref, *refs):
    blocks, weights, refs = refs[:count], refs[count : count + 4], refs[count + 4 :]
    done, extras = refs[:parts], refs[parts:-6]
    out_ref, extra_ref, weight, rows, total, tags = refs[-6:]
    weight_rows(place_ref, weights, weight)
    accumulate(weight, rows, blocks, total)

    @pl.when(pl.program_id(0) == pl.num_programs(0) - 1)
    def _():
        held = [part[...] for part in done] + [gated(total, weights[0].shape[0])]
        hidden = jnp.concatenate(held, axis=1)
        slots = hidden.shape[1]
        peers = out_ref.shape[0]
        each = slots // peers
        start = 0
        for extra in extras:
            tags[pl.ds(start, extra.shape[0]), :] = extra[...]
            start += extra.shape[0]
        held = lax.broadcasted_iota(jnp.int32, (slots, slots), 0)
        turn = held // each
        away = jnp.where(turn % 2 == 1, peers - (turn + 1) // 2, turn // 2)
        goal = (place_ref[1] + away) % peers * each + held % each
        column = lax.broadcasted_iota(jnp.int32, (slots, slots), 1)
        move = jnp.where(goal == column, 1.0, 0.0).astype(jnp.bfloat16)
        hidden = jnp.dot(hidden, move, preferred_element_type=jnp.float32).astype(jnp.bfloat16)
        half = slots // 2
        for peer in range(peers):
            out_ref[peer] = hidden[:, (peer % 2) * half : (peer % 2 + 1) * half]
        extra_ref[...] = lax.dot_general(
            move, tags[...], (((0,), (0,)), ((), ())), preferred_element_type=jnp.float32
        ).astype(jnp.bfloat16)


def row_specs(blocks, weights, step):
    return [pl.BlockSpec((b.shape[0], step), lambda k, *_: (0, k)) for b in blocks] + [
        pl.BlockSpec((w.shape[0], step), lambda k, *_: (0, k)) for w in weights
    ]


def held_scratch(units, count, step):
    return [
        pltpu.VMEM((4 * units, step), jnp.bfloat16),
        pltpu.VMEM((count, step), jnp.bfloat16),
        pltpu.VMEM((4 * units, count), jnp.float32),
    ]


def cost(units, count, width):
    return pl.CostEstimate(
        flops=8 * units * count * width,
        bytes_accessed=2 * (count + 4 * units) * width,
        transcendentals=0,
    )


def first_hidden(zl, blocks, weights, width):
    units, step = weights[0].shape[0], 1024
    count = sum(b.shape[0] for b in blocks)
    return pl.pallas_call(
        first_kernel,
        out_shape=jax.ShapeDtypeStruct((2 * units, count), jnp.bfloat16),
        grid_spec=pltpu.PrefetchScalarGridSpec(
            num_scalar_prefetch=1,
            grid=(width // step,),
            in_specs=row_specs(blocks, weights, step),
            out_specs=whole((2 * units, count)),
            scratch_shapes=held_scratch(units, count, step),
        ),
        compiler_params=pltpu.CompilerParams(vmem_limit_bytes=60 * 2**20),
        cost_estimate=cost(units, count, width),
    )(zl.reshape(1), *blocks, *weights)


def last_hidden(place, blocks, weights, first, every, width, peers):
    units, step = weights[0].shape[0], 1024
    count = sum(b.shape[0] for b in blocks)
    slots = sum(b.shape[0] for b in every)
    pieces = (peers, 2 * units, slots // 2)
    return pl.pallas_call(
        lambda *refs: last_kernel(len(blocks), len(first), *refs),
        out_shape=(
            jax.ShapeDtypeStruct(pieces, jnp.bfloat16),
            jax.ShapeDtypeStruct((slots, EXTRA), jnp.bfloat16),
        ),
        grid_spec=pltpu.PrefetchScalarGridSpec(
            num_scalar_prefetch=1,
            grid=(width // step,),
            in_specs=row_specs(blocks, weights, step)
            + [whole(part.shape) for part in first]
            + [
                pl.BlockSpec((b.shape[0], EXTRA), lambda k, *_: (0, width // EXTRA))
                for b in every
            ],
            out_specs=(whole(pieces), whole((slots, EXTRA))),
            scratch_shapes=held_scratch(units, count, step)
            + [pltpu.VMEM((slots, EXTRA), jnp.bfloat16)],
        ),
        compiler_params=pltpu.CompilerParams(vmem_limit_bytes=60 * 2**20),
        cost_estimate=cost(units, count, width),
    )(place, *blocks, *weights, *first, *every)


def down_kernel(half_ref, hidden_ref, extra_ref, *refs):
    weights, (out_ref, stacked, held, placed, arrived) = refs[:4], refs[4:]
    peers, units, count = hidden_ref.shape
    half = units // 2
    moves = [
        pltpu.make_async_copy(
            hidden_ref.at[peer, pl.ds(z * half, half), :],
            stacked.at[pl.ds((z * peers + peer) * half, half), :],
            placed.at[z * peers + peer],
        )
        for z in range(2)
        for peer in range(peers)
    ]
    copies = [
        pltpu.make_async_copy(weight, held.at[i], arrived.at[i]) for i, weight in enumerate(weights)
    ]
    for copy in moves + copies:
        copy.start()
    blocks = peers // 2
    each = count // blocks
    to = lax.broadcasted_iota(jnp.int32, (count, count), 0)
    owner = to // (2 * blocks)
    source = owner // 8 * 16 + owner % 2 * 8 + owner % 8 // 2 * 2 + to % 2
    source = (to % (2 * blocks)) // 2 * each + source
    column = lax.broadcasted_iota(jnp.int32, (count, count), 1)
    move = jnp.where(source == column, 1.0, 0.0).astype(jnp.bfloat16)
    for copy in moves:
        copy.wait()
    rows = rows_dot(move, stacked[...]).astype(jnp.bfloat16)
    cols = held.shape[2]
    extra = jnp.where(half_ref[0] == 0, extra_ref[:count, :], extra_ref[count:, :])
    extra = jnp.dot(move, extra, preferred_element_type=jnp.float32)
    out_ref[:, 4 * cols :] = extra.astype(jnp.bfloat16)
    for i, copy in enumerate(copies):
        copy.wait()
        result = jnp.dot(rows, held[i], preferred_element_type=jnp.float32)
        out_ref[:, i * cols : (i + 1) * cols] = result.astype(jnp.bfloat16)


def down_slots(half, hidden, extra, weights):
    peers, units, count = hidden.shape
    deep, cols = weights[0].shape
    out = (count, 4 * cols + EXTRA)
    return pl.pallas_call(
        down_kernel,
        out_shape=jax.ShapeDtypeStruct(out, jnp.bfloat16),
        grid_spec=pltpu.PrefetchScalarGridSpec(
            num_scalar_prefetch=1,
            grid=(1,),
            in_specs=[pl.BlockSpec(memory_space=pl.ANY), whole(extra.shape)]
            + [pl.BlockSpec(memory_space=pl.ANY)] * 4,
            out_specs=whole(out),
            scratch_shapes=[
                pltpu.VMEM((deep, count), jnp.bfloat16),
                pltpu.VMEM((4, deep, cols), jnp.bfloat16),
                pltpu.SemaphoreType.DMA((2 * peers,)),
                pltpu.SemaphoreType.DMA((4,)),
            ],
        ),
        compiler_params=pltpu.CompilerParams(vmem_limit_bytes=60 * 2**20),
        cost_estimate=pl.CostEstimate(
            flops=8 * deep * count * cols, bytes_accessed=8 * deep * cols, transcendentals=0
        ),
    )(half.reshape(1), hidden, extra, *weights)


def on_device(
    queries,
    keys,
    values,
    residual,
    out_weight,
    norm_gain,
    expert_ids,
    expert_gates,
    w_gate,
    w_up,
    w_down,
):
    n_zl, n_y = lax.axis_size("zl"), lax.axis_size("y")
    n_x, n_zh, n_co = lax.axis_size("x"), lax.axis_size("zh"), lax.axis_size("co")
    zl, y_pos, x_pos, co = (lax.axis_index(a) for a in ("zl", "y", "x", "co"))
    ctx_count, expert_count = n_zl * n_y, n_x * n_zh * n_co
    width = residual.shape[1]
    tok_dev, top_count = expert_ids.shape
    tok_block = queries.shape[0]
    heads = queries.shape[1] // HEAD_WIDTH
    swap_z = [(i, i ^ 1) for i in range(n_zl)]
    swap_y = [(i, i ^ 1) for i in range(n_y)]
    gate_own, up_own, down_own = w_gate[0].T, w_up[0].T, w_down[0]

    gate_z, up_z = lax.ppermute(gate_own, "zl", swap_z), lax.ppermute(up_own, "zl", swap_z)

    mine = jnp.where(co == 0, keys, values)
    mine = lax.dynamic_slice_in_dim(mine, x_pos * HEAD_WIDTH, HEAD_WIDTH, 1)
    gathered = spread(mine, CTX, ctx_count).reshape(ctx_count * tok_block, HEAD_WIDTH)

    key_all, value_all = spread(gathered, "co", n_co)

    order = np.arange(tok_block).reshape(n_x, n_zh, n_co, tok_dev).transpose(2, 0, 1, 3)
    split = queries.reshape(n_x, n_zh, n_co, tok_dev, heads, HEAD_WIDTH)
    query_rows = jnp.transpose(split, (4, 2, 0, 1, 3, 5)).reshape(heads * tok_block, HEAD_WIDTH)
    query_pos = (zl * n_y + y_pos) * tok_block + jnp.asarray(
        np.tile(order.reshape(-1), heads), jnp.int32
    )
    key_pos = jnp.arange(key_all.shape[0], dtype=jnp.int32)
    allowed = key_pos[None, :] <= query_pos[:, None]
    scores = rows_dot(query_rows, key_all) * (1.0 / HEAD_WIDTH**0.5)
    scores = jnp.where(allowed, scores, NEG_LARGE)
    weights = jnp.exp(scores - jnp.max(scores, axis=1, keepdims=True))
    total = jnp.sum(weights, axis=1, keepdims=True)
    numer = jnp.dot(weights.astype(jnp.bfloat16), value_all, preferred_element_type=jnp.float32)
    done = (numer / total).astype(jnp.bfloat16).reshape(heads, tok_block, HEAD_WIDTH)
    heads_out = jnp.transpose(done, (1, 0, 2)).reshape(tok_block, heads * HEAD_WIDTH)

    partial = jnp.dot(heads_out, out_weight, preferred_element_type=jnp.float32)
    partial = partial.astype(jnp.bfloat16).reshape(n_co, tok_block // n_co, width)
    partial = added(exchange(partial, "co")).astype(jnp.bfloat16)
    partial = added(exchange(partial.reshape(n_x, -1, width), "x"))
    partial, gate_z, up_z, down_own = lax.optimization_barrier((partial, gate_z, up_z, down_own))
    down_y = lax.ppermute(down_own, "y", swap_y)
    high = expert_gates.astype(jnp.bfloat16)
    low = (expert_gates - high.astype(jnp.float32)).astype(jnp.bfloat16)
    room = ((0, 0), (0, EXTRA // 4 - top_count))
    own = [(expert_ids + 1).astype(jnp.bfloat16), high, low, jnp.zeros_like(low)]
    own = jnp.concatenate([residual] + [jnp.pad(part, room) for part in own], axis=1)
    mine = jnp.arange(n_zh, dtype=jnp.int32)[:, None, None] == lax.axis_index("zh")
    own = jnp.where(mine, own[None], 0).reshape(n_zh * tok_dev, width + EXTRA)
    partial = jnp.pad(partial, ((0, 0), (0, EXTRA))) + own.astype(jnp.float32)
    parts = spread(partial.astype(jnp.bfloat16), "zh", n_zh)

    places = n_y * tok_dev
    place = jnp.stack([lax.axis_index("zh"), y_pos])
    mixed, outgoing = dispatch_rows(place, parts, norm_gain, n_x * n_co)
    arrived = exchange(outgoing, ("x", "co")).reshape(-1, width + EXTRA)

    arrived, down_own, down_y = lax.optimization_barrier((arrived, down_own, down_y))
    after = [(i, (i + 1) % n_y) for i in range(n_y)]
    before = [(b, a) for a, b in after]
    weights = (gate_own, gate_z, up_own, up_z)

    def onward(left, right):
        return lax.ppermute(left, "y", after), lax.ppermute(right, "y", before)

    one = onward(arrived, arrived)
    two = onward(*one)
    down_z = lax.ppermute(down_own, "zl", swap_z)
    two, down_z, down_y = lax.optimization_barrier((two, down_z, down_y))
    three = onward(*two)
    down_zy = lax.ppermute(down_y, "zl", swap_z)
    first = first_hidden(zl, (arrived,) + one + two, weights, width)
    three, first = lax.optimization_barrier((three, first))
    last = lax.ppermute(three[0], "y", after)
    second = first_hidden(zl, three, weights, width)
    last, second, down_zy = lax.optimization_barrier((last, second, down_zy))

    hidden, extra = last_hidden(
        jnp.stack([zl, y_pos]),
        (last,),
        weights,
        (first, second),
        (arrived,) + one + two + three + (last,),
        width,
        n_y,
    )
    hidden = exchange(hidden, "y")

    result = down_slots(y_pos % 2, hidden, extra, (down_own, down_y, down_z, down_zy))
    cols = result.shape[1] - EXTRA
    result = exchange(result.reshape(expert_count, -1, cols + EXTRA), EXP)
    result = result.reshape(-1, cols + EXTRA)
    tokens = lax.dot_general(
        result[:, cols : cols + 2 * places],
        result[:, :cols],
        (((0,), (0,)), ((), ())),
        preferred_element_type=jnp.float32,
    )
    tokens = (tokens[:places] + tokens[places:]).astype(jnp.bfloat16)
    tokens = exchange(tokens.reshape(n_y, tok_dev, cols), "y")
    tokens = added(tokens.reshape(n_y // 2, 2, tok_dev, cols).transpose(1, 0, 2, 3))
    tokens = tokens.astype(jnp.bfloat16).reshape(n_y // 2, tok_dev, n_zl, 2, cols // 4)
    tokens = jnp.where(zl == 0, tokens, tokens[:, :, ::-1])
    tokens = jnp.where(y_pos < n_y // 2, tokens, tokens[:, :, :, ::-1])
    tokens = tokens.transpose(1, 2, 0, 3, 4)
    return (mixed, tokens.reshape(tok_dev, width))


def solution(mesh):
    fine = Mesh(mesh.devices.reshape(2, 8, 4, 4, 2), CTX + EXP)
    return jax.shard_map(
        on_device,
        mesh=fine,
        in_specs=(
            P(CTX, EXP),
            P(CTX, None),
            P(CTX, None),
            P(CTX + EXP, None),
            P(EXP, None),
            P(),
            P(CTX + EXP, None),
            P(CTX + EXP, None),
            P(EXP, None, CTX),
            P(EXP, None, CTX),
            P(EXP, None, CTX),
        ),
        out_specs=(P(CTX + EXP, None), P(CTX + EXP, None)),
        check_vma=False,
    )
```

```python
import jax
import jax.numpy as jnp
import numpy as np
from jax import lax
from jax.experimental import pallas as pl
from jax.experimental.pallas import tpu as pltpu
from jax.sharding import Mesh, PartitionSpec as P

HEAD_WIDTH = 128
EXTRA = 128

CTX = ("zl", "y")
EXP = ("x", "zh", "co")
EPS_NORM = 1e-06
NEG_LARGE = -1e30


def exchange(pieces, axis):
    return lax.all_to_all(pieces, axis, 0, 0, tiled=True)


def spread(value, axis, count):
    return exchange(jnp.broadcast_to(value[None], (count,) + value.shape), axis)


def added(pieces):
    return jnp.sum(pieces.astype(jnp.float32), axis=0)


def rows_dot(left, right):
    return lax.dot_general(
        left, right, (((1,), (1,)), ((), ())), preferred_element_type=jnp.float32
    )


def whole(shape):
    return pl.BlockSpec(shape, lambda *_: (0,) * len(shape))


def dispatch_kernel(place_ref, parts_ref, gain_ref, mixed_ref, out_ref):
    parts, tokens, wide = parts_ref.shape
    peers, rows = out_ref.shape[0], out_ref.shape[1]
    width = wide - EXTRA
    tok_dev = tokens // parts
    top = EXTRA // 4
    whole_sum = parts_ref[0].astype(jnp.float32)
    for part in range(1, parts):
        whole_sum += parts_ref[part].astype(jnp.float32)
    mixed = whole_sum[:, :width].astype(jnp.bfloat16)
    for part in range(parts):

        @pl.when(place_ref[0] == part)
        def _():
            mixed_ref[...] = mixed[part * tok_dev : (part + 1) * tok_dev, :]

    stream = mixed.astype(jnp.float32)
    mean_sq = jnp.mean(stream * stream, axis=1, keepdims=True)
    normed = (stream * lax.rsqrt(mean_sq + EPS_NORM) * gain_ref[...]).astype(jnp.bfloat16)

    extra = whole_sum[:, width:]
    named = extra[:, :top]
    high, low = extra[:, top : 2 * top], extra[:, 2 * top : 3 * top]
    place = place_ref[0]
    hits, highs, lows = [], [], []
    for peer in range(peers):
        expert = peer // 2 * (2 * parts) + 2 * place + peer % 2
        match = named == (expert + 1).astype(jnp.float32)
        hits.append(jnp.sum(match.astype(jnp.float32), axis=1, keepdims=True))
        highs.append(jnp.sum(jnp.where(match, high, 0.0), axis=1, keepdims=True))
        lows.append(jnp.sum(jnp.where(match, low, 0.0), axis=1, keepdims=True))
    token = lax.broadcasted_iota(jnp.int32, (tokens, tokens), 0)
    other = lax.broadcasted_iota(jnp.int32, (tokens, tokens), 1)
    earlier = (token // tok_dev == other // tok_dev) & (other < token)
    row = lax.broadcasted_iota(jnp.int32, (rows, tokens), 0)
    column = lax.broadcasted_iota(jnp.int32, (rows, tokens), 1)
    from_block = row // 2 == column // tok_dev
    lane = lax.broadcasted_iota(jnp.int32, (tokens, EXTRA), 1)
    local = lax.broadcasted_iota(jnp.int32, (tokens, EXTRA), 0) % tok_dev
    goal = place_ref[1] * tok_dev + local
    for peer in range(peers):
        hit = hits[peer]
        hit_row = jnp.sum(jnp.where(token == other, hit, 0.0), axis=0, keepdims=True)
        rank = jnp.sum(jnp.where(earlier, hit_row, 0.0), axis=1, keepdims=True)
        rank_row = jnp.sum(jnp.where(token == other, rank, 0.0), axis=0, keepdims=True)
        take = from_block & (hit_row > 0.5) & (rank_row == (row % 2).astype(jnp.float32))
        take = jnp.where(take, 1.0, 0.0).astype(jnp.bfloat16)
        sent = jnp.dot(take, normed, preferred_element_type=jnp.float32)
        out_ref[peer, :, :width] = sent.astype(jnp.bfloat16)
        tag = jnp.where(lane == goal, highs[peer], 0.0)
        tag += jnp.where(lane == goal + 32, lows[peer], 0.0)
        tag = jnp.dot(take, tag.astype(jnp.bfloat16), preferred_element_type=jnp.float32)
        out_ref[peer, :, width:] = tag.astype(jnp.bfloat16)


def dispatch_rows(place, parts, gain, peers):
    count, tokens, wide = parts.shape
    width = wide - EXTRA
    out = (peers, 2 * count, wide)
    return pl.pallas_call(
        dispatch_kernel,
        out_shape=(
            jax.ShapeDtypeStruct((tokens // count, width), jnp.bfloat16),
            jax.ShapeDtypeStruct(out, jnp.bfloat16),
        ),
        grid_spec=pltpu.PrefetchScalarGridSpec(
            num_scalar_prefetch=1,
            grid=(1,),
            in_specs=[whole(parts.shape), whole((1, width))],
            out_specs=(whole((tokens // count, width)), whole(out)),
        ),
        compiler_params=pltpu.CompilerParams(vmem_limit_bytes=24 * 2**20),
        cost_estimate=pl.CostEstimate(
            flops=2 * peers * 2 * count * tokens * wide,
            bytes_accessed=4 * peers * count * wide,
            transcendentals=0,
        ),
    )(place, parts, gain.reshape(1, width))


def weight_rows(zl_ref, refs, weight):
    units = refs[0].shape[0]
    for place in range(2):
        own, other = refs[2 * place], refs[2 * place + 1]
        low = pl.ds(2 * place * units, units)
        high = pl.ds((2 * place + 1) * units, units)

        @pl.when(zl_ref[0] == 0)
        def _():
            weight[low, :] = own[...]
            weight[high, :] = other[...]

        @pl.when(zl_ref[0] != 0)
        def _():
            weight[low, :] = other[...]
            weight[high, :] = own[...]


def gated(total, units):
    gate, upper = total[: 2 * units, :], total[2 * units :, :]
    return (gate / (1.0 + jnp.exp(-gate)) * upper).astype(jnp.bfloat16)


def accumulate(weight, rows, block_refs, total):
    start = 0
    for block in block_refs:
        rows[pl.ds(start, block.shape[0]), :] = block[...]
        start += block.shape[0]

    @pl.when(pl.program_id(0) == 0)
    def _():
        total[...] = jnp.zeros_like(total)

    total[...] += rows_dot(weight[...], rows[...])


def first_kernel(zl_ref, *refs):
    blocks, weights, (out_ref, weight, rows, total) = refs[:-8], refs[-8:-4], refs[-4:]
    weight_rows(zl_ref, weights, weight)
    accumulate(weight, rows, blocks, total)

    @pl.when(pl.program_id(0) == pl.num_programs(0) - 1)
    def _():
        out_ref[...] = gated(total, weights[0].shape[0])


def last_kernel(count, parts, place_ref, *refs):
    blocks, weights, refs = refs[:count], refs[count : count + 4], refs[count + 4 :]
    done, extras = refs[:parts], refs[parts:-6]
    out_ref, extra_ref, weight, rows, total, tags = refs[-6:]
    weight_rows(place_ref, weights, weight)
    accumulate(weight, rows, blocks, total)

    @pl.when(pl.program_id(0) == pl.num_programs(0) - 1)
    def _():
        held = [part[...] for part in done] + [gated(total, weights[0].shape[0])]
        hidden = jnp.concatenate(held, axis=1)
        slots = hidden.shape[1]
        peers = out_ref.shape[0]
        each = slots // peers
        start = 0
        for extra in extras:
            tags[pl.ds(start, extra.shape[0]), :] = extra[...]
            start += extra.shape[0]
        held = lax.broadcasted_iota(jnp.int32, (slots, 1), 0)
        turn = held >> (each.bit_length() - 1)
        away = jnp.where(turn & 1 == 1, peers - ((turn + 1) >> 1), turn >> 1)
        goal = ((place_ref[1] + away) & (peers - 1)) * each + (held & (each - 1))
        column = lax.broadcasted_iota(jnp.int32, (slots, slots), 1)
        move = jnp.where(goal == column, 1.0, 0.0).astype(jnp.bfloat16)
        hidden = jnp.dot(hidden, move, preferred_element_type=jnp.float32).astype(jnp.bfloat16)
        half = slots // 2
        for peer in range(peers):
            out_ref[peer] = hidden[:, (peer % 2) * half : (peer % 2 + 1) * half]
        extra_ref[...] = lax.dot_general(
            move, tags[...], (((0,), (0,)), ((), ())), preferred_element_type=jnp.float32
        ).astype(jnp.bfloat16)


def row_specs(blocks, weights, step):
    return [pl.BlockSpec((b.shape[0], step), lambda k, *_: (0, k)) for b in blocks] + [
        pl.BlockSpec((w.shape[0], step), lambda k, *_: (0, k)) for w in weights
    ]


def held_scratch(units, count, step):
    return [
        pltpu.VMEM((4 * units, step), jnp.bfloat16),
        pltpu.VMEM((count, step), jnp.bfloat16),
        pltpu.VMEM((4 * units, count), jnp.float32),
    ]


def cost(units, count, width):
    return pl.CostEstimate(
        flops=8 * units * count * width,
        bytes_accessed=2 * (count + 4 * units) * width,
        transcendentals=0,
    )


def first_hidden(zl, blocks, weights, width):
    units, step = weights[0].shape[0], 1024
    count = sum(b.shape[0] for b in blocks)
    return pl.pallas_call(
        first_kernel,
        out_shape=jax.ShapeDtypeStruct((2 * units, count), jnp.bfloat16),
        grid_spec=pltpu.PrefetchScalarGridSpec(
            num_scalar_prefetch=1,
            grid=(width // step,),
            in_specs=row_specs(blocks, weights, step),
            out_specs=whole((2 * units, count)),
            scratch_shapes=held_scratch(units, count, step),
        ),
        compiler_params=pltpu.CompilerParams(vmem_limit_bytes=24 * 2**20),
        cost_estimate=cost(units, count, width),
    )(zl.reshape(1), *blocks, *weights)


def last_hidden(place, blocks, weights, first, every, width, peers):
    units, step = weights[0].shape[0], 1024
    count = sum(b.shape[0] for b in blocks)
    slots = sum(b.shape[0] for b in every)
    pieces = (peers, 2 * units, slots // 2)
    return pl.pallas_call(
        lambda *refs: last_kernel(len(blocks), len(first), *refs),
        out_shape=(
            jax.ShapeDtypeStruct(pieces, jnp.bfloat16),
            jax.ShapeDtypeStruct((slots, EXTRA), jnp.bfloat16),
        ),
        grid_spec=pltpu.PrefetchScalarGridSpec(
            num_scalar_prefetch=1,
            grid=(width // step,),
            in_specs=row_specs(blocks, weights, step)
            + [whole(part.shape) for part in first]
            + [
                pl.BlockSpec((b.shape[0], EXTRA), lambda k, *_: (0, width // EXTRA))
                for b in every
            ],
            out_specs=(whole(pieces), whole((slots, EXTRA))),
            scratch_shapes=held_scratch(units, count, step)
            + [pltpu.VMEM((slots, EXTRA), jnp.bfloat16)],
        ),
        compiler_params=pltpu.CompilerParams(vmem_limit_bytes=24 * 2**20),
        cost_estimate=cost(units, count, width),
    )(place, *blocks, *weights, *first, *every)


def down_kernel(half_ref, hidden_ref, extra_ref, *refs):
    weights, (out_ref, stacked, held, placed, arrived) = refs[:4], refs[4:]
    peers, units, count = hidden_ref.shape
    half = units // 2
    moves = [
        pltpu.make_async_copy(
            hidden_ref.at[peer, pl.ds(z * half, half), :],
            stacked.at[pl.ds((z * peers + peer) * half, half), :],
            placed.at[z * peers + peer],
        )
        for z in range(2)
        for peer in range(peers)
    ]
    copies = [
        pltpu.make_async_copy(weight, held.at[i], arrived.at[i]) for i, weight in enumerate(weights)
    ]
    for copy in moves + copies:
        copy.start()
    blocks = peers // 2
    each = count // blocks
    to = lax.broadcasted_iota(jnp.int32, (count, 1), 0)
    owner = to >> blocks.bit_length()
    source = (owner >> 3) * 16 + (owner & 1) * 8 + ((owner & 7) >> 1) * 2 + (to & 1)
    source = ((to & (2 * blocks - 1)) >> 1) * each + source
    column = lax.broadcasted_iota(jnp.int32, (count, count), 1)
    move = jnp.where(source == column, 1.0, 0.0).astype(jnp.bfloat16)
    for copy in moves:
        copy.wait()
    rows = rows_dot(move, stacked[...]).astype(jnp.bfloat16)
    cols = held.shape[2]
    extra = jnp.where(half_ref[0] == 0, extra_ref[:count, :], extra_ref[count:, :])
    extra = jnp.dot(move, extra, preferred_element_type=jnp.float32)
    out_ref[:, 4 * cols :] = extra.astype(jnp.bfloat16)
    for i, copy in enumerate(copies):
        copy.wait()
        result = jnp.dot(rows, held[i], preferred_element_type=jnp.float32)
        out_ref[:, i * cols : (i + 1) * cols] = result.astype(jnp.bfloat16)


def down_slots(half, hidden, extra, weights):
    peers, units, count = hidden.shape
    deep, cols = weights[0].shape
    out = (count, 4 * cols + EXTRA)
    return pl.pallas_call(
        down_kernel,
        out_shape=jax.ShapeDtypeStruct(out, jnp.bfloat16),
        grid_spec=pltpu.PrefetchScalarGridSpec(
            num_scalar_prefetch=1,
            grid=(1,),
            in_specs=[pl.BlockSpec(memory_space=pl.ANY), whole(extra.shape)]
            + [pl.BlockSpec(memory_space=pl.ANY)] * 4,
            out_specs=whole(out),
            scratch_shapes=[
                pltpu.VMEM((deep, count), jnp.bfloat16),
                pltpu.VMEM((4, deep, cols), jnp.bfloat16),
                pltpu.SemaphoreType.DMA((2 * peers,)),
                pltpu.SemaphoreType.DMA((4,)),
            ],
        ),
        compiler_params=pltpu.CompilerParams(vmem_limit_bytes=60 * 2**20),
        cost_estimate=pl.CostEstimate(
            flops=8 * deep * count * cols, bytes_accessed=8 * deep * cols, transcendentals=0
        ),
    )(half.reshape(1), hidden, extra, *weights)


def on_device(
    queries,
    keys,
    values,
    residual,
    out_weight,
    norm_gain,
    expert_ids,
    expert_gates,
    w_gate,
    w_up,
    w_down,
):
    n_zl, n_y = lax.axis_size("zl"), lax.axis_size("y")
    n_x, n_zh, n_co = lax.axis_size("x"), lax.axis_size("zh"), lax.axis_size("co")
    zl, y_pos, x_pos, co = (lax.axis_index(a) for a in ("zl", "y", "x", "co"))
    ctx_count, expert_count = n_zl * n_y, n_x * n_zh * n_co
    width = residual.shape[1]
    tok_dev, top_count = expert_ids.shape
    tok_block = queries.shape[0]
    heads = queries.shape[1] // HEAD_WIDTH
    swap_z = [(i, i ^ 1) for i in range(n_zl)]
    swap_y = [(i, i ^ 1) for i in range(n_y)]
    gate_own, up_own, down_own = w_gate[0].T, w_up[0].T, w_down[0]

    gate_z, up_z = lax.ppermute(gate_own, "zl", swap_z), lax.ppermute(up_own, "zl", swap_z)

    mine = jnp.where(co == 0, keys, values)
    mine = lax.dynamic_slice_in_dim(mine, x_pos * HEAD_WIDTH, HEAD_WIDTH, 1)
    gathered = spread(mine, CTX, ctx_count).reshape(ctx_count * tok_block, HEAD_WIDTH)

    key_all, value_all = spread(gathered, "co", n_co)

    order = np.arange(tok_block).reshape(n_x, n_zh, n_co, tok_dev).transpose(2, 0, 1, 3)
    split = queries.reshape(n_x, n_zh, n_co, tok_dev, heads, HEAD_WIDTH)
    query_rows = jnp.transpose(split, (4, 2, 0, 1, 3, 5)).reshape(heads * tok_block, HEAD_WIDTH)
    query_pos = (zl * n_y + y_pos) * tok_block + jnp.asarray(
        np.tile(order.reshape(-1), heads), jnp.int32
    )
    key_pos = jnp.arange(key_all.shape[0], dtype=jnp.int32)
    allowed = key_pos[None, :] <= query_pos[:, None]
    scores = rows_dot(query_rows, key_all) * (1.0 / HEAD_WIDTH**0.5)
    scores = jnp.where(allowed, scores, NEG_LARGE)
    weights = jnp.exp(scores - jnp.max(scores, axis=1, keepdims=True))
    total = jnp.sum(weights, axis=1, keepdims=True)
    numer = jnp.dot(weights.astype(jnp.bfloat16), value_all, preferred_element_type=jnp.float32)
    done = (numer / total).astype(jnp.bfloat16).reshape(heads, tok_block, HEAD_WIDTH)
    heads_out = jnp.transpose(done, (1, 0, 2)).reshape(tok_block, heads * HEAD_WIDTH)

    partial = jnp.dot(heads_out, out_weight, preferred_element_type=jnp.float32)
    partial = partial.astype(jnp.bfloat16).reshape(n_co, tok_block // n_co, width)
    partial = added(exchange(partial, "co")).astype(jnp.bfloat16)
    partial = added(exchange(partial.reshape(n_x, -1, width), "x"))
    partial, gate_z, up_z, down_own = lax.optimization_barrier((partial, gate_z, up_z, down_own))
    down_y = lax.ppermute(down_own, "y", swap_y)
    high = expert_gates.astype(jnp.bfloat16)
    low = (expert_gates - high.astype(jnp.float32)).astype(jnp.bfloat16)
    room = ((0, 0), (0, EXTRA // 4 - top_count))
    own = [(expert_ids + 1).astype(jnp.bfloat16), high, low, jnp.zeros_like(low)]
    own = jnp.concatenate([residual] + [jnp.pad(part, room) for part in own], axis=1)
    mine = jnp.arange(n_zh, dtype=jnp.int32)[:, None, None] == lax.axis_index("zh")
    own = jnp.where(mine, own[None], 0).reshape(n_zh * tok_dev, width + EXTRA)
    partial = jnp.pad(partial, ((0, 0), (0, EXTRA))) + own.astype(jnp.float32)
    parts = spread(partial.astype(jnp.bfloat16), "zh", n_zh)

    places = n_y * tok_dev
    place = jnp.stack([lax.axis_index("zh"), y_pos])
    mixed, outgoing = dispatch_rows(place, parts, norm_gain, n_x * n_co)
    arrived = exchange(outgoing, ("x", "co")).reshape(-1, width + EXTRA)

    arrived, down_own, down_y = lax.optimization_barrier((arrived, down_own, down_y))
    after = [(i, (i + 1) % n_y) for i in range(n_y)]
    before = [(b, a) for a, b in after]
    weights = (gate_own, gate_z, up_own, up_z)

    def onward(left, right):
        return lax.ppermute(left, "y", after), lax.ppermute(right, "y", before)

    one = onward(arrived, arrived)
    two = onward(*one)
    down_z = lax.ppermute(down_own, "zl", swap_z)
    two, down_z, down_y = lax.optimization_barrier((two, down_z, down_y))
    three = onward(*two)
    down_zy = lax.ppermute(down_y, "zl", swap_z)
    first = first_hidden(zl, (arrived,) + one + two, weights, width)
    three, first = lax.optimization_barrier((three, first))
    last = lax.ppermute(three[0], "y", after)
    second = first_hidden(zl, three, weights, width)
    last, second, down_zy = lax.optimization_barrier((last, second, down_zy))

    hidden, extra = last_hidden(
        jnp.stack([zl, y_pos]),
        (last,),
        weights,
        (first, second),
        (arrived,) + one + two + three + (last,),
        width,
        n_y,
    )
    hidden = exchange(hidden, "y")

    result = down_slots(y_pos % 2, hidden, extra, (down_own, down_y, down_z, down_zy))
    cols = result.shape[1] - EXTRA
    result = exchange(result.reshape(expert_count, -1, cols + EXTRA), EXP)
    result = result.reshape(-1, cols + EXTRA)
    tokens = lax.dot_general(
        result[:, cols : cols + 2 * places],
        result[:, :cols],
        (((0,), (0,)), ((), ())),
        preferred_element_type=jnp.float32,
    )
    tokens = (tokens[:places] + tokens[places:]).astype(jnp.bfloat16)
    tokens = exchange(tokens.reshape(n_y, tok_dev, cols), "y")
    tokens = added(tokens.reshape(n_y // 2, 2, tok_dev, cols).transpose(1, 0, 2, 3))
    tokens = tokens.astype(jnp.bfloat16).reshape(n_y // 2, tok_dev, n_zl, 2, cols // 4)
    tokens = jnp.where(zl == 0, tokens, tokens[:, :, ::-1])
    tokens = jnp.where(y_pos < n_y // 2, tokens, tokens[:, :, :, ::-1])
    tokens = tokens.transpose(1, 2, 0, 3, 4)
    return (mixed, tokens.reshape(tok_dev, width))


def solution(mesh):
    fine = Mesh(mesh.devices.reshape(2, 8, 4, 4, 2), CTX + EXP)
    return jax.shard_map(
        on_device,
        mesh=fine,
        in_specs=(
            P(CTX, EXP),
            P(CTX, None),
            P(CTX, None),
            P(CTX + EXP, None),
            P(EXP, None),
            P(),
            P(CTX + EXP, None),
            P(CTX + EXP, None),
            P(EXP, None, CTX),
            P(EXP, None, CTX),
            P(EXP, None, CTX),
        ),
        out_specs=(P(CTX + EXP, None), P(CTX + EXP, None)),
        check_vma=False,
    )
```

```python
import jax
import jax.numpy as jnp
import numpy as np
from jax import lax
from jax.experimental import pallas as pl
from jax.experimental.pallas import tpu as pltpu
from jax.sharding import Mesh, PartitionSpec as P

HEAD_WIDTH = 128
EXTRA = 128

CTX = ("zl", "y")
EXP = ("x", "zh", "co")
EPS_NORM = 1e-06
NEG_LARGE = -1e30


def exchange(pieces, axis):
    return lax.all_to_all(pieces, axis, 0, 0, tiled=True)


def spread(value, axis, count):
    return exchange(jnp.broadcast_to(value[None], (count,) + value.shape), axis)


def added(pieces):
    return jnp.sum(pieces.astype(jnp.float32), axis=0)


def rows_dot(left, right):
    return lax.dot_general(
        left, right, (((1,), (1,)), ((), ())), preferred_element_type=jnp.float32
    )


def whole(shape):
    return pl.BlockSpec(shape, lambda *_: (0,) * len(shape))


def dispatch_kernel(place_ref, parts_ref, gain_ref, mixed_ref, out_ref):
    parts, tokens, wide = parts_ref.shape
    peers, rows = out_ref.shape[0], out_ref.shape[1]
    width = wide - EXTRA
    tok_dev = tokens // parts
    top = EXTRA // 4
    whole_sum = parts_ref[0].astype(jnp.float32)
    for part in range(1, parts):
        whole_sum += parts_ref[part].astype(jnp.float32)
    mixed = whole_sum[:, :width].astype(jnp.bfloat16)
    for part in range(parts):

        @pl.when(place_ref[0] == part)
        def _():
            mixed_ref[...] = mixed[part * tok_dev : (part + 1) * tok_dev, :]

    stream = mixed.astype(jnp.float32)
    mean_sq = jnp.mean(stream * stream, axis=1, keepdims=True)
    normed = (stream * lax.rsqrt(mean_sq + EPS_NORM) * gain_ref[...]).astype(jnp.bfloat16)

    extra = whole_sum[:, width:]
    named = extra[:, :top]
    high, low = extra[:, top : 2 * top], extra[:, 2 * top : 3 * top]
    place = place_ref[0]
    hits, highs, lows = [], [], []
    for peer in range(peers):
        expert = peer // 2 * (2 * parts) + 2 * place + peer % 2
        match = named == (expert + 1).astype(jnp.float32)
        hits.append(jnp.sum(match.astype(jnp.float32), axis=1, keepdims=True))
        highs.append(jnp.sum(jnp.where(match, high, 0.0), axis=1, keepdims=True))
        lows.append(jnp.sum(jnp.where(match, low, 0.0), axis=1, keepdims=True))
    token = lax.broadcasted_iota(jnp.int32, (tokens, tokens), 0)
    other = lax.broadcasted_iota(jnp.int32, (tokens, tokens), 1)
    earlier = (token // tok_dev == other // tok_dev) & (other < token)
    row = lax.broadcasted_iota(jnp.int32, (rows, tokens), 0)
    column = lax.broadcasted_iota(jnp.int32, (rows, tokens), 1)
    from_block = row // 2 == column // tok_dev
    lane = lax.broadcasted_iota(jnp.int32, (tokens, EXTRA), 1)
    local = lax.broadcasted_iota(jnp.int32, (tokens, EXTRA), 0) % tok_dev
    goal = place_ref[1] * tok_dev + local
    for peer in range(peers):
        hit = hits[peer]
        hit_row = jnp.sum(jnp.where(token == other, hit, 0.0), axis=0, keepdims=True)
        rank = jnp.sum(jnp.where(earlier, hit_row, 0.0), axis=1, keepdims=True)
        rank_row = jnp.sum(jnp.where(token == other, rank, 0.0), axis=0, keepdims=True)
        take = from_block & (hit_row > 0.5) & (rank_row == (row % 2).astype(jnp.float32))
        take = jnp.where(take, 1.0, 0.0).astype(jnp.bfloat16)
        sent = jnp.dot(take, normed, preferred_element_type=jnp.float32)
        out_ref[peer, :, :width] = sent.astype(jnp.bfloat16)
        tag = jnp.where(lane == goal, highs[peer], 0.0)
        tag += jnp.where(lane == goal + 32, lows[peer], 0.0)
        tag = jnp.dot(take, tag.astype(jnp.bfloat16), preferred_element_type=jnp.float32)
        out_ref[peer, :, width:] = tag.astype(jnp.bfloat16)


def dispatch_rows(place, parts, gain, peers):
    count, tokens, wide = parts.shape
    width = wide - EXTRA
    out = (peers, 2 * count, wide)
    return pl.pallas_call(
        dispatch_kernel,
        out_shape=(
            jax.ShapeDtypeStruct((tokens // count, width), jnp.bfloat16),
            jax.ShapeDtypeStruct(out, jnp.bfloat16),
        ),
        grid_spec=pltpu.PrefetchScalarGridSpec(
            num_scalar_prefetch=1,
            grid=(1,),
            in_specs=[whole(parts.shape), whole((1, width))],
            out_specs=(whole((tokens // count, width)), whole(out)),
        ),
        compiler_params=pltpu.CompilerParams(vmem_limit_bytes=24 * 2**20),
        cost_estimate=pl.CostEstimate(
            flops=2 * peers * 2 * count * tokens * wide,
            bytes_accessed=4 * peers * count * wide,
            transcendentals=0,
        ),
    )(place, parts, gain.reshape(1, width))


def weight_rows(zl_ref, refs, weight):
    units = refs[0].shape[0]
    for place in range(2):
        own, other = refs[2 * place], refs[2 * place + 1]
        low = pl.ds(2 * place * units, units)
        high = pl.ds((2 * place + 1) * units, units)

        @pl.when(zl_ref[0] == 0)
        def _():
            weight[low, :] = own[...]
            weight[high, :] = other[...]

        @pl.when(zl_ref[0] != 0)
        def _():
            weight[low, :] = other[...]
            weight[high, :] = own[...]


def gated(total, units):
    gate, upper = total[: 2 * units, :], total[2 * units :, :]
    return (gate / (1.0 + jnp.exp(-gate)) * upper).astype(jnp.bfloat16)


def accumulate(weight, rows, block_refs, total):
    start = 0
    for block in block_refs:
        rows[pl.ds(start, block.shape[0]), :] = block[...]
        start += block.shape[0]

    @pl.when(pl.program_id(0) == 0)
    def _():
        total[...] = jnp.zeros_like(total)

    total[...] += rows_dot(weight[...], rows[...])


def first_kernel(zl_ref, *refs):
    blocks, weights, (out_ref, weight, rows, total) = refs[:-8], refs[-8:-4], refs[-4:]
    weight_rows(zl_ref, weights, weight)
    accumulate(weight, rows, blocks, total)

    @pl.when(pl.program_id(0) == pl.num_programs(0) - 1)
    def _():
        out_ref[...] = gated(total, weights[0].shape[0])


def last_kernel(count, parts, place_ref, *refs):
    blocks, weights, refs = refs[:count], refs[count : count + 4], refs[count + 4 :]
    done, extras = refs[:parts], refs[parts:-6]
    out_ref, extra_ref, weight, rows, total, tags = refs[-6:]
    weight_rows(place_ref, weights, weight)
    accumulate(weight, rows, blocks, total)

    @pl.when(pl.program_id(0) == pl.num_programs(0) - 1)
    def _():
        held = [part[...] for part in done] + [gated(total, weights[0].shape[0])]
        hidden = jnp.concatenate(held, axis=1)
        slots = hidden.shape[1]
        peers = out_ref.shape[0]
        each = slots // peers
        start = 0
        for extra in extras:
            tags[pl.ds(start, extra.shape[0]), :] = extra[...]
            start += extra.shape[0]
        held = lax.broadcasted_iota(jnp.int32, (slots, 1), 0)
        turn = held >> (each.bit_length() - 1)
        away = jnp.where(turn & 1 == 1, peers - ((turn + 1) >> 1), turn >> 1)
        goal = ((place_ref[1] + away) & (peers - 1)) * each + (held & (each - 1))
        column = lax.broadcasted_iota(jnp.int32, (slots, slots), 1)
        move = jnp.where(goal == column, 1.0, 0.0).astype(jnp.bfloat16)
        hidden = jnp.dot(hidden, move, preferred_element_type=jnp.float32).astype(jnp.bfloat16)
        half = slots // 2
        for peer in range(peers):
            out_ref[peer] = hidden[:, (peer % 2) * half : (peer % 2 + 1) * half]
        extra_ref[...] = lax.dot_general(
            move, tags[...], (((0,), (0,)), ((), ())), preferred_element_type=jnp.float32
        ).astype(jnp.bfloat16)


def row_specs(blocks, weights, step):
    return [pl.BlockSpec((b.shape[0], step), lambda k, *_: (0, k)) for b in blocks] + [
        pl.BlockSpec((w.shape[0], step), lambda k, *_: (0, k)) for w in weights
    ]


def held_scratch(units, count, step):
    return [
        pltpu.VMEM((4 * units, step), jnp.bfloat16),
        pltpu.VMEM((count, step), jnp.bfloat16),
        pltpu.VMEM((4 * units, count), jnp.float32),
    ]


def cost(units, count, width):
    return pl.CostEstimate(
        flops=8 * units * count * width,
        bytes_accessed=2 * (count + 4 * units) * width,
        transcendentals=0,
    )


def first_hidden(zl, blocks, weights, width):
    units, step = weights[0].shape[0], 1024
    count = sum(b.shape[0] for b in blocks)
    return pl.pallas_call(
        first_kernel,
        out_shape=jax.ShapeDtypeStruct((2 * units, count), jnp.bfloat16),
        grid_spec=pltpu.PrefetchScalarGridSpec(
            num_scalar_prefetch=1,
            grid=(width // step,),
            in_specs=row_specs(blocks, weights, step),
            out_specs=whole((2 * units, count)),
            scratch_shapes=held_scratch(units, count, step),
        ),
        compiler_params=pltpu.CompilerParams(vmem_limit_bytes=24 * 2**20),
        cost_estimate=cost(units, count, width),
    )(zl.reshape(1), *blocks, *weights)


def last_hidden(place, blocks, weights, first, every, width, peers):
    units, step = weights[0].shape[0], 1024
    count = sum(b.shape[0] for b in blocks)
    slots = sum(b.shape[0] for b in every)
    pieces = (peers, 2 * units, slots // 2)
    return pl.pallas_call(
        lambda *refs: last_kernel(len(blocks), len(first), *refs),
        out_shape=(
            jax.ShapeDtypeStruct(pieces, jnp.bfloat16),
            jax.ShapeDtypeStruct((slots, EXTRA), jnp.bfloat16),
        ),
        grid_spec=pltpu.PrefetchScalarGridSpec(
            num_scalar_prefetch=1,
            grid=(width // step,),
            in_specs=row_specs(blocks, weights, step)
            + [whole(part.shape) for part in first]
            + [
                pl.BlockSpec((b.shape[0], EXTRA), lambda k, *_: (0, width // EXTRA))
                for b in every
            ],
            out_specs=(whole(pieces), whole((slots, EXTRA))),
            scratch_shapes=held_scratch(units, count, step)
            + [pltpu.VMEM((slots, EXTRA), jnp.bfloat16)],
        ),
        compiler_params=pltpu.CompilerParams(vmem_limit_bytes=24 * 2**20),
        cost_estimate=cost(units, count, width),
    )(place, *blocks, *weights, *first, *every)


def down_kernel(half_ref, hidden_ref, extra_ref, *refs):
    weights, (out_ref, stacked, held, placed, arrived) = refs[:4], refs[4:]
    peers, units, count = hidden_ref.shape
    half = units // 2
    moves = [
        pltpu.make_async_copy(
            hidden_ref.at[peer, pl.ds(z * half, half), :],
            stacked.at[pl.ds((z * peers + peer) * half, half), :],
            placed.at[z * peers + peer],
        )
        for z in range(2)
        for peer in range(peers)
    ]
    copies = [
        pltpu.make_async_copy(weight, held.at[i], arrived.at[i]) for i, weight in enumerate(weights)
    ]
    for copy in moves + copies:
        copy.start()
    blocks = peers // 2
    each = count // blocks
    to = lax.broadcasted_iota(jnp.int32, (count, 1), 0)
    owner = to >> blocks.bit_length()
    source = (owner >> 3) * 16 + (owner & 1) * 8 + ((owner & 7) >> 1) * 2 + (to & 1)
    source = ((to & (2 * blocks - 1)) >> 1) * each + source
    column = lax.broadcasted_iota(jnp.int32, (count, count), 1)
    move = jnp.where(source == column, 1.0, 0.0).astype(jnp.bfloat16)
    for copy in moves:
        copy.wait()
    rows = rows_dot(move, stacked[...]).astype(jnp.bfloat16)
    cols = held.shape[2]
    extra = jnp.where(half_ref[0] == 0, extra_ref[:count, :], extra_ref[count:, :])
    extra = jnp.dot(move, extra, preferred_element_type=jnp.float32)
    out_ref[:, 4 * cols :] = extra.astype(jnp.bfloat16)
    for i, copy in enumerate(copies):
        copy.wait()
        result = jnp.dot(rows, held[i], preferred_element_type=jnp.float32)
        out_ref[:, i * cols : (i + 1) * cols] = result.astype(jnp.bfloat16)


def down_slots(half, hidden, extra, weights):
    peers, units, count = hidden.shape
    deep, cols = weights[0].shape
    out = (count, 4 * cols + EXTRA)
    return pl.pallas_call(
        down_kernel,
        out_shape=jax.ShapeDtypeStruct(out, jnp.bfloat16),
        grid_spec=pltpu.PrefetchScalarGridSpec(
            num_scalar_prefetch=1,
            grid=(1,),
            in_specs=[pl.BlockSpec(memory_space=pl.ANY), whole(extra.shape)]
            + [pl.BlockSpec(memory_space=pl.ANY)] * 4,
            out_specs=whole(out),
            scratch_shapes=[
                pltpu.VMEM((deep, count), jnp.bfloat16),
                pltpu.VMEM((4, deep, cols), jnp.bfloat16),
                pltpu.SemaphoreType.DMA((2 * peers,)),
                pltpu.SemaphoreType.DMA((4,)),
            ],
        ),
        compiler_params=pltpu.CompilerParams(vmem_limit_bytes=60 * 2**20),
        cost_estimate=pl.CostEstimate(
            flops=8 * deep * count * cols, bytes_accessed=8 * deep * cols, transcendentals=0
        ),
    )(half.reshape(1), hidden, extra, *weights)


def on_device(
    queries,
    keys,
    values,
    residual,
    out_weight,
    norm_gain,
    expert_ids,
    expert_gates,
    w_gate,
    w_up,
    w_down,
):
    n_zl, n_y = lax.axis_size("zl"), lax.axis_size("y")
    n_x, n_zh, n_co = lax.axis_size("x"), lax.axis_size("zh"), lax.axis_size("co")
    zl, y_pos, x_pos, co = (lax.axis_index(a) for a in ("zl", "y", "x", "co"))
    ctx_count, expert_count = n_zl * n_y, n_x * n_zh * n_co
    width = residual.shape[1]
    tok_dev, top_count = expert_ids.shape
    tok_block = queries.shape[0]
    heads = queries.shape[1] // HEAD_WIDTH
    swap_z = [(i, i ^ 1) for i in range(n_zl)]
    swap_y = [(i, i ^ 1) for i in range(n_y)]
    gate_own, up_own, down_own = w_gate[0].T, w_up[0].T, w_down[0]

    gate_z, up_z = lax.ppermute(gate_own, "zl", swap_z), lax.ppermute(up_own, "zl", swap_z)

    mine = jnp.where(co == 0, keys, values)
    mine = lax.dynamic_slice_in_dim(mine, x_pos * HEAD_WIDTH, HEAD_WIDTH, 1)
    gathered = spread(mine, CTX, ctx_count).reshape(ctx_count * tok_block, HEAD_WIDTH)

    key_all, value_all = spread(gathered, "co", n_co)

    order = np.arange(tok_block).reshape(n_x, n_zh, n_co, tok_dev).transpose(2, 0, 1, 3)
    split = queries.reshape(n_x, n_zh, n_co, tok_dev, heads, HEAD_WIDTH)
    query_rows = jnp.transpose(split, (4, 2, 0, 1, 3, 5)).reshape(heads * tok_block, HEAD_WIDTH)
    query_pos = (zl * n_y + y_pos) * tok_block + jnp.asarray(
        np.tile(order.reshape(-1), heads), jnp.int32
    )
    key_pos = jnp.arange(key_all.shape[0], dtype=jnp.int32)
    allowed = key_pos[None, :] <= query_pos[:, None]
    scores = rows_dot(query_rows, key_all) * (1.0 / HEAD_WIDTH**0.5)
    scores = jnp.where(allowed, scores, NEG_LARGE)
    weights = jnp.exp(scores - jnp.max(scores, axis=1, keepdims=True))
    total = jnp.sum(weights, axis=1, keepdims=True)
    numer = jnp.dot(weights.astype(jnp.bfloat16), value_all, preferred_element_type=jnp.float32)
    done = (numer / total).astype(jnp.bfloat16).reshape(heads, tok_block, HEAD_WIDTH)
    heads_out = jnp.transpose(done, (1, 0, 2)).reshape(tok_block, heads * HEAD_WIDTH)

    partial = jnp.dot(heads_out, out_weight, preferred_element_type=jnp.float32)
    partial = partial.astype(jnp.bfloat16).reshape(n_co, tok_block // n_co, width)
    partial = added(exchange(partial, "co")).astype(jnp.bfloat16)
    partial = added(exchange(partial.reshape(n_x, -1, width), "x"))
    partial, gate_z, up_z, down_own = lax.optimization_barrier((partial, gate_z, up_z, down_own))
    down_y = lax.ppermute(down_own, "y", swap_y)
    high = expert_gates.astype(jnp.bfloat16)
    low = (expert_gates - high.astype(jnp.float32)).astype(jnp.bfloat16)
    room = ((0, 0), (0, EXTRA // 4 - top_count))
    own = [(expert_ids + 1).astype(jnp.bfloat16), high, low, jnp.zeros_like(low)]
    own = jnp.concatenate([residual] + [jnp.pad(part, room) for part in own], axis=1)
    mine = jnp.arange(n_zh, dtype=jnp.int32)[:, None, None] == lax.axis_index("zh")
    own = jnp.where(mine, own[None], 0).reshape(n_zh * tok_dev, width + EXTRA)
    partial = jnp.pad(partial, ((0, 0), (0, EXTRA))) + own.astype(jnp.float32)
    parts = spread(partial.astype(jnp.bfloat16), "zh", n_zh)

    places = n_y * tok_dev
    place = jnp.stack([lax.axis_index("zh"), y_pos])
    mixed, outgoing = dispatch_rows(place, parts, norm_gain, n_x * n_co)
    arrived = exchange(outgoing, ("x", "co")).reshape(-1, width + EXTRA)

    arrived, down_own, down_y = lax.optimization_barrier((arrived, down_own, down_y))
    after = [(i, (i + 1) % n_y) for i in range(n_y)]
    before = [(b, a) for a, b in after]
    weights = (gate_own, gate_z, up_own, up_z)

    def rightward(value):
        return lax.ppermute(value, "y", after)

    def leftward(value):
        return lax.ppermute(value, "y", before)

    left_one, right_one = rightward(arrived), leftward(arrived)
    left_two, right_two = rightward(left_one), leftward(right_one)
    down_z = lax.ppermute(down_own, "zl", swap_z)
    right_two, down_z, down_y = lax.optimization_barrier((right_two, down_z, down_y))
    left_three, right_three = rightward(left_two), leftward(right_two)
    last = rightward(left_three)
    down_zy = lax.ppermute(down_y, "zl", swap_z)
    near = (arrived, left_one, right_one, left_two, right_two)
    far = (left_three, right_three)
    first = first_hidden(zl, near, weights, width)
    second = first_hidden(zl, far, weights, width)
    last, first, second = lax.optimization_barrier((last, first, second))

    hidden, extra = last_hidden(
        jnp.stack([zl, y_pos]),
        (last,),
        weights,
        (first, second),
        near + far + (last,),
        width,
        n_y,
    )
    hidden, down_zy = lax.optimization_barrier((hidden, down_zy))
    hidden = exchange(hidden, "y")

    result = down_slots(y_pos % 2, hidden, extra, (down_own, down_y, down_z, down_zy))
    cols = result.shape[1] - EXTRA
    result = exchange(result.reshape(expert_count, -1, cols + EXTRA), EXP)
    result = result.reshape(-1, cols + EXTRA)
    tokens = lax.dot_general(
        result[:, cols : cols + 2 * places],
        result[:, :cols],
        (((0,), (0,)), ((), ())),
        preferred_element_type=jnp.float32,
    )
    tokens = (tokens[:places] + tokens[places:]).astype(jnp.bfloat16)
    tokens = exchange(tokens.reshape(n_y, tok_dev, cols), "y")
    tokens = added(tokens.reshape(n_y // 2, 2, tok_dev, cols).transpose(1, 0, 2, 3))
    tokens = tokens.astype(jnp.bfloat16).reshape(n_y // 2, tok_dev, n_zl, 2, cols // 4)
    tokens = jnp.where(zl == 0, tokens, tokens[:, :, ::-1])
    tokens = jnp.where(y_pos < n_y // 2, tokens, tokens[:, :, :, ::-1])
    tokens = tokens.transpose(1, 2, 0, 3, 4)
    return (mixed, tokens.reshape(tok_dev, width))


def solution(mesh):
    fine = Mesh(mesh.devices.reshape(2, 8, 4, 4, 2), CTX + EXP)
    return jax.shard_map(
        on_device,
        mesh=fine,
        in_specs=(
            P(CTX, EXP),
            P(CTX, None),
            P(CTX, None),
            P(CTX + EXP, None),
            P(EXP, None),
            P(),
            P(CTX + EXP, None),
            P(CTX + EXP, None),
            P(EXP, None, CTX),
            P(EXP, None, CTX),
            P(EXP, None, CTX),
        ),
        out_specs=(P(CTX + EXP, None), P(CTX + EXP, None)),
        check_vma=False,
    )
```

```python
import jax
import jax.numpy as jnp
import numpy as np
from jax import lax
from jax.experimental import pallas as pl
from jax.experimental.pallas import tpu as pltpu
from jax.sharding import Mesh, PartitionSpec as P

HEAD_WIDTH = 128
EXTRA = 128

CTX = ("zl", "y")
EXP = ("x", "zh", "co")
EPS_NORM = 1e-06
NEG_LARGE = -1e30


def exchange(pieces, axis):
    return lax.all_to_all(pieces, axis, 0, 0, tiled=True)


def spread(value, axis, count):
    return exchange(jnp.broadcast_to(value[None], (count,) + value.shape), axis)


def added(pieces):
    return jnp.sum(pieces.astype(jnp.float32), axis=0)


def rows_dot(left, right):
    return lax.dot_general(
        left, right, (((1,), (1,)), ((), ())), preferred_element_type=jnp.float32
    )


def whole(shape):
    return pl.BlockSpec(shape, lambda *_: (0,) * len(shape))


def dispatch_kernel(place_ref, parts_ref, gain_ref, mixed_ref, out_ref):
    parts, tokens, wide = parts_ref.shape
    peers, rows = out_ref.shape[0], out_ref.shape[1]
    width = wide - EXTRA
    tok_dev = tokens // parts
    top = EXTRA // 4
    whole_sum = parts_ref[0].astype(jnp.float32)
    for part in range(1, parts):
        whole_sum += parts_ref[part].astype(jnp.float32)
    mixed = whole_sum[:, :width].astype(jnp.bfloat16)
    for part in range(parts):

        @pl.when(place_ref[0] == part)
        def _():
            mixed_ref[...] = mixed[part * tok_dev : (part + 1) * tok_dev, :]

    stream = mixed.astype(jnp.float32)
    mean_sq = jnp.mean(stream * stream, axis=1, keepdims=True)
    normed = (stream * lax.rsqrt(mean_sq + EPS_NORM) * gain_ref[...]).astype(jnp.bfloat16)

    extra = whole_sum[:, width:]
    named = extra[:, :top]
    high, low = extra[:, top : 2 * top], extra[:, 2 * top : 3 * top]
    place = place_ref[0]
    hits, highs, lows = [], [], []
    for peer in range(peers):
        expert = peer // 2 * (2 * parts) + 2 * place + peer % 2
        match = named == (expert + 1).astype(jnp.float32)
        hits.append(jnp.sum(match.astype(jnp.float32), axis=1, keepdims=True))
        highs.append(jnp.sum(jnp.where(match, high, 0.0), axis=1, keepdims=True))
        lows.append(jnp.sum(jnp.where(match, low, 0.0), axis=1, keepdims=True))
    token = lax.broadcasted_iota(jnp.int32, (tokens, tokens), 0)
    other = lax.broadcasted_iota(jnp.int32, (tokens, tokens), 1)
    earlier = (token // tok_dev == other // tok_dev) & (other < token)
    row = lax.broadcasted_iota(jnp.int32, (rows, tokens), 0)
    column = lax.broadcasted_iota(jnp.int32, (rows, tokens), 1)
    from_block = row // 2 == column // tok_dev
    lane = lax.broadcasted_iota(jnp.int32, (tokens, EXTRA), 1)
    local = lax.broadcasted_iota(jnp.int32, (tokens, EXTRA), 0) % tok_dev
    goal = place_ref[1] * tok_dev + local
    for peer in range(peers):
        hit = hits[peer]
        hit_row = jnp.sum(jnp.where(token == other, hit, 0.0), axis=0, keepdims=True)
        rank = jnp.sum(jnp.where(earlier, hit_row, 0.0), axis=1, keepdims=True)
        rank_row = jnp.sum(jnp.where(token == other, rank, 0.0), axis=0, keepdims=True)
        take = from_block & (hit_row > 0.5) & (rank_row == (row % 2).astype(jnp.float32))
        take = jnp.where(take, 1.0, 0.0).astype(jnp.bfloat16)
        sent = jnp.dot(take, normed, preferred_element_type=jnp.float32)
        out_ref[peer, :, :width] = sent.astype(jnp.bfloat16)
        tag = jnp.where(lane == goal, highs[peer], 0.0)
        tag += jnp.where(lane == goal + 32, lows[peer], 0.0)
        tag = jnp.dot(take, tag.astype(jnp.bfloat16), preferred_element_type=jnp.float32)
        out_ref[peer, :, width:] = tag.astype(jnp.bfloat16)


def dispatch_rows(place, parts, gain, peers):
    count, tokens, wide = parts.shape
    width = wide - EXTRA
    out = (peers, 2 * count, wide)
    return pl.pallas_call(
        dispatch_kernel,
        out_shape=(
            jax.ShapeDtypeStruct((tokens // count, width), jnp.bfloat16),
            jax.ShapeDtypeStruct(out, jnp.bfloat16),
        ),
        grid_spec=pltpu.PrefetchScalarGridSpec(
            num_scalar_prefetch=1,
            grid=(1,),
            in_specs=[whole(parts.shape), whole((1, width))],
            out_specs=(whole((tokens // count, width)), whole(out)),
        ),
        compiler_params=pltpu.CompilerParams(vmem_limit_bytes=24 * 2**20),
        cost_estimate=pl.CostEstimate(
            flops=2 * peers * 2 * count * tokens * wide,
            bytes_accessed=4 * peers * count * wide,
            transcendentals=0,
        ),
    )(place, parts, gain.reshape(1, width))


def weight_rows(zl_ref, refs, weight):
    units = refs[0].shape[0]
    for place in range(2):
        own, other = refs[2 * place], refs[2 * place + 1]
        low = pl.ds(2 * place * units, units)
        high = pl.ds((2 * place + 1) * units, units)

        @pl.when(zl_ref[0] == 0)
        def _():
            weight[low, :] = own[...]
            weight[high, :] = other[...]

        @pl.when(zl_ref[0] != 0)
        def _():
            weight[low, :] = other[...]
            weight[high, :] = own[...]


def gated(total, units):
    gate, upper = total[: 2 * units, :], total[2 * units :, :]
    return (gate / (1.0 + jnp.exp(-gate)) * upper).astype(jnp.bfloat16)


def accumulate(weight, rows, block_refs, total):
    start = 0
    for block in block_refs:
        rows[pl.ds(start, block.shape[0]), :] = block[...]
        start += block.shape[0]

    @pl.when(pl.program_id(0) == 0)
    def _():
        total[...] = jnp.zeros_like(total)

    total[...] += rows_dot(weight[...], rows[...])


def first_kernel(zl_ref, *refs):
    blocks, weights, (out_ref, weight, rows, total) = refs[:-8], refs[-8:-4], refs[-4:]
    weight_rows(zl_ref, weights, weight)
    accumulate(weight, rows, blocks, total)

    @pl.when(pl.program_id(0) == pl.num_programs(0) - 1)
    def _():
        out_ref[...] = gated(total, weights[0].shape[0])


def last_kernel(count, parts, place_ref, *refs):
    blocks, weights, refs = refs[:count], refs[count : count + 4], refs[count + 4 :]
    done, extras = refs[:parts], refs[parts:-6]
    out_ref, extra_ref, weight, rows, total, tags = refs[-6:]
    weight_rows(place_ref, weights, weight)
    accumulate(weight, rows, blocks, total)

    @pl.when(pl.program_id(0) == pl.num_programs(0) - 1)
    def _():
        held = [part[...] for part in done] + [gated(total, weights[0].shape[0])]
        hidden = jnp.concatenate(held, axis=1)
        slots = hidden.shape[1]
        peers = out_ref.shape[0]
        each = slots // peers
        start = 0
        for extra in extras:
            tags[pl.ds(start, extra.shape[0]), :] = extra[...]
            start += extra.shape[0]
        held = lax.broadcasted_iota(jnp.int32, (slots, 1), 0)
        turn = held >> (each.bit_length() - 1)
        away = jnp.where(turn & 1 == 1, peers - ((turn + 1) >> 1), turn >> 1)
        goal = ((place_ref[1] + away) & (peers - 1)) * each + (held & (each - 1))
        column = lax.broadcasted_iota(jnp.int32, (slots, slots), 1)
        move = jnp.where(goal == column, 1.0, 0.0).astype(jnp.bfloat16)
        hidden = jnp.dot(hidden, move, preferred_element_type=jnp.float32).astype(jnp.bfloat16)
        half = slots // 2
        for peer in range(peers):
            out_ref[peer] = hidden[:, (peer % 2) * half : (peer % 2 + 1) * half]
        extra_ref[...] = lax.dot_general(
            move, tags[...], (((0,), (0,)), ((), ())), preferred_element_type=jnp.float32
        ).astype(jnp.bfloat16)


def row_specs(blocks, weights, step):
    return [pl.BlockSpec((b.shape[0], step), lambda k, *_: (0, k)) for b in blocks] + [
        pl.BlockSpec((w.shape[0], step), lambda k, *_: (0, k)) for w in weights
    ]


def held_scratch(units, count, step):
    return [
        pltpu.VMEM((4 * units, step), jnp.bfloat16),
        pltpu.VMEM((count, step), jnp.bfloat16),
        pltpu.VMEM((4 * units, count), jnp.float32),
    ]


def cost(units, count, width):
    return pl.CostEstimate(
        flops=8 * units * count * width,
        bytes_accessed=2 * (count + 4 * units) * width,
        transcendentals=0,
    )


def first_hidden(zl, blocks, weights, width):
    units, step = weights[0].shape[0], 1024
    count = sum(b.shape[0] for b in blocks)
    return pl.pallas_call(
        first_kernel,
        out_shape=jax.ShapeDtypeStruct((2 * units, count), jnp.bfloat16),
        grid_spec=pltpu.PrefetchScalarGridSpec(
            num_scalar_prefetch=1,
            grid=(width // step,),
            in_specs=row_specs(blocks, weights, step),
            out_specs=whole((2 * units, count)),
            scratch_shapes=held_scratch(units, count, step),
        ),
        compiler_params=pltpu.CompilerParams(vmem_limit_bytes=24 * 2**20),
        cost_estimate=cost(units, count, width),
    )(zl.reshape(1), *blocks, *weights)


def last_hidden(place, blocks, weights, first, every, width, peers):
    units, step = weights[0].shape[0], 1024
    count = sum(b.shape[0] for b in blocks)
    slots = sum(b.shape[0] for b in every)
    pieces = (peers, 2 * units, slots // 2)
    return pl.pallas_call(
        lambda *refs: last_kernel(len(blocks), len(first), *refs),
        out_shape=(
            jax.ShapeDtypeStruct(pieces, jnp.bfloat16),
            jax.ShapeDtypeStruct((slots, EXTRA), jnp.bfloat16),
        ),
        grid_spec=pltpu.PrefetchScalarGridSpec(
            num_scalar_prefetch=1,
            grid=(width // step,),
            in_specs=row_specs(blocks, weights, step)
            + [whole(part.shape) for part in first]
            + [
                pl.BlockSpec((b.shape[0], EXTRA), lambda k, *_: (0, width // EXTRA))
                for b in every
            ],
            out_specs=(whole(pieces), whole((slots, EXTRA))),
            scratch_shapes=held_scratch(units, count, step)
            + [pltpu.VMEM((slots, EXTRA), jnp.bfloat16)],
        ),
        compiler_params=pltpu.CompilerParams(vmem_limit_bytes=24 * 2**20),
        cost_estimate=cost(units, count, width),
    )(place, *blocks, *weights, *first, *every)


def down_kernel(half_ref, hidden_ref, extra_ref, *refs):
    weights, (out_ref, stacked, held, arrived) = refs[:4], refs[4:]
    peers, units, count = hidden_ref.shape
    half = units // 2
    copies = [
        pltpu.make_async_copy(weight, held.at[i], arrived.at[i]) for i, weight in enumerate(weights)
    ]
    for copy in copies:
        copy.start()
    for peer in range(peers):
        for z in range(2):
            rows = pl.ds((z * peers + peer) * half, half)
            stacked[rows, :] = hidden_ref[peer, z * half : (z + 1) * half, :]
    blocks = peers // 2
    each = count // blocks
    to = lax.broadcasted_iota(jnp.int32, (count, 1), 0)
    owner = to >> blocks.bit_length()
    source = (owner >> 3) * 16 + (owner & 1) * 8 + ((owner & 7) >> 1) * 2 + (to & 1)
    source = ((to & (2 * blocks - 1)) >> 1) * each + source
    column = lax.broadcasted_iota(jnp.int32, (count, count), 1)
    move = jnp.where(source == column, 1.0, 0.0).astype(jnp.bfloat16)
    rows = rows_dot(move, stacked[...]).astype(jnp.bfloat16)
    cols = held.shape[2]
    extra = jnp.where(half_ref[0] == 0, extra_ref[:count, :], extra_ref[count:, :])
    extra = jnp.dot(move, extra, preferred_element_type=jnp.float32)
    out_ref[:, 4 * cols :] = extra.astype(jnp.bfloat16)
    for i, copy in enumerate(copies):
        copy.wait()
        result = jnp.dot(rows, held[i], preferred_element_type=jnp.float32)
        out_ref[:, i * cols : (i + 1) * cols] = result.astype(jnp.bfloat16)


def down_slots(half, hidden, extra, weights):
    peers, units, count = hidden.shape
    deep, cols = weights[0].shape
    out = (count, 4 * cols + EXTRA)
    return pl.pallas_call(
        down_kernel,
        out_shape=jax.ShapeDtypeStruct(out, jnp.bfloat16),
        grid_spec=pltpu.PrefetchScalarGridSpec(
            num_scalar_prefetch=1,
            grid=(1,),
            in_specs=[whole(hidden.shape), whole(extra.shape)]
            + [pl.BlockSpec(memory_space=pl.ANY)] * 4,
            out_specs=whole(out),
            scratch_shapes=[
                pltpu.VMEM((deep, count), jnp.bfloat16),
                pltpu.VMEM((4, deep, cols), jnp.bfloat16),
                pltpu.SemaphoreType.DMA((4,)),
            ],
        ),
        compiler_params=pltpu.CompilerParams(vmem_limit_bytes=24 * 2**20),
        cost_estimate=pl.CostEstimate(
            flops=8 * deep * count * cols, bytes_accessed=8 * deep * cols, transcendentals=0
        ),
    )(half.reshape(1), hidden, extra, *weights)


def on_device(
    queries,
    keys,
    values,
    residual,
    out_weight,
    norm_gain,
    expert_ids,
    expert_gates,
    w_gate,
    w_up,
    w_down,
):
    n_zl, n_y = lax.axis_size("zl"), lax.axis_size("y")
    n_x, n_zh, n_co = lax.axis_size("x"), lax.axis_size("zh"), lax.axis_size("co")
    zl, y_pos, x_pos, co = (lax.axis_index(a) for a in ("zl", "y", "x", "co"))
    ctx_count, expert_count = n_zl * n_y, n_x * n_zh * n_co
    width = residual.shape[1]
    tok_dev, top_count = expert_ids.shape
    tok_block = queries.shape[0]
    heads = queries.shape[1] // HEAD_WIDTH
    swap_z = [(i, i ^ 1) for i in range(n_zl)]
    swap_y = [(i, i ^ 1) for i in range(n_y)]
    gate_own, up_own, down_own = w_gate[0].T, w_up[0].T, w_down[0]

    gate_z, up_z = lax.ppermute(gate_own, "zl", swap_z), lax.ppermute(up_own, "zl", swap_z)

    mine = jnp.where(co == 0, keys, values)
    mine = lax.dynamic_slice_in_dim(mine, x_pos * HEAD_WIDTH, HEAD_WIDTH, 1)
    gathered = spread(mine, CTX, ctx_count).reshape(ctx_count * tok_block, HEAD_WIDTH)

    key_all, value_all = spread(gathered, "co", n_co)

    order = np.arange(tok_block).reshape(n_x, n_zh, n_co, tok_dev).transpose(2, 0, 1, 3)
    split = queries.reshape(n_x, n_zh, n_co, tok_dev, heads, HEAD_WIDTH)
    query_rows = jnp.transpose(split, (4, 2, 0, 1, 3, 5)).reshape(heads * tok_block, HEAD_WIDTH)
    query_pos = (zl * n_y + y_pos) * tok_block + jnp.asarray(
        np.tile(order.reshape(-1), heads), jnp.int32
    )
    key_pos = jnp.arange(key_all.shape[0], dtype=jnp.int32)
    allowed = key_pos[None, :] <= query_pos[:, None]
    scores = rows_dot(query_rows, key_all) * (1.0 / HEAD_WIDTH**0.5)
    scores = jnp.where(allowed, scores, NEG_LARGE)
    weights = jnp.exp(scores - jnp.max(scores, axis=1, keepdims=True))
    total = jnp.sum(weights, axis=1, keepdims=True)
    numer = jnp.dot(weights.astype(jnp.bfloat16), value_all, preferred_element_type=jnp.float32)
    done = (numer / total).astype(jnp.bfloat16).reshape(heads, tok_block, HEAD_WIDTH)
    heads_out = jnp.transpose(done, (1, 0, 2)).reshape(tok_block, heads * HEAD_WIDTH)

    partial = jnp.dot(heads_out, out_weight, preferred_element_type=jnp.float32)
    partial = partial.astype(jnp.bfloat16).reshape(n_co, tok_block // n_co, width)
    partial = added(exchange(partial, "co")).astype(jnp.bfloat16)
    partial = added(exchange(partial.reshape(n_x, -1, width), "x"))
    partial, gate_z, up_z, down_own = lax.optimization_barrier((partial, gate_z, up_z, down_own))
    down_y = lax.ppermute(down_own, "y", swap_y)
    high = expert_gates.astype(jnp.bfloat16)
    low = (expert_gates - high.astype(jnp.float32)).astype(jnp.bfloat16)
    room = ((0, 0), (0, EXTRA // 4 - top_count))
    own = [(expert_ids + 1).astype(jnp.bfloat16), high, low, jnp.zeros_like(low)]
    own = jnp.concatenate([residual] + [jnp.pad(part, room) for part in own], axis=1)
    mine = jnp.arange(n_zh, dtype=jnp.int32)[:, None, None] == lax.axis_index("zh")
    own = jnp.where(mine, own[None], 0).reshape(n_zh * tok_dev, width + EXTRA)
    partial = jnp.pad(partial, ((0, 0), (0, EXTRA))) + own.astype(jnp.float32)
    parts = spread(partial.astype(jnp.bfloat16), "zh", n_zh)

    places = n_y * tok_dev
    place = jnp.stack([lax.axis_index("zh"), y_pos])
    mixed, outgoing = dispatch_rows(place, parts, norm_gain, n_x * n_co)
    arrived = exchange(outgoing, ("x", "co")).reshape(-1, width + EXTRA)

    arrived, down_own, down_y = lax.optimization_barrier((arrived, down_own, down_y))
    after = [(i, (i + 1) % n_y) for i in range(n_y)]
    before = [(b, a) for a, b in after]
    weights = (gate_own, gate_z, up_own, up_z)

    def rightward(value):
        return lax.ppermute(value, "y", after)

    def leftward(value):
        return lax.ppermute(value, "y", before)

    left_one, right_one = rightward(arrived), leftward(arrived)
    left_two, right_two = rightward(left_one), leftward(right_one)
    down_z = lax.ppermute(down_own, "zl", swap_z)
    right_two, down_z, down_y = lax.optimization_barrier((right_two, down_z, down_y))
    left_three, right_three = rightward(left_two), leftward(right_two)
    last = rightward(left_three)
    down_zy = lax.ppermute(down_y, "zl", swap_z)
    near = (arrived, left_one, right_one, left_two, right_two)
    far = (left_three, right_three)
    first = first_hidden(zl, near, weights, width)
    second = first_hidden(zl, far, weights, width)
    last, first, second = lax.optimization_barrier((last, first, second))

    hidden, extra = last_hidden(
        jnp.stack([zl, y_pos]),
        (last,),
        weights,
        (first, second),
        near + far + (last,),
        width,
        n_y,
    )
    hidden, down_zy = lax.optimization_barrier((hidden, down_zy))
    hidden = exchange(hidden, "y")

    result = down_slots(y_pos % 2, hidden, extra, (down_own, down_y, down_z, down_zy))
    cols = result.shape[1] - EXTRA
    result = exchange(result.reshape(expert_count, -1, cols + EXTRA), EXP)
    result = result.reshape(-1, cols + EXTRA)
    tokens = lax.dot_general(
        result[:, cols : cols + 2 * places],
        result[:, :cols],
        (((0,), (0,)), ((), ())),
        preferred_element_type=jnp.float32,
    )
    tokens = (tokens[:places] + tokens[places:]).astype(jnp.bfloat16)
    tokens = exchange(tokens.reshape(n_y, tok_dev, cols), "y")
    tokens = added(tokens.reshape(n_y // 2, 2, tok_dev, cols).transpose(1, 0, 2, 3))
    tokens = tokens.astype(jnp.bfloat16).reshape(n_y // 2, tok_dev, n_zl, 2, cols // 4)
    tokens = jnp.where(zl == 0, tokens, tokens[:, :, ::-1])
    tokens = jnp.where(y_pos < n_y // 2, tokens, tokens[:, :, :, ::-1])
    tokens = tokens.transpose(1, 2, 0, 3, 4)
    return (mixed, tokens.reshape(tok_dev, width))


def solution(mesh):
    fine = Mesh(mesh.devices.reshape(2, 8, 4, 4, 2), CTX + EXP)
    return jax.shard_map(
        on_device,
        mesh=fine,
        in_specs=(
            P(CTX, EXP),
            P(CTX, None),
            P(CTX, None),
            P(CTX + EXP, None),
            P(EXP, None),
            P(),
            P(CTX + EXP, None),
            P(CTX + EXP, None),
            P(EXP, None, CTX),
            P(EXP, None, CTX),
            P(EXP, None, CTX),
        ),
        out_specs=(P(CTX + EXP, None), P(CTX + EXP, None)),
        check_vma=False,
    )
```

```python
import jax
import jax.numpy as jnp
import numpy as np
from jax import lax
from jax.experimental import pallas as pl
from jax.experimental.pallas import tpu as pltpu
from jax.sharding import Mesh, PartitionSpec as P

HEAD_WIDTH = 128
EXTRA = 128

CTX = ("zl", "y")
EXP = ("x", "zh", "co")
EPS_NORM = 1e-06
NEG_LARGE = -1e30


def exchange(pieces, axis):
    return lax.all_to_all(pieces, axis, 0, 0, tiled=True)


def spread(value, axis, count):
    return exchange(jnp.broadcast_to(value[None], (count,) + value.shape), axis)


def added(pieces):
    return jnp.sum(pieces.astype(jnp.float32), axis=0)


def rows_dot(left, right):
    return lax.dot_general(
        left, right, (((1,), (1,)), ((), ())), preferred_element_type=jnp.float32
    )


def whole(shape):
    return pl.BlockSpec(shape, lambda *_: (0,) * len(shape))


def dispatch_kernel(place_ref, parts_ref, gain_ref, mixed_ref, out_ref):
    parts, tokens, wide = parts_ref.shape
    peers, rows = out_ref.shape[0], out_ref.shape[1]
    width = wide - EXTRA
    tok_dev = tokens // parts
    top = EXTRA // 4
    whole_sum = parts_ref[0].astype(jnp.float32)
    for part in range(1, parts):
        whole_sum += parts_ref[part].astype(jnp.float32)
    mixed = whole_sum[:, :width].astype(jnp.bfloat16)
    for part in range(parts):

        @pl.when(place_ref[0] == part)
        def _():
            mixed_ref[...] = mixed[part * tok_dev : (part + 1) * tok_dev, :]

    stream = mixed.astype(jnp.float32)
    mean_sq = jnp.mean(stream * stream, axis=1, keepdims=True)
    normed = (stream * lax.rsqrt(mean_sq + EPS_NORM) * gain_ref[...]).astype(jnp.bfloat16)

    extra = whole_sum[:, width:]
    named = extra[:, :top]
    high, low = extra[:, top : 2 * top], extra[:, 2 * top : 3 * top]
    place = place_ref[0]
    hits, highs, lows = [], [], []
    for peer in range(peers):
        expert = peer // 2 * (2 * parts) + 2 * place + peer % 2
        match = named == (expert + 1).astype(jnp.float32)
        hits.append(jnp.sum(match.astype(jnp.float32), axis=1, keepdims=True))
        highs.append(jnp.sum(jnp.where(match, high, 0.0), axis=1, keepdims=True))
        lows.append(jnp.sum(jnp.where(match, low, 0.0), axis=1, keepdims=True))
    token = lax.broadcasted_iota(jnp.int32, (tokens, tokens), 0)
    other = lax.broadcasted_iota(jnp.int32, (tokens, tokens), 1)
    earlier = (token // tok_dev == other // tok_dev) & (other < token)
    row = lax.broadcasted_iota(jnp.int32, (rows, tokens), 0)
    column = lax.broadcasted_iota(jnp.int32, (rows, tokens), 1)
    from_block = row // 2 == column // tok_dev
    lane = lax.broadcasted_iota(jnp.int32, (tokens, EXTRA), 1)
    local = lax.broadcasted_iota(jnp.int32, (tokens, EXTRA), 0) % tok_dev
    goal = place_ref[1] * tok_dev + local
    for peer in range(peers):
        hit = hits[peer]
        hit_row = jnp.sum(jnp.where(token == other, hit, 0.0), axis=0, keepdims=True)
        rank = jnp.sum(jnp.where(earlier, hit_row, 0.0), axis=1, keepdims=True)
        rank_row = jnp.sum(jnp.where(token == other, rank, 0.0), axis=0, keepdims=True)
        take = from_block & (hit_row > 0.5) & (rank_row == (row % 2).astype(jnp.float32))
        take = jnp.where(take, 1.0, 0.0).astype(jnp.bfloat16)
        sent = jnp.dot(take, normed, preferred_element_type=jnp.float32)
        out_ref[peer, :, :width] = sent.astype(jnp.bfloat16)
        tag = jnp.where(lane == goal, highs[peer], 0.0)
        tag += jnp.where(lane == goal + 32, lows[peer], 0.0)
        tag = jnp.dot(take, tag.astype(jnp.bfloat16), preferred_element_type=jnp.float32)
        out_ref[peer, :, width:] = tag.astype(jnp.bfloat16)


def dispatch_rows(place, parts, gain, peers):
    count, tokens, wide = parts.shape
    width = wide - EXTRA
    out = (peers, 2 * count, wide)
    return pl.pallas_call(
        dispatch_kernel,
        out_shape=(
            jax.ShapeDtypeStruct((tokens // count, width), jnp.bfloat16),
            jax.ShapeDtypeStruct(out, jnp.bfloat16),
        ),
        grid_spec=pltpu.PrefetchScalarGridSpec(
            num_scalar_prefetch=1,
            grid=(1,),
            in_specs=[whole(parts.shape), whole((1, width))],
            out_specs=(whole((tokens // count, width)), whole(out)),
        ),
        compiler_params=pltpu.CompilerParams(vmem_limit_bytes=24 * 2**20),
        cost_estimate=pl.CostEstimate(
            flops=2 * peers * 2 * count * tokens * wide,
            bytes_accessed=4 * peers * count * wide,
            transcendentals=0,
        ),
    )(place, parts, gain.reshape(1, width))


def weight_rows(zl_ref, refs, weight):
    units = refs[0].shape[0]
    for place in range(2):
        own, other = refs[2 * place], refs[2 * place + 1]
        low = pl.ds(2 * place * units, units)
        high = pl.ds((2 * place + 1) * units, units)

        @pl.when(zl_ref[0] == 0)
        def _():
            weight[low, :] = own[...]
            weight[high, :] = other[...]

        @pl.when(zl_ref[0] != 0)
        def _():
            weight[low, :] = other[...]
            weight[high, :] = own[...]


def gated(total, units):
    gate, upper = total[: 2 * units, :], total[2 * units :, :]
    return (gate / (1.0 + jnp.exp(-gate)) * upper).astype(jnp.bfloat16)


def accumulate(weight, rows, block_refs, total):
    start = 0
    for block in block_refs:
        rows[pl.ds(start, block.shape[0]), :] = block[...]
        start += block.shape[0]

    @pl.when(pl.program_id(0) == 0)
    def _():
        total[...] = jnp.zeros_like(total)

    total[...] += rows_dot(weight[...], rows[...])


def first_kernel(zl_ref, *refs):
    blocks, weights, (out_ref, weight, rows, total) = refs[:-8], refs[-8:-4], refs[-4:]
    weight_rows(zl_ref, weights, weight)
    accumulate(weight, rows, blocks, total)

    @pl.when(pl.program_id(0) == pl.num_programs(0) - 1)
    def _():
        out_ref[...] = gated(total, weights[0].shape[0])


def last_kernel(count, parts, place_ref, *refs):
    blocks, weights, refs = refs[:count], refs[count : count + 4], refs[count + 4 :]
    done, extras = refs[:parts], refs[parts:-6]
    out_ref, extra_ref, weight, rows, total, tags = refs[-6:]
    weight_rows(place_ref, weights, weight)
    accumulate(weight, rows, blocks, total)

    @pl.when(pl.program_id(0) == pl.num_programs(0) - 1)
    def _():
        held = [part[...] for part in done] + [gated(total, weights[0].shape[0])]
        hidden = jnp.concatenate(held, axis=1)
        slots = hidden.shape[1]
        peers = out_ref.shape[0]
        each = slots // peers
        start = 0
        for extra in extras:
            tags[pl.ds(start, extra.shape[0]), :] = extra[...]
            start += extra.shape[0]
        held = lax.broadcasted_iota(jnp.int32, (slots, 1), 0)
        turn = held >> (each.bit_length() - 1)
        away = jnp.where(turn & 1 == 1, peers - ((turn + 1) >> 1), turn >> 1)
        goal = ((place_ref[1] + away) & (peers - 1)) * each + (held & (each - 1))
        column = lax.broadcasted_iota(jnp.int32, (slots, slots), 1)
        move = jnp.where(goal == column, 1.0, 0.0).astype(jnp.bfloat16)
        hidden = jnp.dot(hidden, move, preferred_element_type=jnp.float32).astype(jnp.bfloat16)
        half = slots // 2
        for peer in range(peers):
            out_ref[peer] = hidden[:, (peer % 2) * half : (peer % 2 + 1) * half]
        extra_ref[...] = lax.dot_general(
            move, tags[...], (((0,), (0,)), ((), ())), preferred_element_type=jnp.float32
        ).astype(jnp.bfloat16)


def row_specs(blocks, weights, step):
    return [pl.BlockSpec((b.shape[0], step), lambda k, *_: (0, k)) for b in blocks] + [
        pl.BlockSpec((w.shape[0], step), lambda k, *_: (0, k)) for w in weights
    ]


def held_scratch(units, count, step):
    return [
        pltpu.VMEM((4 * units, step), jnp.bfloat16),
        pltpu.VMEM((count, step), jnp.bfloat16),
        pltpu.VMEM((4 * units, count), jnp.float32),
    ]


def cost(units, count, width):
    return pl.CostEstimate(
        flops=8 * units * count * width,
        bytes_accessed=2 * (count + 4 * units) * width,
        transcendentals=0,
    )


def first_hidden(zl, blocks, weights, width):
    units, step = weights[0].shape[0], 1024
    count = sum(b.shape[0] for b in blocks)
    return pl.pallas_call(
        first_kernel,
        out_shape=jax.ShapeDtypeStruct((2 * units, count), jnp.bfloat16),
        grid_spec=pltpu.PrefetchScalarGridSpec(
            num_scalar_prefetch=1,
            grid=(width // step,),
            in_specs=row_specs(blocks, weights, step),
            out_specs=whole((2 * units, count)),
            scratch_shapes=held_scratch(units, count, step),
        ),
        compiler_params=pltpu.CompilerParams(vmem_limit_bytes=24 * 2**20),
        cost_estimate=cost(units, count, width),
    )(zl.reshape(1), *blocks, *weights)


def last_hidden(place, blocks, weights, first, every, width, peers):
    units, step = weights[0].shape[0], 1024
    count = sum(b.shape[0] for b in blocks)
    slots = sum(b.shape[0] for b in every)
    pieces = (peers, 2 * units, slots // 2)
    return pl.pallas_call(
        lambda *refs: last_kernel(len(blocks), len(first), *refs),
        out_shape=(
            jax.ShapeDtypeStruct(pieces, jnp.bfloat16),
            jax.ShapeDtypeStruct((slots, EXTRA), jnp.bfloat16),
        ),
        grid_spec=pltpu.PrefetchScalarGridSpec(
            num_scalar_prefetch=1,
            grid=(width // step,),
            in_specs=row_specs(blocks, weights, step)
            + [whole(part.shape) for part in first]
            + [
                pl.BlockSpec((b.shape[0], EXTRA), lambda k, *_: (0, width // EXTRA))
                for b in every
            ],
            out_specs=(whole(pieces), whole((slots, EXTRA))),
            scratch_shapes=held_scratch(units, count, step)
            + [pltpu.VMEM((slots, EXTRA), jnp.bfloat16)],
        ),
        compiler_params=pltpu.CompilerParams(vmem_limit_bytes=24 * 2**20),
        cost_estimate=cost(units, count, width),
    )(place, *blocks, *weights, *first, *every)


def down_kernel(half_ref, hidden_ref, extra_ref, *refs):
    weights, (out_ref, stacked, held, arrived) = refs[:4], refs[4:]
    peers, units, count = hidden_ref.shape
    half = units // 2
    copies = [
        pltpu.make_async_copy(weight, held.at[i], arrived.at[i]) for i, weight in enumerate(weights)
    ]
    for copy in copies:
        copy.start()
    for peer in range(peers):
        for z in range(2):
            rows = pl.ds((z * peers + peer) * half, half)
            stacked[rows, :] = hidden_ref[peer, z * half : (z + 1) * half, :]
    blocks = peers // 2
    each = count // blocks
    to = lax.broadcasted_iota(jnp.int32, (count, 1), 0)
    owner = to >> blocks.bit_length()
    source = (owner >> 3) * 16 + (owner & 1) * 8 + ((owner & 7) >> 1) * 2 + (to & 1)
    source = ((to & (2 * blocks - 1)) >> 1) * each + source
    column = lax.broadcasted_iota(jnp.int32, (count, count), 1)
    move = jnp.where(source == column, 1.0, 0.0).astype(jnp.bfloat16)
    rows = rows_dot(move, stacked[...]).astype(jnp.bfloat16)
    cols = held.shape[2]
    extra = jnp.where(half_ref[0] == 0, extra_ref[:count, :], extra_ref[count:, :])
    extra = jnp.dot(move, extra, preferred_element_type=jnp.float32)
    out_ref[:, 4 * cols :] = extra.astype(jnp.bfloat16)
    for i, copy in enumerate(copies):
        copy.wait()
        result = jnp.dot(rows, held[i], preferred_element_type=jnp.float32)
        out_ref[:, i * cols : (i + 1) * cols] = result.astype(jnp.bfloat16)


def down_slots(half, hidden, extra, weights):
    peers, units, count = hidden.shape
    deep, cols = weights[0].shape
    out = (count, 4 * cols + EXTRA)
    return pl.pallas_call(
        down_kernel,
        out_shape=jax.ShapeDtypeStruct(out, jnp.bfloat16),
        grid_spec=pltpu.PrefetchScalarGridSpec(
            num_scalar_prefetch=1,
            grid=(1,),
            in_specs=[whole(hidden.shape), whole(extra.shape)]
            + [pl.BlockSpec(memory_space=pl.ANY)] * 4,
            out_specs=whole(out),
            scratch_shapes=[
                pltpu.VMEM((deep, count), jnp.bfloat16),
                pltpu.VMEM((4, deep, cols), jnp.bfloat16),
                pltpu.SemaphoreType.DMA((4,)),
            ],
        ),
        compiler_params=pltpu.CompilerParams(vmem_limit_bytes=24 * 2**20),
        cost_estimate=pl.CostEstimate(
            flops=8 * deep * count * cols, bytes_accessed=8 * deep * cols, transcendentals=0
        ),
    )(half.reshape(1), hidden, extra, *weights)


def on_device(
    queries,
    keys,
    values,
    residual,
    out_weight,
    norm_gain,
    expert_ids,
    expert_gates,
    w_gate,
    w_up,
    w_down,
):
    n_zl, n_y = lax.axis_size("zl"), lax.axis_size("y")
    n_x, n_zh, n_co = lax.axis_size("x"), lax.axis_size("zh"), lax.axis_size("co")
    zl, y_pos, x_pos, co = (lax.axis_index(a) for a in ("zl", "y", "x", "co"))
    ctx_count, expert_count = n_zl * n_y, n_x * n_zh * n_co
    width = residual.shape[1]
    tok_dev, top_count = expert_ids.shape
    tok_block = queries.shape[0]
    heads = queries.shape[1] // HEAD_WIDTH
    swap_z = [(i, i ^ 1) for i in range(n_zl)]
    swap_y = [(i, i ^ 1) for i in range(n_y)]
    gate_own, up_own, down_own = w_gate[0].T, w_up[0].T, w_down[0]

    gate_z, up_z = lax.ppermute(gate_own, "zl", swap_z), lax.ppermute(up_own, "zl", swap_z)

    mine = jnp.where(co == 0, keys, values)
    mine = lax.dynamic_slice_in_dim(mine, x_pos * HEAD_WIDTH, HEAD_WIDTH, 1)
    gathered = spread(mine, CTX, ctx_count).reshape(ctx_count * tok_block, HEAD_WIDTH)

    key_all, value_all = spread(gathered, "co", n_co)

    order = np.arange(tok_block).reshape(n_x, n_zh, n_co, tok_dev).transpose(2, 0, 1, 3)
    split = queries.reshape(n_x, n_zh, n_co, tok_dev, heads, HEAD_WIDTH)
    query_rows = jnp.transpose(split, (4, 2, 0, 1, 3, 5)).reshape(heads * tok_block, HEAD_WIDTH)
    query_pos = (zl * n_y + y_pos) * tok_block + jnp.asarray(
        np.tile(order.reshape(-1), heads), jnp.int32
    )
    key_pos = jnp.arange(key_all.shape[0], dtype=jnp.int32)
    allowed = key_pos[None, :] <= query_pos[:, None]
    scores = rows_dot(query_rows, key_all) * (1.0 / HEAD_WIDTH**0.5)
    scores = jnp.where(allowed, scores, NEG_LARGE)
    weights = jnp.exp(scores - jnp.max(scores, axis=1, keepdims=True))
    total = jnp.sum(weights, axis=1, keepdims=True)
    numer = jnp.dot(weights.astype(jnp.bfloat16), value_all, preferred_element_type=jnp.float32)
    done = (numer / total).astype(jnp.bfloat16).reshape(heads, tok_block, HEAD_WIDTH)
    heads_out = jnp.transpose(done, (1, 0, 2)).reshape(tok_block, heads * HEAD_WIDTH)

    partial = jnp.dot(heads_out, out_weight, preferred_element_type=jnp.float32)
    partial = partial.astype(jnp.bfloat16).reshape(n_co, tok_block // n_co, width)
    partial = added(exchange(partial, "co")).astype(jnp.bfloat16)
    partial = added(exchange(partial.reshape(n_x, -1, width), "x"))
    partial, gate_z, up_z, down_own = lax.optimization_barrier((partial, gate_z, up_z, down_own))
    down_y = lax.ppermute(down_own, "y", swap_y)
    high = expert_gates.astype(jnp.bfloat16)
    low = (expert_gates - high.astype(jnp.float32)).astype(jnp.bfloat16)
    room = ((0, 0), (0, EXTRA // 4 - top_count))
    own = [(expert_ids + 1).astype(jnp.bfloat16), high, low, jnp.zeros_like(low)]
    own = jnp.concatenate([residual] + [jnp.pad(part, room) for part in own], axis=1)
    mine = jnp.arange(n_zh, dtype=jnp.int32)[:, None, None] == lax.axis_index("zh")
    own = jnp.where(mine, own[None], 0).reshape(n_zh * tok_dev, width + EXTRA)
    partial = jnp.pad(partial, ((0, 0), (0, EXTRA))) + own.astype(jnp.float32)
    parts = spread(partial.astype(jnp.bfloat16), "zh", n_zh)

    places = n_y * tok_dev
    place = jnp.stack([lax.axis_index("zh"), y_pos])
    mixed, outgoing = dispatch_rows(place, parts, norm_gain, n_x * n_co)
    arrived = exchange(outgoing, ("x", "co")).reshape(-1, width + EXTRA)

    arrived, down_own, down_y = lax.optimization_barrier((arrived, down_own, down_y))
    after = [(i, (i + 1) % n_y) for i in range(n_y)]
    before = [(b, a) for a, b in after]
    weights = (gate_own, gate_z, up_own, up_z)

    def rightward(value):
        return lax.ppermute(value, "y", after)

    def leftward(value):
        return lax.ppermute(value, "y", before)

    left_one, right_one = rightward(arrived), leftward(arrived)
    left_two, right_two = rightward(left_one), leftward(right_one)
    down_z = lax.ppermute(down_own, "zl", swap_z)
    right_two, down_z, down_y = lax.optimization_barrier((right_two, down_z, down_y))
    left_three, right_three = rightward(left_two), leftward(right_two)
    last = rightward(left_three)
    down_zy = lax.ppermute(down_y, "zl", swap_z)
    near = (arrived, left_one, right_one, left_two, right_two)
    far = (left_three, right_three)
    first = first_hidden(zl, near, weights, width)
    second = first_hidden(zl, far, weights, width)
    last, first, second = lax.optimization_barrier((last, first, second))

    hidden, extra = last_hidden(
        jnp.stack([zl, y_pos]),
        (last,),
        weights,
        (first, second),
        near + far + (last,),
        width,
        n_y,
    )
    hidden = exchange(hidden, "y")

    result = down_slots(y_pos % 2, hidden, extra, (down_own, down_y, down_z, down_zy))
    cols = result.shape[1] - EXTRA
    result = exchange(result.reshape(expert_count, -1, cols + EXTRA), EXP)
    result = result.reshape(-1, cols + EXTRA)
    tokens = lax.dot_general(
        result[:, cols : cols + 2 * places],
        result[:, :cols],
        (((0,), (0,)), ((), ())),
        preferred_element_type=jnp.float32,
    )
    tokens = (tokens[:places] + tokens[places:]).astype(jnp.bfloat16)
    tokens = exchange(tokens.reshape(n_y, tok_dev, cols), "y")
    tokens = added(tokens.reshape(n_y // 2, 2, tok_dev, cols).transpose(1, 0, 2, 3))
    tokens = tokens.astype(jnp.bfloat16).reshape(n_y // 2, tok_dev, n_zl, 2, cols // 4)
    tokens = jnp.where(zl == 0, tokens, tokens[:, :, ::-1])
    tokens = jnp.where(y_pos < n_y // 2, tokens, tokens[:, :, :, ::-1])
    tokens = tokens.transpose(1, 2, 0, 3, 4)
    return (mixed, tokens.reshape(tok_dev, width))


def solution(mesh):
    fine = Mesh(mesh.devices.reshape(2, 8, 4, 4, 2), CTX + EXP)
    return jax.shard_map(
        on_device,
        mesh=fine,
        in_specs=(
            P(CTX, EXP),
            P(CTX, None),
            P(CTX, None),
            P(CTX + EXP, None),
            P(EXP, None),
            P(),
            P(CTX + EXP, None),
            P(CTX + EXP, None),
            P(EXP, None, CTX),
            P(EXP, None, CTX),
            P(EXP, None, CTX),
        ),
        out_specs=(P(CTX + EXP, None), P(CTX + EXP, None)),
        check_vma=False,
    )
```
